32 devices in a mesh: groups: 2 (over y), tx: 16 (over z, x, core).
Axes of the slice: x: 2, y: 2, z: 4, core: 2. Of those that a mesh axis runs over, the one named last changes fastest.
Arguments:
- mask: bfloat16 [8192, 1024], P(('groups', 'tx')), parts along dimension 0, may hold values from -1 to 1
- kernel_spectra: float32 [2, 96, 12, 128], replicated, may hold values from -3 to 3
- kernel_weights: float32 [12], replicated, may hold values from 0.1 to 1
- threshold: float32 [1], replicated, may hold values from 0.4 to 1.2
- eval_tile: int32 [16384], P(('groups', 'tx')), parts along dimension 0, may hold values from 0 to 15, as said below
- site_coords: float32 [2, 16, 16384], P(None, None, ('groups', 'tx')), parts along dimension 2, may hold values from 0 to 1
- bias_steps: int32 [16384], P(('groups', 'tx')), parts along dimension 0, may hold values from -4 to 4
Outputs:
- resist: float32 [8192, 1024], P(('groups', 'tx')), parts along dimension 0
- new_bias: float32 [16384], P(('groups', 'tx')), parts along dimension 0
The draws below stay inside these ranges and needn't reach their ends.
There are 2 independent parts, one for each index of `groups`. The reference program is written for one: setup_inputs(seed, part) draws one part's arguments, and reference() takes and returns one part's arrays. A program takes and returns all parts, laid end to end along the dimension named above; an argument that names none is the same for every part. Nothing has to cross between parts.
Inputs may be any that keep to these rules, and one draw needn't show every extreme that they name: `eval_tile`: the evaluating tile of a fragment owned by tile t is t - 1, t or t + 1. One owning tile sends at most 256 fragments to each evaluating tile and exactly 256 to at least one of them; in every draw some tile receives exactly 256 fragments from each of the three owners beside it or itself.
All inputs are finite; a program needn't handle non-finite values.
Results may differ from the reference program's by a relative error of at most 0.0019.
Values may be sent and summed in bfloat16 or wider, within the bound.
No kernel may reach another device: no remote copies, remote signals or barrier semaphores. Data moves between devices by JAX's collectives and lax.ppermute only.
A program may use at most 64 MiB of HBM per device.

```python
import math
import jax
import jax.numpy as jnp
from jax import lax

ROWS_DEV = 256
COLS = 1024
HALO = 256
BLUR_REACH = 8
KERNELS = 12
SITES = 16
FRAG_DEV = 512
WINDOW = 768
ROW_FREQS = 96
COL_FREQS = 128
REGION_ROWS = 4096
FRAGS = 8192
N_TX = 16


def permuted_order(order_key):
    return jax.random.permutation(order_key, FRAG_DEV)


def draw_eval_tile(key, part):
    tile_total = FRAGS // FRAG_DEV
    capacity = FRAG_DEV // 2
    key_full, key_split, key_dense, key_order = jax.random.split(key, 4)
    owners = jnp.arange(tile_total, dtype=jnp.int32)
    full_side = jax.random.randint(key_full, (tile_total,), 0, 3)
    dense_tile = jax.random.randint(key_dense, (), 1, tile_total - 1)
    full_side = jnp.where(owners == dense_tile - 1, 2, full_side)
    full_side = jnp.where(owners == dense_tile, 1, full_side)
    full_side = jnp.where(owners == dense_tile + 1, 0, full_side)
    split_count = jax.random.randint(key_split, (tile_total,), 0, capacity + 1)
    sides = jnp.arange(3, dtype=jnp.int32)
    is_full = sides[None, :] == full_side[:, None]
    other_rank = jnp.cumsum(1 - is_full.astype(jnp.int32), axis=1) - 1
    counts = jnp.where(is_full, capacity, jnp.where(other_rank == 0, split_count[:, None], capacity - split_count[:, None]))
    first_row = jnp.where(sides == 0, 0, capacity)
    last_row = jnp.where(sides == 2, 0, capacity)
    counts = jnp.where((owners == 0)[:, None], first_row[None, :], counts)
    counts = jnp.where((owners == tile_total - 1)[:, None], last_row[None, :], counts)
    position = jnp.arange(FRAG_DEV, dtype=jnp.int32)
    side_of = (position[None, :] >= counts[:, 0:1]).astype(jnp.int32) + (position[None, :] >= counts[:, 0:1] + counts[:, 1:2]).astype(jnp.int32)
    order_keys = jax.random.split(key_order, tile_total)
    orders = jax.vmap(permuted_order)(order_keys)
    shuffled = jnp.take_along_axis(side_of, orders, axis=1)
    return (owners[:, None] + shuffled - 1).reshape(-1).astype(jnp.int32)


def with_ends(array, stream_key, low, largest):
    index_at = [jax.random.randint(jax.random.fold_in(stream_key, axis), (), 0, length) for axis, length in enumerate(array.shape)]
    widest = array.shape.index(max(array.shape))
    neighbour = index_at[:widest] + [(index_at[widest] + 1) % array.shape[widest]] + index_at[widest + 1:]
    return array.at[tuple(index_at)].set(low).at[tuple(neighbour)].set(largest)


def block_levels(own_key, dims, cuts, smallest, largest):
    def one(dim, parts):
        steps = jax.random.uniform(jax.random.fold_in(jax.random.fold_in(own_key, 6), dim), (parts,), jnp.float32, smallest / len(cuts), largest / len(cuts))
        return jnp.repeat(jnp.exp(steps), dims[dim] // parts).reshape((-1,) + (1,) * (len(dims) - dim - 1))

    factor_of = one(*cuts[0])
    for cut in cuts[1:]:
        factor_of = factor_of * one(*cut)
    return factor_of


def noise(rng, dims, spread, most, held_as=jnp.bfloat16):
    result = jax.random.normal(rng, dims, jnp.float32) * spread
    return jnp.minimum(jnp.maximum(result, -most), most).astype(held_as)


def setup_inputs(seed: int = 0, part: int = 0) -> dict:
    seeds = jax.random.split(jax.random.key(seed), 8)
    own_keys = jax.random.split(jax.random.fold_in(seeds[7], part), 8)
    mask = jnp.clip(jax.random.uniform(own_keys[0], (REGION_ROWS, COLS), jnp.float32, -1.0, 1.0) * block_levels(own_keys[0], (REGION_ROWS, COLS), ((0, 16),), -0.4, 0.0), -1.0, 1.0).astype(jnp.bfloat16)
    kernel_spectra = noise(seeds[1], (2, ROW_FREQS, KERNELS, COL_FREQS), 0.5, 3.0, jnp.float32)
    kernel_weights = jnp.clip(jnp.exp(jax.random.uniform(seeds[2], (KERNELS,), jnp.float32, math.log(0.1), math.log(1.0))), 0.1, 1.0)
    threshold = jnp.clip(jax.random.uniform(seeds[3], (1,), jnp.float32, 0.4, 1.2), 0.4, 1.2)
    eval_tile = draw_eval_tile(jax.random.fold_in(jax.random.fold_in(seeds[7], part), 71), part)
    site_coords = jnp.clip(1.0 * jax.random.uniform(own_keys[5], (2, SITES, FRAGS), jnp.float32) ** block_levels(own_keys[5], (2, SITES, FRAGS), ((2, 16),), -0.2, 0.2), 0.0, 1.0)
    bias_steps = with_ends(jax.random.randint(own_keys[6], (FRAGS,), -4, 5), jax.random.fold_in(own_keys[6], 1), -4, 4).astype(jnp.int32)
    return {"mask": mask, "kernel_spectra": kernel_spectra, "kernel_weights": kernel_weights, "threshold": threshold, "eval_tile": eval_tile, "site_coords": site_coords, "bias_steps": bias_steps}


blur_sigma = 3.0
bias_step = 0.5
bias_gain = 2.0

def twiddle(position, frequency, period, amplitude):
    phase_index = position[:, None] * frequency[None, :] % period
    phase_angle = phase_index.astype(jnp.float32) * (2.0 * math.pi / period)
    return (jnp.cos(phase_angle) * amplitude, jnp.sin(phase_angle) * amplitude)

def centered(count):
    return jnp.arange(count, dtype=jnp.int32) - count // 2

def imaging_tables(tile_rows, tile_cols, window_rows, row_freqs, col_freqs, halo_rows):
    col_cos, col_sin = twiddle(jnp.arange(tile_cols, dtype=jnp.int32), centered(col_freqs), tile_cols, 1.0 / math.sqrt(tile_cols))
    col_forward = jnp.concatenate([col_cos, -col_sin], axis=1).astype(jnp.bfloat16)
    row_cos, row_sin = twiddle(centered(row_freqs), jnp.arange(window_rows, dtype=jnp.int32), window_rows, 1.0 / math.sqrt(window_rows))
    row_forward = jnp.concatenate([row_cos, -row_sin], axis=0).astype(jnp.bfloat16)
    back_cos, back_sin = twiddle(jnp.arange(tile_rows, dtype=jnp.int32) + halo_rows, centered(row_freqs), window_rows, 1.0 / math.sqrt(row_freqs))
    row_inverse = jnp.concatenate([back_cos, back_sin], axis=0).astype(jnp.bfloat16)
    out_cos, out_sin = twiddle(centered(col_freqs), jnp.arange(tile_cols, dtype=jnp.int32), tile_cols, 1.0 / math.sqrt(col_freqs))
    upper_half = jnp.concatenate([out_cos, out_sin], axis=1)
    lower_half = jnp.concatenate([-out_sin, out_cos], axis=1)
    col_inverse = jnp.concatenate([upper_half, lower_half], axis=0).astype(jnp.bfloat16)
    return (col_forward, row_forward, row_inverse, col_inverse)

def tile_intensity(col_spectra, tables, kernel_spectra, kernel_weights):
    row_forward = tables[1]
    row_inverse = tables[2]
    col_inverse = tables[3]
    row_freqs = kernel_spectra.shape[1]
    kernel_count = kernel_spectra.shape[2]
    col_freqs = kernel_spectra.shape[3]
    tile_rows = row_inverse.shape[0] // 2
    tile_cols = col_inverse.shape[1] // 2
    row_product = jnp.dot(row_forward, col_spectra, preferred_element_type=jnp.float32)
    spec_real = row_product[:row_freqs, :col_freqs] - row_product[row_freqs:, col_freqs:]
    spec_imag = row_product[:row_freqs, col_freqs:] + row_product[row_freqs:, :col_freqs]
    kern_real = kernel_spectra[0]
    kern_imag = kernel_spectra[1]
    prod_real = (kern_real * spec_real[:, None, :] - kern_imag * spec_imag[:, None, :]).astype(jnp.bfloat16)
    prod_imag = (kern_real * spec_imag[:, None, :] + kern_imag * spec_real[:, None, :]).astype(jnp.bfloat16)
    flat_width = kernel_count * col_freqs
    joined = jnp.concatenate([prod_real.reshape(row_freqs, flat_width), prod_imag.reshape(row_freqs, flat_width)], axis=1)
    back_product = jnp.dot(row_inverse, joined, preferred_element_type=jnp.float32)
    half_real = (back_product[:tile_rows, :flat_width] - back_product[tile_rows:, flat_width:]).astype(jnp.bfloat16)
    half_imag = (back_product[:tile_rows, flat_width:] + back_product[tile_rows:, :flat_width]).astype(jnp.bfloat16)
    stacked = jnp.concatenate([half_real.reshape(tile_rows, kernel_count, col_freqs), half_imag.reshape(tile_rows, kernel_count, col_freqs)], axis=2)
    stacked = jnp.transpose(stacked, (1, 0, 2))

    def add_kernel(intensity_sum, inputs):
        kernel_block, kernel_weight = inputs
        field_pair = jnp.dot(kernel_block, col_inverse, preferred_element_type=jnp.float32)
        field_real = field_pair[:, :tile_cols]
        field_imag = field_pair[:, tile_cols:]
        return (intensity_sum + kernel_weight * (field_real * field_real + field_imag * field_imag), None)
    start_sum = jnp.zeros((tile_rows, tile_cols), jnp.float32)
    intensity_sum, unused_out = lax.scan(add_kernel, start_sum, (stacked, kernel_weights))
    return intensity_sum.astype(jnp.bfloat16)

def blur_weight(offset, reach):
    offset_value = offset.astype(jnp.float32)
    all_offsets = jnp.arange(-reach, reach + 1, dtype=jnp.int32).astype(jnp.float32)
    norm_sum = jnp.sum(jnp.exp(-all_offsets * all_offsets / (2.0 * blur_sigma * blur_sigma)))
    inside = jnp.abs(offset) <= reach
    return jnp.where(inside, jnp.exp(-offset_value * offset_value / (2.0 * blur_sigma * blur_sigma)) / norm_sum, jnp.float32(0.0))

def blur_tables(tile_rows, tile_cols, reach):
    col_diff = jnp.arange(tile_cols, dtype=jnp.int32)[None, :] - jnp.arange(tile_cols, dtype=jnp.int32)[:, None]
    col_blur = blur_weight(col_diff, reach).astype(jnp.bfloat16)
    row_diff = jnp.arange(tile_rows + 2 * reach, dtype=jnp.int32)[None, :] - reach - jnp.arange(tile_rows, dtype=jnp.int32)[:, None]
    row_blur = blur_weight(row_diff, reach).astype(jnp.bfloat16)
    return (col_blur, row_blur)

def sample_resist(resist, row_frac, col_frac, row_base, tile_rows):
    tile_cols = resist.shape[1]
    row_pos = row_frac * (tile_rows - 1)
    col_pos = col_frac * (tile_cols - 1)
    row_low = jnp.minimum(jnp.floor(row_pos), tile_rows - 2)
    col_low = jnp.minimum(jnp.floor(col_pos), tile_cols - 2)
    row_part = row_pos - row_low
    col_part = col_pos - col_low
    first_index = (row_low.astype(jnp.int32) + row_base) * tile_cols + col_low.astype(jnp.int32)
    flat_resist = resist.reshape(-1)
    upper_left = flat_resist[first_index]
    upper_right = flat_resist[first_index + 1]
    lower_left = flat_resist[first_index + tile_cols]
    lower_right = flat_resist[first_index + tile_cols + 1]
    top_line = (1.0 - col_part) * upper_left + col_part * upper_right
    bottom_line = (1.0 - col_part) * lower_left + col_part * lower_right
    return (1.0 - row_part) * top_line + row_part * bottom_line

def reference(mask, kernel_spectra, kernel_weights, threshold, eval_tile, site_coords, bias_steps):
    tables = imaging_tables(ROWS_DEV, COLS, WINDOW, ROW_FREQS, COL_FREQS, HALO)
    padded_mask = jnp.pad(mask, ((HALO, HALO), (0, 0)))

    def one_tile(tile_index):
        window = lax.dynamic_slice_in_dim(padded_mask, (tile_index * ROWS_DEV).astype(jnp.int32), WINDOW, 0)
        col_spectra = jnp.dot(window, tables[0], preferred_element_type=jnp.float32).astype(jnp.bfloat16)
        return tile_intensity(col_spectra, tables, kernel_spectra, kernel_weights)
    tile_numbers = jnp.arange(N_TX, dtype=jnp.int32)
    intensity = lax.map(one_tile, tile_numbers).reshape(REGION_ROWS, COLS)
    col_blur, row_blur = blur_tables(ROWS_DEV, COLS, BLUR_REACH)
    padded_intensity = jnp.pad(intensity, ((BLUR_REACH, BLUR_REACH), (0, 0)))
    col_blurred = jnp.dot(padded_intensity, col_blur, preferred_element_type=jnp.float32).astype(jnp.bfloat16)

    def blur_tile(tile_index):
        row_block = lax.dynamic_slice_in_dim(col_blurred, (tile_index * ROWS_DEV).astype(jnp.int32), ROWS_DEV + 2 * BLUR_REACH, 0)
        return jnp.dot(row_blur, row_block, preferred_element_type=jnp.float32)
    resist = lax.map(blur_tile, tile_numbers).reshape(REGION_ROWS, COLS)
    site_values = sample_resist(resist, site_coords[0], site_coords[1], eval_tile[None, :] * ROWS_DEV, ROWS_DEV)
    site_mean = lax.optimization_barrier(jnp.mean(site_values, axis=0))
    new_bias = bias_step * bias_steps.astype(jnp.float32) - bias_gain * (site_mean - threshold[0])
    return (resist, new_bias)
```

```python
import math

import jax
import jax.numpy as jnp
import ml_dtypes
import numpy as np
from jax import lax
from jax.experimental import pallas as pl
from jax.experimental.pallas import tpu as pltpu
from jax.sharding import PartitionSpec as P

HALO = 256
BLUR_REACH = 8
SITES = 16

blur_sigma = 3.0
bias_step = 0.5
bias_gain = 2.0

F32 = jnp.float32
BF16 = jnp.bfloat16
BLOCK = 64
VMEM_BYTES = 48 * 1024 * 1024


def rounded(table):
    return np.asarray(table, np.float32).astype(ml_dtypes.bfloat16)


def halves(table):
    high = rounded(table)
    low = rounded(np.asarray(table, np.float64) - high.astype(np.float64))
    return high, low


def twiddle(position, frequency, period, amplitude):
    phase_index = (position[:, None] * frequency[None, :]) % period
    phase_angle = phase_index * (2.0 * math.pi / period)
    return np.cos(phase_angle) * amplitude, np.sin(phase_angle) * amplitude


def centered(count):
    return np.arange(count) - count // 2


def imaging_tables(tile_rows, tile_cols, row_freqs, col_freqs):
    window_rows = tile_rows + 2 * HALO
    col_cos, col_sin = twiddle(
        np.arange(tile_cols), centered(col_freqs), tile_cols, 1.0 / math.sqrt(tile_cols)
    )
    col_forward = rounded(np.concatenate([col_cos, -col_sin], axis=1))
    row_cos, row_sin = twiddle(
        centered(row_freqs), np.arange(window_rows), window_rows, 1.0 / math.sqrt(window_rows)
    )
    row_forward = rounded(np.concatenate([row_cos, -row_sin], axis=0))
    row_blocks = np.stack(
        [row_forward[:, i * tile_rows : (i + 1) * tile_rows] for i in range(3)]
    )
    back_cos, back_sin = twiddle(
        np.arange(tile_rows) + HALO, centered(row_freqs), window_rows, 1.0 / math.sqrt(row_freqs)
    )
    row_inverse = rounded(
        np.block([[back_cos, -back_sin], [back_sin, back_cos]])
    )
    samples = 2 * col_freqs
    step = tile_cols // samples
    out_cos, out_sin = twiddle(
        centered(col_freqs), np.arange(samples) * step, tile_cols, 1.0 / math.sqrt(col_freqs)
    )
    col_inverse = rounded(np.block([[out_cos, out_sin], [-out_sin, out_cos]]))
    return col_forward, row_blocks, row_inverse, col_inverse


def blur_weight(offset, reach):
    every = np.arange(-reach, reach + 1).astype(np.float64)
    norm = np.sum(np.exp(-every * every / (2.0 * blur_sigma * blur_sigma)))
    weight = np.exp(-offset.astype(np.float64) ** 2 / (2.0 * blur_sigma * blur_sigma)) / norm
    return np.where(np.abs(offset) <= reach, weight, 0.0)


def blur_tables(tile_rows, tile_cols, col_freqs, reach):
    line = np.arange(tile_cols)
    col_blur = rounded(blur_weight(line[None, :] - line[:, None], reach))
    samples = 2 * col_freqs
    step = tile_cols // samples
    offset = (line[None, :] - step * np.arange(samples)[:, None]).astype(np.float64)
    half = np.where(offset == 0, 1.0, np.sin(math.pi * offset / tile_cols))
    spread = np.where(
        offset == 0,
        (samples - 1) / samples,
        np.sin((samples - 1) * math.pi * offset / tile_cols) / (samples * half),
    )
    spread_blur = spread @ col_blur.astype(np.float64)
    row_diff = (
        np.arange(tile_rows + 2 * reach)[None, :] - reach - np.arange(tile_rows)[:, None]
    )
    row_blur = rounded(blur_weight(row_diff, reach))
    inner = row_blur[:, reach : reach + tile_rows]
    outer = np.concatenate([row_blur[:, :reach], row_blur[:, reach + tile_rows :]], axis=1)
    return halves(spread_blur), np.ascontiguousarray(inner), np.ascontiguousarray(outer)


def parity():
    return lax.rem(lax.axis_index("tx"), 2)


def spectra_kernel(mask_ref, forward_ref, rows_ref, own_ref, core_ref, chip_ref):
    col_spectra = jnp.dot(mask_ref[...], forward_ref[...], preferred_element_type=F32).astype(BF16)
    freqs, cols = own_ref.shape[0] // 2, own_ref.shape[1]
    odd = parity()

    def partial(block, out_ref):
        product = jnp.dot(rows_ref[block], col_spectra, preferred_element_type=F32)
        out_ref[:freqs, :] = product[:freqs, :cols] - product[freqs:, cols:]
        out_ref[freqs:, :] = product[:freqs, cols:] + product[freqs:, :cols]

    partial(1, own_ref)
    partial(2 * odd, core_ref)
    partial(2 - 2 * odd, chip_ref)


def pack_kernel(eval_ref, records_ref, core_ref, chip_ref, own_ref, code_ref):
    frags = eval_ref.shape[1]
    capacity = frags // 2
    me = lax.axis_index("tx")
    odd = parity()
    offset = eval_ref[...] - me + 1
    member = (
        lax.broadcasted_iota(jnp.int32, (8, frags), 0) == offset
    )
    before = lax.broadcasted_iota(jnp.int32, (frags, frags), 0)
    after = lax.broadcasted_iota(jnp.int32, (frags, frags), 1)
    upper = (before <= after).astype(F32).astype(BF16)
    counts = jnp.dot(member.astype(F32).astype(BF16), upper, preferred_element_type=F32)
    code_ref[...] = jnp.where(member, counts - 1.0, -1.0)
    records = records_ref[...]
    first = records.astype(BF16)
    rest = records - first.astype(F32)
    second = rest.astype(BF16)
    third = (rest - second.astype(F32)).astype(BF16)
    pieces = jnp.concatenate([first, second, third], axis=0)
    slots = lax.broadcasted_iota(jnp.int32, (capacity, frags), 0).astype(F32)
    count = records.shape[0]

    def packed(side, out_ref):
        chosen = (slots == code_ref[pl.ds(side, 1), :]).astype(F32).astype(BF16)
        got = lax.dot_general(
            pieces, chosen, (((1,), (1,)), ((), ())), preferred_element_type=F32
        )
        out_ref[...] = got[:count] + got[count : 2 * count] + got[2 * count :]

    packed(2 - 2 * odd, core_ref)
    packed(2 * odd, chip_ref)
    packed(1, own_ref)


def has_chip_side():
    me = lax.axis_index("tx")
    return jnp.logical_and(me != 0, me != lax.axis_size("tx") - 1)


def across():
    rest = lax.rem(lax.axis_index("tx"), 4)
    return jnp.logical_or(rest == 1, rest == 2)


def imaging_kernel(
    weights_ref, own_ref, core_ref, near_ref, far_ref, kern_ref, inverse_ref, spread_ref,
    packed_core_ref, packed_chip_ref,
    intensity_ref, pay_core_ref, pay_chip_ref,
    product_ref, half_ref,
):
    freqs, cols = own_ref.shape[0] // 2, own_ref.shape[1]
    rows = intensity_ref.shape[0]
    kernels = kern_ref.shape[1]
    odd = parity()
    chip = jnp.where(across(), near_ref[...], far_ref[...])
    chip = jnp.where(has_chip_side(), chip, 0.0)
    spectrum = own_ref[...] + core_ref[...] + chip
    spec_real, spec_imag = spectrum[:freqs], spectrum[freqs:]
    for k in range(kernels):
        kern_real, kern_imag = kern_ref[0, k], kern_ref[1, k]
        lanes = slice(k * cols, (k + 1) * cols)
        product_ref[:freqs, lanes] = (kern_real * spec_real - kern_imag * spec_imag).astype(BF16)
        product_ref[freqs:, lanes] = (kern_real * spec_imag + kern_imag * spec_real).astype(BF16)
    half_ref[...] = jnp.dot(
        inverse_ref[...], product_ref[...], preferred_element_type=F32
    ).astype(BF16)
    total = None
    for k in range(kernels):
        lanes = slice(k * cols, (k + 1) * cols)
        pair = jnp.concatenate([half_ref[:rows, lanes], half_ref[rows:, lanes]], axis=1)
        field = jnp.dot(pair, spread_ref[...], preferred_element_type=F32)
        real, imag = field[:, : 2 * cols], field[:, 2 * cols :]
        term = weights_ref[0, k] * (real * real + imag * imag)
        total = term if total is None else total + term
    rounded_total = total.astype(BF16)
    intensity_ref[...] = rounded_total
    values = rounded_total.astype(F32)
    top, bottom = values[:BLUR_REACH], values[rows - BLUR_REACH :]
    count = packed_core_ref.shape[0]
    pay_core_ref[:count] = packed_core_ref[...]
    pay_chip_ref[:count] = packed_chip_ref[...]
    pay_core_ref[count:] = jnp.where(odd == 1, top, bottom)
    pay_chip_ref[count:] = jnp.where(odd == 1, bottom, top)


def site_means(table_ref, fetch):
    tile_cols, tile_rows = table_ref.shape
    slots = fetch(0).shape[1]
    grid_rows = lax.broadcasted_iota(jnp.int32, (tile_rows, slots), 0).astype(F32)
    eight = lax.broadcasted_iota(jnp.int32, (8, slots), 0).astype(F32)
    groups = BLOCK // 8
    blocks = tile_cols // BLOCK

    def one_site(site, total):
        row_pos = fetch(site) * (tile_rows - 1)
        tent = jnp.maximum(1.0 - jnp.abs(row_pos - grid_rows), 0.0).astype(BF16)
        picked = jnp.dot(table_ref[...], tent, preferred_element_type=F32)
        col_pos = fetch(SITES + site) * (tile_cols - 1)
        block = jnp.minimum(jnp.floor(col_pos * (1.0 / BLOCK)), blocks - 1.0)
        within = jnp.broadcast_to(col_pos - block * BLOCK, (8, slots))
        block = jnp.broadcast_to(block, (8, slots))
        held = [jnp.zeros((8, slots), F32) for _ in range(groups + 1)]
        for b in range(blocks):
            hit = block == float(b)
            start = b * BLOCK
            last = groups + 1 if b < blocks - 1 else groups
            for g in range(last):
                held[g] = jnp.where(hit, picked[start + 8 * g : start + 8 * g + 8], held[g])
        for g in range(groups + 1):
            weight = jnp.maximum(1.0 - jnp.abs(within - (eight + 8.0 * g)), 0.0)
            total = total + held[g] * weight
        return total

    total = lax.fori_loop(0, SITES, one_site, jnp.zeros((8, slots), F32))
    return jnp.broadcast_to(jnp.sum(total, axis=0, keepdims=True) * (1.0 / SITES), (8, slots))


def resist_kernel(
    intensity_ref, core_ref, near_ref, far_ref, inner_ref, outer_ref,
    high_ref, low_ref, high_t_ref, low_t_ref,
    resist_ref, table_ref, coords_core_ref, mean_chip_ref, coords_ref,
):
    odd = parity()
    count = coords_ref.shape[0]
    chip = jnp.where(across(), near_ref[...], far_ref[...])
    coords_ref[...] = chip[:count]
    core = core_ref[...]
    coords_core_ref[...] = core[:count]
    chip_edge = jnp.where(has_chip_side(), chip[count:], 0.0)
    core_edge = core[count:]
    above = jnp.where(odd == 1, core_edge, chip_edge)
    below = jnp.where(odd == 1, chip_edge, core_edge)
    edges = jnp.concatenate([above, below], axis=0).astype(BF16)
    blurred = jnp.dot(inner_ref[...], intensity_ref[...], preferred_element_type=F32)
    blurred += jnp.dot(outer_ref[...], edges, preferred_element_type=F32)
    high = blurred.astype(BF16)
    low = (blurred - high.astype(F32)).astype(BF16)

    resist_ref[...] = (
        jnp.dot(high, high_ref[...], preferred_element_type=F32)
        + jnp.dot(low, high_ref[...], preferred_element_type=F32)
        + jnp.dot(high, low_ref[...], preferred_element_type=F32)
    )

    def crossed(left, right):
        return lax.dot_general(left, right, (((1,), (1,)), ((), ())), preferred_element_type=F32)

    table_ref[...] = (
        crossed(high_t_ref[...], high)
        + crossed(high_t_ref[...], low)
        + crossed(low_t_ref[...], high)
    ).astype(BF16)
    mean_chip_ref[...] = site_means(table_ref, lambda i: coords_ref[pl.ds(i, 1), :])


def mean_kernel(table_ref, coords_ref, mean_ref):
    mean_ref[...] = site_means(table_ref, lambda i: coords_ref[pl.ds(i, 1), :])


def bias_kernel(threshold_ref, code_ref, own_ref, core_ref, near_ref, far_ref, steps_ref, out_ref):
    frags = code_ref.shape[1]
    capacity = frags // 2
    odd = parity()
    chip = jnp.where(across(), near_ref[...], far_ref[...])
    slots = lax.broadcasted_iota(jnp.int32, (capacity, frags), 0).astype(F32)
    lanes = lax.broadcasted_iota(jnp.int32, (8, capacity), 0)
    total = jnp.zeros((1, frags), F32)
    for side, mean in ((1, own_ref[...]), (2 - 2 * odd, core_ref[...]), (2 * odd, chip)):
        first = mean.astype(BF16)
        rest = mean - first.astype(F32)
        second = rest.astype(BF16)
        third = (rest - second.astype(F32)).astype(BF16)
        parts = jnp.where(
            lanes == 0, first.astype(F32),
            jnp.where(lanes == 1, second.astype(F32), jnp.where(lanes == 2, third.astype(F32), 0.0)),
        ).astype(BF16)
        chosen = (slots == code_ref[pl.ds(side, 1), :]).astype(F32).astype(BF16)
        got = jnp.dot(parts, chosen, preferred_element_type=F32)
        total = total + jnp.sum(got, axis=0, keepdims=True)
    out_ref[...] = bias_step * steps_ref[...].astype(F32) - bias_gain * (total - threshold_ref[0])


def swaps(count):
    core = [(i, i ^ 1) for i in range(count)]
    near = [(i, i ^ 3) for i in range(count)]
    partner = {0: 1, 1: 0, count - 1: count - 2, count - 2: count - 1}
    for low in range(0, count - 4, 4):
        for a, b in ((low + 3, low + 4), (low + 2, low + 5)):
            partner[a], partner[b] = b, a
    far = [(i, partner[i]) for i in range(count)]
    return core, near, far


def exchange(to_core, to_chip):
    core, near, far = swaps(lax.axis_size("tx"))
    got_far = lax.ppermute(to_chip, "tx", far)
    got_near = lax.ppermute(to_chip, "tx", near)
    got_core = lax.ppermute(to_core, "tx", core)
    return got_core, got_near, got_far


def call(kernel, outs, args, smem=(), scratch=(), name=None):
    specs = [
        pl.BlockSpec(memory_space=pltpu.SMEM if i in smem else pltpu.VMEM) for i in range(len(args))
    ]
    return pl.pallas_call(
        kernel,
        out_shape=[jax.ShapeDtypeStruct(s, d) for s, d in outs],
        in_specs=specs,
        out_specs=[pl.BlockSpec(memory_space=pltpu.VMEM) for _ in outs],
        scratch_shapes=list(scratch),
        compiler_params=pltpu.CompilerParams(vmem_limit_bytes=VMEM_BYTES),
        name=name,
    )(*args)


def shards(mask, kernel_spectra, kernel_weights, threshold, eval_tile, site_coords, bias_steps):
    tile_rows, tile_cols = mask.shape
    _, row_freqs, kernels, col_freqs = kernel_spectra.shape
    frags = eval_tile.shape[0]
    capacity = frags // 2
    samples = 2 * col_freqs
    flat = kernels * col_freqs
    records = 2 * SITES
    col_forward, row_blocks, row_inverse, col_inverse = imaging_tables(
        tile_rows, tile_cols, row_freqs, col_freqs
    )
    (high, low), inner, outer = blur_tables(tile_rows, tile_cols, col_freqs, BLUR_REACH)
    spectrum = ((2 * row_freqs, col_freqs), F32)
    packed = ((records, capacity), F32)
    payload = ((records + BLUR_REACH, capacity), F32)
    means = ((8, capacity), F32)

    own, to_core, to_chip = call(
        spectra_kernel, [spectrum] * 3, (mask, col_forward, row_blocks), name="spectra"
    )
    from_core, from_near, from_far = exchange(to_core, to_chip)
    packed_core, packed_chip, packed_own, code = call(
        pack_kernel,
        [packed] * 3 + [((8, frags), F32)],
        (eval_tile.reshape(1, frags), site_coords.reshape(records, frags)),
        name="pack",
    )
    kern = jnp.transpose(kernel_spectra, (0, 2, 1, 3))
    intensity, pay_core, pay_chip = call(
        imaging_kernel,
        [((tile_rows, samples), BF16), payload, payload],
        (
            kernel_weights.reshape(1, kernels), own, from_core, from_near, from_far,
            kern, row_inverse, col_inverse, packed_core, packed_chip,
        ),
        smem=(0,),
        scratch=[
            pltpu.VMEM((2 * row_freqs, flat), BF16),
            pltpu.VMEM((2 * tile_rows, flat), BF16),
        ],
        name="imaging",
    )
    edge_core, edge_near, edge_far = exchange(pay_core, pay_chip)
    resist, table, coords_core, mean_chip = call(
        resist_kernel,
        [
            ((tile_rows, tile_cols), F32),
            ((tile_cols, tile_rows), BF16),
            packed,
            means,
        ],
        (
            intensity, edge_core, edge_near, edge_far, inner, outer,
            high, low, np.ascontiguousarray(high.T), np.ascontiguousarray(low.T),
        ),
        scratch=[pltpu.VMEM((records, capacity), F32)],
        name="resist",
    )
    core, near, far = swaps(lax.axis_size("tx"))
    back_far = lax.ppermute(mean_chip, "tx", far)
    back_near = lax.ppermute(mean_chip, "tx", near)
    (mean_core,) = call(mean_kernel, [means], (table, coords_core), name="mean_core")
    back_core = lax.ppermute(mean_core, "tx", core)
    (mean_own,) = call(mean_kernel, [means], (table, packed_own), name="mean_own")
    (new_bias,) = call(
        bias_kernel,
        [((1, frags), F32)],
        (threshold, code, mean_own, back_core, back_near, back_far, bias_steps.reshape(1, frags)),
        smem=(0,),
        name="bias",
    )
    return resist, new_bias.reshape(frags)


def solution(mesh):
    placed = (
        P(("groups", "tx"), None),
        P(),
        P(),
        P(),
        P(("groups", "tx")),
        P(None, None, ("groups", "tx")),
        P(("groups", "tx")),
    )
    return jax.shard_map(
        shards,
        mesh=mesh,
        in_specs=placed,
        out_specs=(P(("groups", "tx"), None), P(("groups", "tx"))),
        check_vma=False,
    )
```

```python
import math

import jax
import jax.numpy as jnp
import ml_dtypes
import numpy as np
from jax import lax
from jax.experimental import pallas as pl
from jax.experimental.pallas import tpu as pltpu
from jax.sharding import PartitionSpec as P

HALO = 256
BLUR_REACH = 8
SITES = 16

blur_sigma = 3.0
bias_step = 0.5
bias_gain = 2.0

F32 = jnp.float32
BF16 = jnp.bfloat16
BLOCK = 64
VMEM_BYTES = 48 * 1024 * 1024


def rounded(table):
    return np.asarray(table, np.float32).astype(ml_dtypes.bfloat16)


def halves(table):
    high = rounded(table)
    low = rounded(np.asarray(table, np.float64) - high.astype(np.float64))
    return high, low


def twiddle(position, frequency, period, amplitude):
    phase_index = (position[:, None] * frequency[None, :]) % period
    phase_angle = phase_index * (2.0 * math.pi / period)
    return np.cos(phase_angle) * amplitude, np.sin(phase_angle) * amplitude


def centered(count):
    return np.arange(count) - count // 2


def imaging_tables(tile_rows, tile_cols, row_freqs, col_freqs):
    window_rows = tile_rows + 2 * HALO
    col_cos, col_sin = twiddle(
        np.arange(tile_cols), centered(col_freqs), tile_cols, 1.0 / math.sqrt(tile_cols)
    )
    col_forward = rounded(np.concatenate([col_cos, -col_sin], axis=1))
    row_cos, row_sin = twiddle(
        centered(row_freqs), np.arange(window_rows), window_rows, 1.0 / math.sqrt(window_rows)
    )
    row_forward = rounded(np.concatenate([row_cos, -row_sin], axis=0))
    row_blocks = np.stack(
        [row_forward[:, i * tile_rows : (i + 1) * tile_rows] for i in range(3)]
    )
    back_cos, back_sin = twiddle(
        np.arange(tile_rows) + HALO, centered(row_freqs), window_rows, 1.0 / math.sqrt(row_freqs)
    )
    row_inverse = rounded(
        np.block([[back_cos, -back_sin], [back_sin, back_cos]])
    )
    samples = 2 * col_freqs
    step = tile_cols // samples
    out_cos, out_sin = twiddle(
        centered(col_freqs), np.arange(samples) * step, tile_cols, 1.0 / math.sqrt(col_freqs)
    )
    col_inverse = rounded(np.block([[out_cos, out_sin], [-out_sin, out_cos]]))
    return col_forward, row_blocks, row_inverse, col_inverse


def blur_weight(offset, reach):
    every = np.arange(-reach, reach + 1).astype(np.float64)
    norm = np.sum(np.exp(-every * every / (2.0 * blur_sigma * blur_sigma)))
    weight = np.exp(-offset.astype(np.float64) ** 2 / (2.0 * blur_sigma * blur_sigma)) / norm
    return np.where(np.abs(offset) <= reach, weight, 0.0)


def blur_tables(tile_rows, tile_cols, col_freqs, reach):
    line = np.arange(tile_cols)
    col_blur = rounded(blur_weight(line[None, :] - line[:, None], reach))
    samples = 2 * col_freqs
    step = tile_cols // samples
    offset = (line[None, :] - step * np.arange(samples)[:, None]).astype(np.float64)
    half = np.where(offset == 0, 1.0, np.sin(math.pi * offset / tile_cols))
    spread = np.where(
        offset == 0,
        (samples - 1) / samples,
        np.sin((samples - 1) * math.pi * offset / tile_cols) / (samples * half),
    )
    spread_blur = spread @ col_blur.astype(np.float64)
    row_diff = (
        np.arange(tile_rows + 2 * reach)[None, :] - reach - np.arange(tile_rows)[:, None]
    )
    row_blur = rounded(blur_weight(row_diff, reach))
    inner = row_blur[:, reach : reach + tile_rows]
    outer = np.concatenate([row_blur[:, :reach], row_blur[:, reach + tile_rows :]], axis=1)
    return halves(spread_blur), np.ascontiguousarray(inner), np.ascontiguousarray(outer)


def parity():
    return lax.rem(lax.axis_index("tx"), 2)


def has_chip_side():
    me = lax.axis_index("tx")
    return jnp.logical_and(me != 0, me != lax.axis_size("tx") - 1)


def across():
    rest = lax.rem(lax.axis_index("tx"), 4)
    return jnp.logical_or(rest == 1, rest == 2)


def from_chip(near_ref, far_ref):
    return jnp.where(across(), near_ref[...], far_ref[...])


def three_parts(values):
    first = values.astype(BF16)
    rest = values - first.astype(F32)
    second = rest.astype(BF16)
    third = (rest - second.astype(F32)).astype(BF16)
    return first, second, third


def transposed_dot(left, right):
    return lax.dot_general(left, right, (((1,), (1,)), ((), ())), preferred_element_type=F32)


def front_kernel(
    eval_hbm, records_hbm, mask_hbm, forward_hbm, rows_hbm,
    own_ref, core_ref, chip_ref, packed_core_ref, packed_chip_ref, packed_own_ref, chosen_ref,
    eval_ref, records_ref, mask_ref, forward_ref, rows_ref, sems,
):
    copies = [
        pltpu.make_async_copy(source, target, sems.at[i])
        for i, (source, target) in enumerate(
            (
                (eval_hbm, eval_ref),
                (records_hbm, records_ref),
                (mask_hbm, mask_ref),
                (forward_hbm, forward_ref),
                (rows_hbm, rows_ref),
            )
        )
    ]
    for copy in copies:
        copy.start()
    me = lax.axis_index("tx")
    odd = parity()
    frags = eval_ref.shape[1]
    capacity = frags // 2
    count = records_ref.shape[0]
    before = lax.broadcasted_iota(jnp.int32, (frags, frags), 0)
    after = lax.broadcasted_iota(jnp.int32, (frags, frags), 1)
    upper = (before <= after).astype(F32).astype(BF16)
    slots = lax.broadcasted_iota(jnp.int32, (capacity, frags), 0).astype(F32).astype(BF16)
    copies[0].wait()
    copies[1].wait()
    member = lax.broadcasted_iota(jnp.int32, (8, frags), 0) == eval_ref[...] - me + 1
    counts = jnp.dot(member.astype(F32).astype(BF16), upper, preferred_element_type=F32)
    code = jnp.where(member, counts - 1.0, -1.0)
    for side in range(3):
        row = jnp.broadcast_to(code[side : side + 1].astype(BF16), (capacity, frags))
        chosen_ref[side] = jnp.where(slots == row, jnp.ones_like(slots), jnp.zeros_like(slots))
    pieces = jnp.concatenate(three_parts(records_ref[...]), axis=0)

    def packed(side, out_ref):
        got = transposed_dot(pieces, chosen_ref[side])
        out_ref[...] = got[:count] + got[count : 2 * count] + got[2 * count :]

    packed(2 - 2 * odd, packed_core_ref)
    packed(2 * odd, packed_chip_ref)
    packed(1, packed_own_ref)

    for copy in copies[2:]:
        copy.wait()
    col_spectra = jnp.dot(mask_ref[...], forward_ref[...], preferred_element_type=F32).astype(BF16)
    freqs, cols = own_ref.shape[0] // 2, own_ref.shape[1]

    def partial(block, out_ref):
        product = jnp.dot(rows_ref[block], col_spectra, preferred_element_type=F32)
        out_ref[:freqs, :] = product[:freqs, :cols] - product[freqs:, cols:]
        out_ref[freqs:, :] = product[:freqs, cols:] + product[freqs:, :cols]

    partial(2 - 2 * odd, chip_ref)
    partial(2 * odd, core_ref)
    partial(1, own_ref)


def load_kernel(after_ref, *refs):
    count = (len(refs) - 1) // 2
    sems = refs[-1]
    copies = [
        pltpu.make_async_copy(refs[i], refs[count + i], sems.at[i]) for i in range(count)
    ]
    for copy in copies:
        copy.start()
    for copy in copies:
        copy.wait()


def summed_intensity(half, rows, kernels, cols, spread, weights_ref):
    total = None
    for k in range(kernels):
        lanes = slice(k * cols, (k + 1) * cols)
        pair = jnp.concatenate([half[:rows, lanes], half[rows:, lanes]], axis=1)
        field = jnp.dot(pair, spread, preferred_element_type=F32)
        real, imag = field[:, : 2 * cols], field[:, 2 * cols :]
        term = weights_ref[0, k] * (real * real + imag * imag)
        total = term if total is None else total + term
    return total


def edge_kernel(
    weights_ref, own_ref, core_ref, near_ref, far_ref, kern_ref, inverse_ref, spread_ref,
    product_ref, edge_core_ref, edge_chip_ref,
):
    freqs, cols = own_ref.shape[0] // 2, own_ref.shape[1]
    rows = inverse_ref.shape[0] // 2
    kernels = kern_ref.shape[1]
    odd = parity()
    chip = jnp.where(has_chip_side(), from_chip(near_ref, far_ref), 0.0)
    spectrum = own_ref[...] + core_ref[...] + chip
    spec_real, spec_imag = spectrum[:freqs], spectrum[freqs:]
    for k in range(kernels):
        kern_real, kern_imag = kern_ref[0, k], kern_ref[1, k]
        lanes = slice(k * cols, (k + 1) * cols)
        product_ref[:freqs, lanes] = (kern_real * spec_real - kern_imag * spec_imag).astype(BF16)
        product_ref[freqs:, lanes] = (kern_real * spec_imag + kern_imag * spec_real).astype(BF16)
    reach = BLUR_REACH
    lines = jnp.concatenate(
        [
            inverse_ref[:reach], inverse_ref[rows - reach : rows],
            inverse_ref[rows : rows + reach], inverse_ref[2 * rows - reach :],
        ],
        axis=0,
    )
    half = jnp.dot(lines, product_ref[...], preferred_element_type=F32).astype(BF16)
    total = summed_intensity(half, 2 * reach, kernels, cols, spread_ref[...], weights_ref)
    values = total.astype(BF16).astype(F32)
    top, bottom = values[:reach], values[reach:]
    edge_core_ref[...] = jnp.where(odd == 1, top, bottom)
    edge_chip_ref[...] = jnp.where(odd == 1, bottom, top)


def imaging_kernel(weights_ref, product_ref, inverse_ref, spread_ref, intensity_ref, half_ref):
    rows, samples = intensity_ref.shape
    cols = samples // 2
    kernels = product_ref.shape[1] // cols
    half_ref[...] = jnp.dot(
        inverse_ref[...], product_ref[...], preferred_element_type=F32
    ).astype(BF16)
    total = summed_intensity(half_ref, rows, kernels, cols, spread_ref[...], weights_ref)
    intensity_ref[...] = total.astype(BF16)


def site_means(table, coords):
    tile_rows, tile_cols = table.shape
    slots = coords.shape[1]
    width = 256
    low_line = lax.broadcasted_iota(jnp.int32, (width, slots), 0).astype(F32).astype(BF16)
    none = jnp.zeros((width, slots), BF16)
    eight = lax.broadcasted_iota(jnp.int32, (8, slots), 0).astype(F32)
    groups = BLOCK // 8
    blocks = tile_rows // BLOCK
    total = jnp.zeros((8, slots), F32)
    for site in range(SITES):
        col_pos = coords[SITES + site : SITES + site + 1] * (tile_cols - 1)
        low = jnp.minimum(jnp.floor(col_pos), tile_cols - 2.0)
        part = col_pos - low
        low_weight = jnp.broadcast_to((1.0 - part).astype(BF16), (width, slots))
        high_weight = jnp.broadcast_to(part.astype(BF16), (width, slots))
        tents = []
        for start in range(0, tile_cols, width):
            hits = []
            for index in (low - start, low + (1.0 - start)):
                inside = jnp.logical_and(index >= 0.0, index < width)
                index = jnp.where(inside, index, -1.0).astype(BF16)
                hits.append(low_line == jnp.broadcast_to(index, (width, slots)))
            tents.append(jnp.where(hits[0], low_weight, jnp.where(hits[1], high_weight, none)))
        picked = jnp.dot(table, jnp.concatenate(tents, axis=0), preferred_element_type=F32)
        row_pos = coords[site : site + 1] * (tile_rows - 1)
        block = jnp.minimum(jnp.floor(row_pos * (1.0 / BLOCK)), blocks - 1.0)
        within = jnp.broadcast_to(row_pos - block * BLOCK, (8, slots))
        block = jnp.broadcast_to(block, (8, slots))
        held = [jnp.zeros((8, slots), F32) for _ in range(groups + 1)]
        for b in range(blocks):
            hit = block == float(b)
            for g in range(groups + 1 if b < blocks - 1 else groups):
                first = b * BLOCK + 8 * g
                held[g] = jnp.where(hit, picked[first : first + 8], held[g])
        for g in range(groups + 1):
            weight = jnp.maximum(1.0 - jnp.abs(within - (eight + 8.0 * g)), 0.0)
            total = total + held[g] * weight
    return jnp.broadcast_to(jnp.sum(total, axis=0, keepdims=True) * (1.0 / SITES), (8, slots))


def resist_kernel(
    intensity_ref, core_ref, near_ref, far_ref, inner_ref, outer_ref, high_ref, low_ref,
    coords_near_ref, coords_far_ref,
    resist_ref, table_ref, mean_chip_ref,
):
    odd = parity()
    chip_edge = jnp.where(has_chip_side(), from_chip(near_ref, far_ref), 0.0)
    core_edge = core_ref[...]
    above = jnp.where(odd == 1, core_edge, chip_edge)
    below = jnp.where(odd == 1, chip_edge, core_edge)
    edges = jnp.concatenate([above, below], axis=0).astype(BF16)
    blurred = jnp.dot(inner_ref[...], intensity_ref[...], preferred_element_type=F32)
    blurred += jnp.dot(outer_ref[...], edges, preferred_element_type=F32)
    high = blurred.astype(BF16)
    low = (blurred - high.astype(F32)).astype(BF16)
    resist = (
        jnp.dot(high, high_ref[...], preferred_element_type=F32)
        + jnp.dot(low, high_ref[...], preferred_element_type=F32)
        + jnp.dot(high, low_ref[...], preferred_element_type=F32)
    )
    resist_ref[...] = resist
    table_ref[...] = resist.astype(BF16)
    mean_chip_ref[...] = site_means(table_ref[...], from_chip(coords_near_ref, coords_far_ref))


def mean_kernel(table_ref, coords_ref, mean_ref):
    mean_ref[...] = site_means(table_ref[...], coords_ref[...])


def bias_kernel(threshold_ref, chosen_ref, own_ref, core_ref, near_ref, far_ref, steps_ref, out_ref):
    frags = steps_ref.shape[1]
    odd = parity()
    lanes = lax.broadcasted_iota(jnp.int32, own_ref.shape, 0)
    total = jnp.zeros((8, frags), F32)
    for side, mean in (
        (1, own_ref[...]), (2 - 2 * odd, core_ref[...]), (2 * odd, from_chip(near_ref, far_ref))
    ):
        first, second, third = (part.astype(F32) for part in three_parts(mean))
        parts = jnp.where(
            lanes == 0, first, jnp.where(lanes == 1, second, jnp.where(lanes == 2, third, 0.0))
        ).astype(BF16)
        total = total + jnp.dot(parts, chosen_ref[side], preferred_element_type=F32)
    site_mean = jnp.sum(total, axis=0, keepdims=True)
    out_ref[...] = bias_step * steps_ref[...].astype(F32) - bias_gain * (
        site_mean - threshold_ref[0]
    )


def swaps(count):
    def whole(pairs):
        partner = {}
        for a, b in pairs:
            partner[a], partner[b] = b, a
        return [(i, partner[i]) for i in range(count)]

    quads = count // 4
    core = [(i, i + 1) for i in range(0, count, 2)]
    near = [(i + 1, i + 2) for i in range(0, count, 4)]
    for quad in range(0, quads - 1, 2):
        near += [(4 * quad + i, 4 * quad + 4 + i) for i in (0, 3)]
    if quads % 2:
        near.append((count - 4, count - 1))
    far = [(0, 1), (count - 2, count - 1)] + [(i + 3, i + 4) for i in range(0, count - 4, 4)]
    far += [(i + 2, i + 5) for i in range(0, count - 4, 4)]
    return whole(core), whole(near), whole(far)


def exchange_chip(to_chip):
    _, near, far = swaps(lax.axis_size("tx"))
    return lax.ppermute(to_chip, "tx", near), lax.ppermute(to_chip, "tx", far)


def exchange_core(to_core):
    return lax.ppermute(to_core, "tx", swaps(lax.axis_size("tx"))[0])


def call(kernel, outs, args, smem=(), hbm=(), scratch=(), name=None):
    specs = [
        pl.BlockSpec(
            memory_space=pltpu.SMEM if i in smem else pltpu.HBM if i in hbm else pltpu.VMEM
        )
        for i in range(len(args))
    ]
    args = [
        pltpu.with_memory_space_constraint(arg, pltpu.HBM) if i in hbm else arg
        for i, arg in enumerate(args)
    ]
    return pl.pallas_call(
        kernel,
        out_shape=[jax.ShapeDtypeStruct(s, d) for s, d in outs],
        in_specs=specs,
        out_specs=[pl.BlockSpec(memory_space=pltpu.VMEM) for _ in outs],
        scratch_shapes=list(scratch),
        compiler_params=pltpu.CompilerParams(vmem_limit_bytes=VMEM_BYTES),
        name=name,
    )(*args)


def shards(mask, kernel_spectra, kernel_weights, threshold, eval_tile, site_coords, bias_steps):
    tile_rows, tile_cols = mask.shape
    _, row_freqs, kernels, col_freqs = kernel_spectra.shape
    frags = eval_tile.shape[0]
    capacity = frags // 2
    samples = 2 * col_freqs
    flat = kernels * col_freqs
    records = 2 * SITES
    col_forward, row_blocks, row_inverse, col_inverse = imaging_tables(
        tile_rows, tile_cols, row_freqs, col_freqs
    )
    (high, low), inner, outer = blur_tables(tile_rows, tile_cols, col_freqs, BLUR_REACH)
    spectrum = ((2 * row_freqs, col_freqs), F32)
    packed = ((records, capacity), F32)
    edge = ((BLUR_REACH, samples), F32)
    means = ((8, capacity), F32)
    weights = kernel_weights.reshape(1, kernels)

    own, to_core, to_chip, packed_core, packed_chip, packed_own, chosen = call(
        front_kernel,
        [spectrum] * 3 + [packed] * 3 + [((3, capacity, frags), BF16)],
        (
            eval_tile.reshape(1, frags), site_coords.reshape(records, frags),
            mask, col_forward, row_blocks,
        ),
        hbm=range(5),
        scratch=[
            pltpu.VMEM((1, frags), jnp.int32),
            pltpu.VMEM((records, frags), F32),
            pltpu.VMEM(mask.shape, BF16),
            pltpu.VMEM(col_forward.shape, BF16),
            pltpu.VMEM(row_blocks.shape, BF16),
            pltpu.SemaphoreType.DMA((5,)),
        ],
        name="front",
    )
    got_near, got_far = exchange_chip(to_chip)
    got_core = exchange_core(to_core)
    coords_near, coords_far = exchange_chip(packed_chip)
    coords_core = exchange_core(packed_core)
    inverse, spread = call(
        load_kernel,
        [(row_inverse.shape, BF16), (col_inverse.shape, BF16)],
        (own, row_inverse, col_inverse),
        hbm=(1, 2),
        scratch=[pltpu.SemaphoreType.DMA((2,))],
        name="load",
    )
    product, edge_core, edge_chip = call(
        edge_kernel,
        [((2 * row_freqs, flat), BF16), edge, edge],
        (
            weights, own, got_core, got_near, got_far,
            jnp.transpose(kernel_spectra, (0, 2, 1, 3)), inverse, spread,
        ),
        smem=(0,),
        name="edges",
    )
    edge_near, edge_far = exchange_chip(edge_chip)
    edge_core = exchange_core(edge_core)
    (intensity,) = call(
        imaging_kernel,
        [((tile_rows, samples), BF16)],
        (weights, product, inverse, spread),
        smem=(0,),
        scratch=[pltpu.VMEM((2 * tile_rows, flat), BF16)],
        name="imaging",
    )
    resist, table, mean_chip = call(
        resist_kernel,
        [((tile_rows, tile_cols), F32), ((tile_rows, tile_cols), BF16), means],
        (
            intensity, edge_core, edge_near, edge_far, inner, outer, high, low,
            coords_near, coords_far,
        ),
        name="resist",
    )
    back_near, back_far = exchange_chip(mean_chip)
    (mean_core,) = call(mean_kernel, [means], (table, coords_core), name="mean_core")
    back_core = exchange_core(mean_core)
    (mean_own,) = call(mean_kernel, [means], (table, packed_own), name="mean_own")
    (new_bias,) = call(
        bias_kernel,
        [((1, frags), F32)],
        (
            threshold, chosen, mean_own, back_core, back_near, back_far,
            bias_steps.reshape(1, frags),
        ),
        smem=(0,),
        name="bias",
    )
    return resist, new_bias.reshape(frags)


def solution(mesh):
    placed = (
        P(("groups", "tx"), None),
        P(),
        P(),
        P(),
        P(("groups", "tx")),
        P(None, None, ("groups", "tx")),
        P(("groups", "tx")),
    )
    return jax.shard_map(
        shards,
        mesh=mesh,
        in_specs=placed,
        out_specs=(P(("groups", "tx"), None), P(("groups", "tx"))),
        check_vma=False,
    )
```

```python
import math

import jax
import jax.numpy as jnp
import ml_dtypes
import numpy as np
from jax import lax
from jax.experimental import pallas as pl
from jax.experimental.pallas import tpu as pltpu
from jax.sharding import PartitionSpec as P

HALO = 256
BLUR_REACH = 8
SITES = 16

blur_sigma = 3.0
bias_step = 0.5
bias_gain = 2.0

F32 = jnp.float32
BF16 = jnp.bfloat16
BLOCK = 64
VMEM_BYTES = 48 * 1024 * 1024


def rounded(table):
    return np.asarray(table, np.float32).astype(ml_dtypes.bfloat16)


def halves(table):
    high = rounded(table)
    low = rounded(np.asarray(table, np.float64) - high.astype(np.float64))
    return high, low


def twiddle(position, frequency, period, amplitude):
    phase_index = (position[:, None] * frequency[None, :]) % period
    phase_angle = phase_index * (2.0 * math.pi / period)
    return np.cos(phase_angle) * amplitude, np.sin(phase_angle) * amplitude


def centered(count):
    return np.arange(count) - count // 2


def imaging_tables(tile_rows, tile_cols, row_freqs, col_freqs):
    window_rows = tile_rows + 2 * HALO
    col_cos, col_sin = twiddle(
        np.arange(tile_cols), centered(col_freqs), tile_cols, 1.0 / math.sqrt(tile_cols)
    )
    col_forward = rounded(np.concatenate([col_cos, -col_sin], axis=1))
    row_cos, row_sin = twiddle(
        centered(row_freqs), np.arange(window_rows), window_rows, 1.0 / math.sqrt(window_rows)
    )
    row_forward = rounded(np.concatenate([row_cos, -row_sin], axis=0))
    row_blocks = np.concatenate(
        [row_forward[:, i * tile_rows : (i + 1) * tile_rows] for i in range(3)], axis=0
    )
    back_cos, back_sin = twiddle(
        np.arange(tile_rows) + HALO, centered(row_freqs), window_rows, 1.0 / math.sqrt(row_freqs)
    )
    row_inverse = rounded(
        np.block([[back_cos, -back_sin], [back_sin, back_cos]])
    )
    samples = 2 * col_freqs
    step = tile_cols // samples
    out_cos, out_sin = twiddle(
        centered(col_freqs), np.arange(samples) * step, tile_cols, 1.0 / math.sqrt(col_freqs)
    )
    col_inverse = rounded(np.block([[out_cos, out_sin], [-out_sin, out_cos]]))
    return col_forward, row_blocks, row_inverse, col_inverse


def blur_weight(offset, reach):
    every = np.arange(-reach, reach + 1).astype(np.float64)
    norm = np.sum(np.exp(-every * every / (2.0 * blur_sigma * blur_sigma)))
    weight = np.exp(-offset.astype(np.float64) ** 2 / (2.0 * blur_sigma * blur_sigma)) / norm
    return np.where(np.abs(offset) <= reach, weight, 0.0)


def blur_tables(tile_rows, tile_cols, col_freqs, reach):
    line = np.arange(tile_cols)
    col_blur = rounded(blur_weight(line[None, :] - line[:, None], reach))
    samples = 2 * col_freqs
    step = tile_cols // samples
    offset = (line[None, :] - step * np.arange(samples)[:, None]).astype(np.float64)
    half = np.where(offset == 0, 1.0, np.sin(math.pi * offset / tile_cols))
    spread = np.where(
        offset == 0,
        (samples - 1) / samples,
        np.sin((samples - 1) * math.pi * offset / tile_cols) / (samples * half),
    )
    spread_blur = spread @ col_blur.astype(np.float64)
    row_diff = (
        np.arange(tile_rows + 2 * reach)[None, :] - reach - np.arange(tile_rows)[:, None]
    )
    row_blur = rounded(blur_weight(row_diff, reach))
    inner = row_blur[:, reach : reach + tile_rows]
    outer = np.concatenate([row_blur[:, :reach], row_blur[:, reach + tile_rows :]], axis=1)
    return halves(spread_blur), np.ascontiguousarray(inner), np.ascontiguousarray(outer)


def parity():
    return lax.rem(lax.axis_index("tx"), 2)


def has_chip_side():
    me = lax.axis_index("tx")
    return jnp.logical_and(me != 0, me != lax.axis_size("tx") - 1)


def three_parts(values):
    first = values.astype(BF16)
    rest = values - first.astype(F32)
    second = rest.astype(BF16)
    third = (rest - second.astype(F32)).astype(BF16)
    return first, second, third


def transposed_dot(left, right):
    return lax.dot_general(left, right, (((1,), (1,)), ((), ())), preferred_element_type=F32)


def front_kernel(
    eval_hbm, records_hbm, mask_hbm, forward_hbm, rows_hbm, inverse_hbm, spread_hbm,
    inverse_ref, spread_ref, own_ref, core_ref, chip_ref, packed_core_ref, packed_chip_ref, packed_own_ref, chosen_ref,
    eval_ref, records_ref, mask_ref, forward_ref, rows_ref, sems,
):
    copies = [
        pltpu.make_async_copy(source, target, sems.at[i])
        for i, (source, target) in enumerate(
            (
                (eval_hbm, eval_ref),
                (records_hbm, records_ref),
                (mask_hbm, mask_ref),
                (forward_hbm, forward_ref),
                (rows_hbm, rows_ref),
                (inverse_hbm, inverse_ref),
                (spread_hbm, spread_ref),
            )
        )
    ]
    for copy in copies:
        copy.start()
    me = lax.axis_index("tx")
    odd = parity()
    frags = eval_ref.shape[1]
    capacity = frags // 2
    count = records_ref.shape[0]
    before = lax.broadcasted_iota(jnp.int32, (frags, frags), 0)
    after = lax.broadcasted_iota(jnp.int32, (frags, frags), 1)
    upper = (before <= after).astype(F32).astype(BF16)
    slots = lax.broadcasted_iota(jnp.int32, (capacity, frags), 0).astype(F32).astype(BF16)
    copies[0].wait()
    copies[1].wait()
    member = lax.broadcasted_iota(jnp.int32, (8, frags), 0) == eval_ref[...] - me + 1
    counts = jnp.dot(member.astype(F32).astype(BF16), upper, preferred_element_type=F32)
    code = jnp.where(member, counts - 1.0, -1.0)
    for side in range(3):
        row = jnp.broadcast_to(code[side : side + 1].astype(BF16), (capacity, frags))
        chosen_ref[side] = jnp.where(slots == row, jnp.ones_like(slots), jnp.zeros_like(slots))
    pieces = jnp.concatenate(three_parts(records_ref[...]), axis=0)

    def packed(side, out_ref):
        got = transposed_dot(pieces, chosen_ref[side])
        out_ref[...] = got[:count] + got[count : 2 * count] + got[2 * count :]

    packed(2 - 2 * odd, packed_core_ref)
    packed(2 * odd, packed_chip_ref)
    packed(1, packed_own_ref)

    for copy in copies[2:5]:
        copy.wait()
    col_spectra = jnp.dot(mask_ref[...], forward_ref[...], preferred_element_type=F32).astype(BF16)
    product = jnp.dot(rows_ref[...], col_spectra, preferred_element_type=F32)
    freqs, cols = own_ref.shape[0] // 2, own_ref.shape[1]

    def partial(block):
        part = product[2 * freqs * block : 2 * freqs * (block + 1)]
        real = part[:freqs, :cols] - part[freqs:, cols:]
        imag = part[:freqs, cols:] + part[freqs:, :cols]
        return jnp.concatenate([real, imag], axis=0)

    upper_side, own, lower_side = partial(0), partial(1), partial(2)
    chip_ref[...] = jnp.where(odd == 1, upper_side, lower_side)
    core_ref[...] = jnp.where(odd == 1, lower_side, upper_side)
    own_ref[...] = own
    for copy in copies[5:]:
        copy.wait()


def summed_intensity(half, rows, kernels, cols, spread, weights_ref):
    total = None
    for k in range(kernels):
        lanes = slice(k * cols, (k + 1) * cols)
        pair = jnp.concatenate([half[:rows, lanes], half[rows:, lanes]], axis=1)
        field = jnp.dot(pair, spread, preferred_element_type=F32)
        real, imag = field[:, : 2 * cols], field[:, 2 * cols :]
        term = weights_ref[0, k] * (real * real + imag * imag)
        total = term if total is None else total + term
    return total


def edge_kernel(
    weights_ref, own_ref, core_ref, chip_ref, kern_ref, inverse_ref, spread_ref,
    product_ref, edge_core_ref, edge_chip_ref,
):
    freqs, cols = own_ref.shape[0] // 2, own_ref.shape[1]
    rows = inverse_ref.shape[0] // 2
    kernels = kern_ref.shape[1]
    odd = parity()
    chip = jnp.where(has_chip_side(), chip_ref[...], 0.0)
    spectrum = own_ref[...] + core_ref[...] + chip
    spec_real, spec_imag = spectrum[:freqs], spectrum[freqs:]
    for k in range(kernels):
        kern_real, kern_imag = kern_ref[0, k], kern_ref[1, k]
        lanes = slice(k * cols, (k + 1) * cols)
        product_ref[:freqs, lanes] = (kern_real * spec_real - kern_imag * spec_imag).astype(BF16)
        product_ref[freqs:, lanes] = (kern_real * spec_imag + kern_imag * spec_real).astype(BF16)
    reach = BLUR_REACH
    lines = jnp.concatenate(
        [
            inverse_ref[:reach], inverse_ref[rows - reach : rows],
            inverse_ref[rows : rows + reach], inverse_ref[2 * rows - reach :],
        ],
        axis=0,
    )
    half = jnp.dot(lines, product_ref[...], preferred_element_type=F32).astype(BF16)
    pairs = jnp.concatenate(
        [
            jnp.concatenate(
                [half[: 2 * reach, k * cols : (k + 1) * cols], half[2 * reach :, k * cols : (k + 1) * cols]],
                axis=1,
            )
            for k in range(kernels)
        ],
        axis=0,
    )
    field = jnp.dot(pairs, spread_ref[...], preferred_element_type=F32)
    total = jnp.zeros((2 * reach, 2 * cols), F32)
    for k in range(kernels):
        part = field[2 * reach * k : 2 * reach * (k + 1)]
        real, imag = part[:, : 2 * cols], part[:, 2 * cols :]
        total = total + weights_ref[0, k] * (real * real + imag * imag)
    values = total.astype(BF16).astype(F32)
    top, bottom = values[:reach], values[reach:]
    edge_core_ref[...] = jnp.where(odd == 1, top, bottom)
    edge_chip_ref[...] = jnp.where(odd == 1, bottom, top)


def imaging_kernel(weights_ref, product_ref, inverse_ref, spread_ref, intensity_ref, half_ref):
    rows, samples = intensity_ref.shape
    cols = samples // 2
    kernels = product_ref.shape[1] // cols
    half_ref[...] = jnp.dot(
        inverse_ref[...], product_ref[...], preferred_element_type=F32
    ).astype(BF16)
    total = summed_intensity(half_ref, rows, kernels, cols, spread_ref[...], weights_ref)
    intensity_ref[...] = total.astype(BF16)


def site_means(table, coords):
    tile_rows, tile_cols = table.shape
    slots = coords.shape[1]
    width = 256
    low_line = lax.broadcasted_iota(jnp.int32, (width, slots), 0).astype(F32).astype(BF16)
    none = jnp.zeros((width, slots), BF16)
    eight = lax.broadcasted_iota(jnp.int32, (8, slots), 0).astype(F32)
    groups = BLOCK // 8
    blocks = tile_rows // BLOCK
    total = jnp.zeros((8, slots), F32)
    for site in range(SITES):
        col_pos = coords[SITES + site : SITES + site + 1] * (tile_cols - 1)
        low = jnp.minimum(jnp.floor(col_pos), tile_cols - 2.0)
        part = col_pos - low
        low_weight = jnp.broadcast_to((1.0 - part).astype(BF16), (width, slots))
        high_weight = jnp.broadcast_to(part.astype(BF16), (width, slots))
        tents = []
        for start in range(0, tile_cols, width):
            hits = []
            for index in (low - start, low + (1.0 - start)):
                inside = jnp.logical_and(index >= 0.0, index < width)
                index = jnp.where(inside, index, -1.0).astype(BF16)
                hits.append(low_line == jnp.broadcast_to(index, (width, slots)))
            tents.append(jnp.where(hits[0], low_weight, jnp.where(hits[1], high_weight, none)))
        picked = jnp.dot(table, jnp.concatenate(tents, axis=0), preferred_element_type=F32)
        row_pos = coords[site : site + 1] * (tile_rows - 1)
        block = jnp.minimum(jnp.floor(row_pos * (1.0 / BLOCK)), blocks - 1.0)
        within = jnp.broadcast_to(row_pos - block * BLOCK, (8, slots))
        block = jnp.broadcast_to(block, (8, slots))
        held = [jnp.zeros((8, slots), F32) for _ in range(groups + 1)]
        for b in range(blocks):
            hit = block == float(b)
            for g in range(groups + 1 if b < blocks - 1 else groups):
                first = b * BLOCK + 8 * g
                held[g] = jnp.where(hit, picked[first : first + 8], held[g])
        for g in range(groups + 1):
            weight = jnp.maximum(1.0 - jnp.abs(within - (eight + 8.0 * g)), 0.0)
            total = total + held[g] * weight
    return jnp.broadcast_to(jnp.sum(total, axis=0, keepdims=True) * (1.0 / SITES), (8, slots))


def resist_kernel(
    intensity_ref, core_ref, chip_ref, inner_ref, outer_ref, high_ref, low_ref,
    coords_ref,
    resist_hbm, table_ref, mean_chip_ref,
    resist_ref, sem,
):
    odd = parity()
    chip_edge = jnp.where(has_chip_side(), chip_ref[...], 0.0)
    core_edge = core_ref[...]
    above = jnp.where(odd == 1, core_edge, chip_edge)
    below = jnp.where(odd == 1, chip_edge, core_edge)
    edges = jnp.concatenate([above, below], axis=0).astype(BF16)
    blurred = jnp.dot(inner_ref[...], intensity_ref[...], preferred_element_type=F32)
    blurred += jnp.dot(outer_ref[...], edges, preferred_element_type=F32)
    high = blurred.astype(BF16)
    low = (blurred - high.astype(F32)).astype(BF16)
    resist = (
        jnp.dot(high, high_ref[...], preferred_element_type=F32)
        + jnp.dot(low, high_ref[...], preferred_element_type=F32)
        + jnp.dot(high, low_ref[...], preferred_element_type=F32)
    )
    resist_ref[...] = resist
    copy = pltpu.make_async_copy(resist_ref, resist_hbm, sem)
    copy.start()
    table_ref[...] = resist.astype(BF16)
    mean_chip_ref[...] = site_means(table_ref[...], coords_ref[...])
    copy.wait()


def mean_kernel(table_ref, coords_ref, mean_ref):
    mean_ref[...] = site_means(table_ref[...], coords_ref[...])


def bias_kernel(threshold_ref, chosen_ref, own_ref, core_ref, chip_ref, steps_ref, out_ref):
    frags = steps_ref.shape[1]
    odd = parity()
    lanes = lax.broadcasted_iota(jnp.int32, own_ref.shape, 0)
    total = jnp.zeros((8, frags), F32)
    for side, mean in (
        (1, own_ref[...]), (2 - 2 * odd, core_ref[...]), (2 * odd, chip_ref[...])
    ):
        first, second, third = (part.astype(F32) for part in three_parts(mean))
        parts = jnp.where(
            lanes == 0, first, jnp.where(lanes == 1, second, jnp.where(lanes == 2, third, 0.0))
        ).astype(BF16)
        total = total + jnp.dot(parts, chosen_ref[side], preferred_element_type=F32)
    site_mean = jnp.sum(total, axis=0, keepdims=True)
    out_ref[...] = bias_step * steps_ref[...].astype(F32) - bias_gain * (
        site_mean - threshold_ref[0]
    )


def chip_pairs(groups, count):
    pairs = []
    for group in range(groups):
        first = group * count
        for i in range(1, count - 1, 2):
            pairs += [(first + i, first + i + 1), (first + i + 1, first + i)]
    if groups % 2:
        for group in range(groups):
            pairs += [(group * count, (group + 1) * count - 1), ((group + 1) * count - 1, group * count)]
    else:
        for group in range(groups):
            for end in (0, count - 1):
                pairs.append((group * count + end, (group ^ 1) * count + end))
    return pairs


def swap_chips(to_chip):
    pairs = chip_pairs(lax.axis_size("groups"), lax.axis_size("tx"))
    return lax.ppermute(to_chip, ("groups", "tx"), pairs)


def swap_cores(to_core):
    return lax.ppermute(to_core, "tx", [(i, i ^ 1) for i in range(lax.axis_size("tx"))])


def call(kernel, outs, args, smem=(), hbm=(), hbm_outs=(), scratch=(), name=None):
    specs = [
        pl.BlockSpec(
            memory_space=pltpu.SMEM if i in smem else pltpu.HBM if i in hbm else pltpu.VMEM
        )
        for i in range(len(args))
    ]
    args = [
        pltpu.with_memory_space_constraint(arg, pltpu.HBM) if i in hbm else arg
        for i, arg in enumerate(args)
    ]
    return pl.pallas_call(
        kernel,
        out_shape=[jax.ShapeDtypeStruct(s, d) for s, d in outs],
        in_specs=specs,
        out_specs=[
            pl.BlockSpec(memory_space=pltpu.HBM if i in hbm_outs else pltpu.VMEM)
            for i in range(len(outs))
        ],
        scratch_shapes=list(scratch),
        compiler_params=pltpu.CompilerParams(vmem_limit_bytes=VMEM_BYTES),
        name=name,
    )(*args)


def shards(mask, kernel_spectra, kernel_weights, threshold, eval_tile, site_coords, bias_steps):
    tile_rows, tile_cols = mask.shape
    _, row_freqs, kernels, col_freqs = kernel_spectra.shape
    frags = eval_tile.shape[0]
    capacity = frags // 2
    samples = 2 * col_freqs
    flat = kernels * col_freqs
    records = 2 * SITES
    col_forward, row_blocks, row_inverse, col_inverse = imaging_tables(
        tile_rows, tile_cols, row_freqs, col_freqs
    )
    (high, low), inner, outer = blur_tables(tile_rows, tile_cols, col_freqs, BLUR_REACH)
    spectrum = ((2 * row_freqs, col_freqs), F32)
    packed = ((records, capacity), F32)
    edge = ((BLUR_REACH, samples), F32)
    means = ((8, capacity), F32)
    weights = kernel_weights.reshape(1, kernels)

    inverse, spread, own, to_core, to_chip, packed_core, packed_chip, packed_own, chosen = call(
        front_kernel,
        [(row_inverse.shape, BF16), (col_inverse.shape, BF16)]
        + [spectrum] * 3
        + [packed] * 3
        + [((3, capacity, frags), BF16)],
        (
            eval_tile.reshape(1, frags), site_coords.reshape(records, frags),
            mask, col_forward, row_blocks, row_inverse, col_inverse,
        ),
        hbm=range(7),
        scratch=[
            pltpu.VMEM((1, frags), jnp.int32),
            pltpu.VMEM((records, frags), F32),
            pltpu.VMEM(mask.shape, BF16),
            pltpu.VMEM(col_forward.shape, BF16),
            pltpu.VMEM(row_blocks.shape, BF16),
            pltpu.SemaphoreType.DMA((7,)),
        ],
        name="front",
    )
    got_chip = swap_chips(to_chip)
    got_core = swap_cores(to_core)
    coords_chip = swap_chips(packed_chip)
    coords_core = swap_cores(packed_core)
    product, edge_core, edge_chip = call(
        edge_kernel,
        [((2 * row_freqs, flat), BF16), edge, edge],
        (
            weights, own, got_core, got_chip,
            jnp.transpose(kernel_spectra, (0, 2, 1, 3)), inverse, spread,
        ),
        smem=(0,),
        name="edges",
    )
    edge_chip = swap_chips(edge_chip)
    edge_core = swap_cores(edge_core)
    (intensity,) = call(
        imaging_kernel,
        [((tile_rows, samples), BF16)],
        (weights, product, inverse, spread),
        smem=(0,),
        scratch=[pltpu.VMEM((2 * tile_rows, flat), BF16)],
        name="imaging",
    )
    resist, table, mean_chip = call(
        resist_kernel,
        [((tile_rows, tile_cols), F32), ((tile_rows, tile_cols), BF16), means],
        (intensity, edge_core, edge_chip, inner, outer, high, low, coords_chip),
        hbm_outs=(0,),
        scratch=[pltpu.VMEM((tile_rows, tile_cols), F32), pltpu.SemaphoreType.DMA],
        name="resist",
    )
    back_chip = swap_chips(mean_chip)
    (mean_core,) = call(mean_kernel, [means], (table, coords_core), name="mean_core")
    back_core = swap_cores(mean_core)
    (mean_own,) = call(mean_kernel, [means], (table, packed_own), name="mean_own")
    (new_bias,) = call(
        bias_kernel,
        [((1, frags), F32)],
        (threshold, chosen, mean_own, back_core, back_chip, bias_steps.reshape(1, frags)),
        smem=(0,),
        name="bias",
    )
    return resist, new_bias.reshape(frags)


def solution(mesh):
    placed = (
        P(("groups", "tx"), None),
        P(),
        P(),
        P(),
        P(("groups", "tx")),
        P(None, None, ("groups", "tx")),
        P(("groups", "tx")),
    )
    return jax.shard_map(
        shards,
        mesh=mesh,
        in_specs=placed,
        out_specs=(P(("groups", "tx"), None), P(("groups", "tx"))),
        check_vma=False,
    )
```

```python
import math

import jax
import jax.numpy as jnp
import ml_dtypes
import numpy as np
from jax import lax
from jax.experimental import pallas as pl
from jax.experimental.pallas import tpu as pltpu
from jax.sharding import PartitionSpec as P

HALO = 256
BLUR_REACH = 8
SITES = 16

blur_sigma = 3.0
bias_step = 0.5
bias_gain = 2.0

F32 = jnp.float32
BF16 = jnp.bfloat16
BLOCK = 64
TOGETHER = 12
VMEM_BYTES = 48 * 1024 * 1024


def rounded(table):
    return np.asarray(table, np.float32).astype(ml_dtypes.bfloat16)


def halves(table):
    high = rounded(table)
    low = rounded(np.asarray(table, np.float64) - high.astype(np.float64))
    return high, low


def twiddle(position, frequency, period, amplitude):
    phase_index = (position[:, None] * frequency[None, :]) % period
    phase_angle = phase_index * (2.0 * math.pi / period)
    return np.cos(phase_angle) * amplitude, np.sin(phase_angle) * amplitude


def centered(count):
    return np.arange(count) - count // 2


def imaging_tables(tile_rows, tile_cols, row_freqs, col_freqs):
    window_rows = tile_rows + 2 * HALO
    col_cos, col_sin = twiddle(
        np.arange(tile_cols), centered(col_freqs), tile_cols, 1.0 / math.sqrt(tile_cols)
    )
    col_forward = rounded(np.concatenate([col_cos, -col_sin], axis=1))
    row_cos, row_sin = twiddle(
        centered(row_freqs), np.arange(window_rows), window_rows, 1.0 / math.sqrt(window_rows)
    )
    row_forward = rounded(np.concatenate([row_cos, -row_sin], axis=0))
    row_blocks = np.concatenate(
        [row_forward[:, i * tile_rows : (i + 1) * tile_rows] for i in range(3)], axis=0
    )
    back_cos, back_sin = twiddle(
        np.arange(tile_rows) + HALO, centered(row_freqs), window_rows, 1.0 / math.sqrt(row_freqs)
    )
    row_inverse = rounded(
        np.block([[back_cos, -back_sin], [back_sin, back_cos]])
    )
    samples = 2 * col_freqs
    step = tile_cols // samples
    out_cos, out_sin = twiddle(
        centered(col_freqs), np.arange(samples) * step, tile_cols, 1.0 / math.sqrt(col_freqs)
    )
    col_inverse = rounded(np.block([[out_cos, out_sin], [-out_sin, out_cos]]))
    return col_forward, row_blocks, row_inverse, col_inverse


def blur_weight(offset, reach):
    every = np.arange(-reach, reach + 1).astype(np.float64)
    norm = np.sum(np.exp(-every * every / (2.0 * blur_sigma * blur_sigma)))
    weight = np.exp(-offset.astype(np.float64) ** 2 / (2.0 * blur_sigma * blur_sigma)) / norm
    return np.where(np.abs(offset) <= reach, weight, 0.0)


def blur_tables(tile_rows, tile_cols, col_freqs, reach):
    line = np.arange(tile_cols)
    col_blur = rounded(blur_weight(line[None, :] - line[:, None], reach))
    samples = 2 * col_freqs
    step = tile_cols // samples
    offset = (line[None, :] - step * np.arange(samples)[:, None]).astype(np.float64)
    half = np.where(offset == 0, 1.0, np.sin(math.pi * offset / tile_cols))
    spread = np.where(
        offset == 0,
        (samples - 1) / samples,
        np.sin((samples - 1) * math.pi * offset / tile_cols) / (samples * half),
    )
    spread_blur = spread @ col_blur.astype(np.float64)
    row_diff = (
        np.arange(tile_rows + 2 * reach)[None, :] - reach - np.arange(tile_rows)[:, None]
    )
    row_blur = rounded(blur_weight(row_diff, reach))
    inner = row_blur[:, reach : reach + tile_rows]
    outer = np.concatenate([row_blur[:, :reach], row_blur[:, reach + tile_rows :]], axis=1)
    high, low = halves(spread_blur)
    return np.concatenate([high, high, low], axis=0), np.ascontiguousarray(inner), np.ascontiguousarray(outer)


def parity():
    return lax.rem(lax.axis_index("tx"), 2)


def has_chip_side():
    me = lax.axis_index("tx")
    return jnp.logical_and(me != 0, me != lax.axis_size("tx") - 1)


def three_parts(values):
    first = values.astype(BF16)
    rest = values - first.astype(F32)
    second = rest.astype(BF16)
    third = (rest - second.astype(F32)).astype(BF16)
    return first, second, third


def transposed_dot(left, right):
    return lax.dot_general(left, right, (((1,), (1,)), ((), ())), preferred_element_type=F32)


def started(sems, first, *moves):
    copies = []
    for source, target, pieces in moves:
        rows = source.shape[0] // pieces
        for i in range(pieces):
            part = pl.ds(i * rows, rows)
            copies.append(
                pltpu.make_async_copy(
                    source.at[part], target.at[part], sems.at[first + len(copies)]
                )
            )
            copies[-1].start()
    return copies


def load_kernel(
    after_ref, threshold_ref, kern_hbm, inverse_hbm, spread_hbm,
    level_ref, kern_ref, inverse_ref, spread_ref, sems,
):
    copies = started(
        sems, 0, (kern_hbm, kern_ref, 2), (inverse_hbm, inverse_ref, 1), (spread_hbm, spread_ref, 1)
    )
    level_ref[...] = jnp.full(level_ref.shape, threshold_ref[0], F32)
    for copy in copies:
        copy.wait()


def front_kernel(
    eval_hbm, records_hbm, mask_hbm, forward_hbm, rows_hbm,
    own_ref, core_ref, chip_ref, packed_core_ref, packed_chip_ref, packed_own_ref, chosen_ref,
    eval_ref, records_ref, mask_ref, forward_ref, rows_ref, sems,
):
    small = started(sems, 0, (eval_hbm, eval_ref, 1), (records_hbm, records_ref, 1))
    large = started(
        sems, 2, (mask_hbm, mask_ref, 2), (forward_hbm, forward_ref, 2), (rows_hbm, rows_ref, 1)
    )
    me = lax.axis_index("tx")
    odd = parity()
    frags = eval_ref.shape[1]
    capacity = frags // 2
    count = records_ref.shape[0]
    before = lax.broadcasted_iota(jnp.int32, (frags, frags), 0)
    after = lax.broadcasted_iota(jnp.int32, (frags, frags), 1)
    upper = (before <= after).astype(F32).astype(BF16)
    slots = lax.broadcasted_iota(jnp.int32, (capacity, frags), 0).astype(F32).astype(BF16)
    for copy in small:
        copy.wait()
    member = lax.broadcasted_iota(jnp.int32, (8, frags), 0) == eval_ref[...] - me + 1
    counts = jnp.dot(member.astype(F32).astype(BF16), upper, preferred_element_type=F32)
    code = jnp.where(member, counts - 1.0, -1.0)
    for side in range(3):
        row = jnp.broadcast_to(code[side : side + 1].astype(BF16), (capacity, frags))
        chosen_ref[pl.ds(side * capacity, capacity)] = jnp.where(slots == row, jnp.ones_like(slots), jnp.zeros_like(slots))
    pieces = jnp.concatenate(three_parts(records_ref[...]), axis=0)

    def packed(side, out_ref):
        chosen = chosen_ref[pl.ds(pl.multiple_of(side * capacity, capacity), capacity)]
        got = transposed_dot(pieces, chosen)
        out_ref[...] = got[:count] + got[count : 2 * count] + got[2 * count :]

    packed(2 - 2 * odd, packed_core_ref)
    packed(2 * odd, packed_chip_ref)
    packed(1, packed_own_ref)

    for copy in large:
        copy.wait()
    col_spectra = jnp.dot(mask_ref[...], forward_ref[...], preferred_element_type=F32).astype(BF16)
    product = jnp.dot(rows_ref[...], col_spectra, preferred_element_type=F32)
    freqs, cols = own_ref.shape[0] // 2, own_ref.shape[1]

    def partial(block):
        part = product[2 * freqs * block : 2 * freqs * (block + 1)]
        real = part[:freqs, :cols] - part[freqs:, cols:]
        imag = part[:freqs, cols:] + part[freqs:, :cols]
        return jnp.concatenate([real, imag], axis=0)

    upper_side, own, lower_side = partial(0), partial(1), partial(2)
    chip_ref[...] = jnp.where(odd == 1, upper_side, lower_side)
    core_ref[...] = jnp.where(odd == 1, lower_side, upper_side)
    own_ref[...] = own


def edge_kernel(
    weights_ref, own_ref, core_ref, chip_ref, kern_ref, inverse_ref, spread_ref,
    product_ref, edge_core_ref, edge_chip_ref,
):
    freqs, cols = own_ref.shape[0] // 2, own_ref.shape[1]
    rows = inverse_ref.shape[0] // 2
    kernels = kern_ref.shape[1]
    odd = parity()
    chip = jnp.where(has_chip_side(), chip_ref[...], 0.0)
    spectrum = own_ref[...] + core_ref[...] + chip
    spec_real, spec_imag = spectrum[:freqs], spectrum[freqs:]
    for k in range(kernels):
        kern_real, kern_imag = kern_ref[0, k], kern_ref[1, k]
        lanes = slice(k * cols, (k + 1) * cols)
        product_ref[:freqs, lanes] = (kern_real * spec_real - kern_imag * spec_imag).astype(BF16)
        product_ref[freqs:, lanes] = (kern_real * spec_imag + kern_imag * spec_real).astype(BF16)
    reach = BLUR_REACH
    lines = jnp.concatenate(
        [
            inverse_ref[:reach], inverse_ref[rows - reach : rows],
            inverse_ref[rows : rows + reach], inverse_ref[2 * rows - reach :],
        ],
        axis=0,
    )
    half = jnp.dot(lines, product_ref[...], preferred_element_type=F32).astype(BF16)
    pairs = jnp.concatenate(
        [
            jnp.concatenate(
                [half[: 2 * reach, k * cols : (k + 1) * cols], half[2 * reach :, k * cols : (k + 1) * cols]],
                axis=1,
            )
            for k in range(kernels)
        ],
        axis=0,
    )
    field = jnp.dot(pairs, spread_ref[...], preferred_element_type=F32)
    total = jnp.zeros((2 * reach, 2 * cols), F32)
    for k in range(kernels):
        part = field[2 * reach * k : 2 * reach * (k + 1)]
        real, imag = part[:, : 2 * cols], part[:, 2 * cols :]
        total = total + weights_ref[:, k : k + 1] * (real * real + imag * imag)
    values = total.astype(BF16).astype(F32)
    top, bottom = values[:reach], values[reach:]
    edge_core_ref[...] = jnp.where(odd == 1, top, bottom)
    edge_chip_ref[...] = jnp.where(odd == 1, bottom, top)


def imaging_kernel(weights_ref, product_ref, inverse_ref, spread_ref, intensity_ref):
    rows, samples = intensity_ref.shape
    cols = samples // 2
    kernels = product_ref.shape[1] // cols
    total = jnp.zeros((rows, samples), F32)
    for first in range(0, kernels, TOGETHER):
        lanes = slice(first * cols, (first + TOGETHER) * cols)
        half = jnp.dot(
            inverse_ref[...], product_ref[:, lanes], preferred_element_type=F32
        ).astype(BF16)
        pairs = [
            jnp.concatenate(
                [half[:rows, i * cols : (i + 1) * cols], half[rows:, i * cols : (i + 1) * cols]],
                axis=1,
            )
            for i in range(TOGETHER)
        ]
        fields = jnp.dot(
            jnp.concatenate(pairs, axis=0), spread_ref[...], preferred_element_type=F32
        )
        for i in range(TOGETHER):
            field = fields[i * rows : (i + 1) * rows]
            real, imag = field[:, :samples], field[:, samples:]
            k = first + i
            total = total + weights_ref[:, k : k + 1] * (real * real + imag * imag)
    intensity_ref[...] = total.astype(BF16)


def site_means(table, coords, middle):
    tile_rows, tile_cols = table.shape
    slots = coords.shape[1]
    width = 256
    low_line = lax.broadcasted_iota(jnp.int32, (width, slots), 0).astype(F32).astype(BF16)
    none = jnp.zeros((width, slots), BF16)
    eight = lax.broadcasted_iota(jnp.int32, (8, slots), 0).astype(F32)
    groups = BLOCK // 8
    blocks = tile_rows // BLOCK
    total = jnp.zeros((8, slots), F32)
    for site in range(SITES):
        col_pos = coords[SITES + site : SITES + site + 1] * (tile_cols - 1)
        low = jnp.minimum(jnp.floor(col_pos), tile_cols - 2.0)
        part = col_pos - low
        low_weight = jnp.broadcast_to((1.0 - part).astype(BF16), (width, slots))
        high_weight = jnp.broadcast_to(part.astype(BF16), (width, slots))
        tents = []
        for start in range(0, tile_cols, width):
            hits = []
            for index in (low - start, low + (1.0 - start)):
                inside = jnp.logical_and(index >= 0.0, index < width)
                index = jnp.where(inside, index, -1.0).astype(BF16)
                hits.append(low_line == jnp.broadcast_to(index, (width, slots)))
            tents.append(jnp.where(hits[0], low_weight, jnp.where(hits[1], high_weight, none)))
        picked = jnp.dot(table, jnp.concatenate(tents, axis=0), preferred_element_type=F32)
        row_pos = coords[site : site + 1] * (tile_rows - 1)
        block = jnp.minimum(jnp.floor(row_pos * (1.0 / BLOCK)), blocks - 1.0)
        within = jnp.broadcast_to(row_pos - block * BLOCK, (8, slots))
        block = jnp.broadcast_to(block, (8, slots))
        held = [jnp.zeros((8, slots), F32) for _ in range(groups + 1)]
        for b in range(blocks):
            hit = block == float(b)
            for g in range(groups + 1 if b < blocks - 1 else groups):
                first = b * BLOCK + 8 * g
                held[g] = jnp.where(hit, picked[first : first + 8], held[g])
        for g in range(groups + 1):
            weight = jnp.maximum(1.0 - jnp.abs(within - (eight + 8.0 * g)), 0.0)
            total = total + held[g] * weight
    mean = middle + jnp.sum(total, axis=0, keepdims=True) * (1.0 / SITES)
    return jnp.broadcast_to(mean, (8, slots))


def resist_kernel(
    intensity_ref, core_ref, chip_ref, inner_ref, outer_ref, operator_ref,
    coords_ref,
    resist_hbm, table_ref, middle_ref, mean_chip_ref,
    resist_ref, sem,
):
    odd = parity()
    chip_edge = jnp.where(has_chip_side(), chip_ref[...], 0.0)
    core_edge = core_ref[...]
    above = jnp.where(odd == 1, core_edge, chip_edge)
    below = jnp.where(odd == 1, chip_edge, core_edge)
    edges = jnp.concatenate([above, below], axis=0).astype(BF16)
    blurred = jnp.dot(inner_ref[...], intensity_ref[...], preferred_element_type=F32)
    blurred += jnp.dot(outer_ref[...], edges, preferred_element_type=F32)
    middle = jnp.sum(jnp.sum(blurred, axis=0, keepdims=True), axis=1, keepdims=True)
    middle = middle * (1.0 / (blurred.shape[0] * blurred.shape[1]))
    high = blurred.astype(BF16)
    low = (blurred - high.astype(F32)).astype(BF16)
    resist = jnp.dot(
        jnp.concatenate([high, low, high], axis=1), operator_ref[...], preferred_element_type=F32
    )
    resist_ref[...] = resist
    copy = pltpu.make_async_copy(resist_ref, resist_hbm, sem)
    copy.start()
    table_ref[...] = (resist - middle).astype(BF16)
    middle_ref[...] = jnp.broadcast_to(middle, middle_ref.shape)
    mean_chip_ref[...] = site_means(table_ref[...], coords_ref[...], middle_ref[:1, :1])
    copy.wait()


def mean_kernel(table_ref, middle_ref, coords_ref, mean_ref):
    mean_ref[...] = site_means(table_ref[...], coords_ref[...], middle_ref[:1, :1])


def bias_kernel(level_ref, chosen_ref, own_ref, core_ref, chip_ref, steps_ref, out_ref):
    odd = parity() == 1
    core, chip = core_ref[...], chip_ref[...]
    means = jnp.concatenate(
        [jnp.where(odd, core, chip), own_ref[...], jnp.where(odd, chip, core)], axis=1
    )
    lines = lax.broadcasted_iota(jnp.int32, means.shape, 0)
    first, second, third = (part.astype(F32) for part in three_parts(means))
    parts = jnp.where(lines == 0, first, jnp.where(lines == 1, second, third))
    parts = jnp.where(lines < 3, parts, 0.0).astype(BF16)
    found = jnp.dot(parts, chosen_ref[...], preferred_element_type=F32)
    site_mean = jnp.sum(found, axis=0, keepdims=True)
    out_ref[...] = bias_step * steps_ref[...].astype(F32) - bias_gain * (
        site_mean - level_ref[:1, :1]
    )


def chip_pairs(groups, count):
    pairs = []
    for group in range(groups):
        first = group * count
        for i in range(1, count - 1, 2):
            pairs += [(first + i, first + i + 1), (first + i + 1, first + i)]
    if groups % 2:
        for group in range(groups):
            pairs += [(group * count, (group + 1) * count - 1), ((group + 1) * count - 1, group * count)]
    else:
        for group in range(groups):
            for end in (0, count - 1):
                pairs.append((group * count + end, (group ^ 1) * count + end))
    return pairs


def swap_chips(to_chip):
    pairs = chip_pairs(lax.axis_size("groups"), lax.axis_size("tx"))
    return lax.ppermute(to_chip, ("groups", "tx"), pairs)


def swap_cores(to_core):
    return lax.ppermute(to_core, "tx", [(i, i ^ 1) for i in range(lax.axis_size("tx"))])


def call(kernel, outs, args, smem=(), hbm=(), hbm_outs=(), scratch=(), name=None):
    specs = [
        pl.BlockSpec(
            memory_space=pltpu.SMEM if i in smem else pltpu.HBM if i in hbm else pltpu.VMEM
        )
        for i in range(len(args))
    ]
    args = [
        pltpu.with_memory_space_constraint(arg, pltpu.HBM) if i in hbm else arg
        for i, arg in enumerate(args)
    ]
    return pl.pallas_call(
        kernel,
        out_shape=[jax.ShapeDtypeStruct(s, d) for s, d in outs],
        in_specs=specs,
        out_specs=[
            pl.BlockSpec(memory_space=pltpu.HBM if i in hbm_outs else pltpu.VMEM)
            for i in range(len(outs))
        ],
        scratch_shapes=list(scratch),
        compiler_params=pltpu.CompilerParams(vmem_limit_bytes=VMEM_BYTES),
        name=name,
    )(*args)


def shards(mask, kernel_spectra, kernel_weights, threshold, eval_tile, site_coords, bias_steps):
    tile_rows, tile_cols = mask.shape
    _, row_freqs, kernels, col_freqs = kernel_spectra.shape
    frags = eval_tile.shape[0]
    capacity = frags // 2
    samples = 2 * col_freqs
    flat = kernels * col_freqs
    records = 2 * SITES
    col_forward, row_blocks, row_inverse, col_inverse = imaging_tables(
        tile_rows, tile_cols, row_freqs, col_freqs
    )
    operator, inner, outer = blur_tables(tile_rows, tile_cols, col_freqs, BLUR_REACH)
    spectrum = ((2 * row_freqs, col_freqs), F32)
    packed = ((records, capacity), F32)
    edge = ((BLUR_REACH, samples), F32)
    means = ((8, capacity), F32)
    weights = kernel_weights.reshape(1, kernels)

    own, to_core, to_chip, packed_core, packed_chip, packed_own, chosen = call(
        front_kernel,
        [spectrum] * 3
        + [packed] * 3
        + [((3 * capacity, frags), BF16)],
        (
            eval_tile.reshape(1, frags), site_coords.reshape(records, frags),
            mask, col_forward, row_blocks,
        ),
        hbm=range(5),
        scratch=[
            pltpu.VMEM((1, frags), jnp.int32),
            pltpu.VMEM((records, frags), F32),
            pltpu.VMEM(mask.shape, BF16),
            pltpu.VMEM(col_forward.shape, BF16),
            pltpu.VMEM(row_blocks.shape, BF16),
            pltpu.SemaphoreType.DMA((7,)),
        ],
        name="front",
    )
    got_chip = swap_chips(to_chip)
    got_core = swap_cores(to_core)
    coords_chip = swap_chips(packed_chip)
    coords_core = swap_cores(packed_core)
    kern = jnp.transpose(kernel_spectra, (0, 2, 1, 3))
    level, kern, inverse, spread = call(
        load_kernel,
        [((8, 128), F32), (kern.shape, F32), (row_inverse.shape, BF16), (col_inverse.shape, BF16)],
        (own, threshold, kern, row_inverse, col_inverse),
        smem=(1,),
        hbm=(2, 3, 4),
        scratch=[pltpu.SemaphoreType.DMA((4,))],
        name="load",
    )
    product, edge_core, edge_chip = call(
        edge_kernel,
        [((2 * row_freqs, flat), BF16), edge, edge],
        (
            weights, own, got_core, got_chip, kern, inverse, spread,
        ),
        name="edges",
    )
    edge_chip = swap_chips(edge_chip)
    edge_core = swap_cores(edge_core)
    (intensity,) = call(
        imaging_kernel,
        [((tile_rows, samples), BF16)],
        (weights, product, inverse, spread),
        name="imaging",
    )
    resist, table, middle, mean_chip = call(
        resist_kernel,
        [((tile_rows, tile_cols), F32), ((tile_rows, tile_cols), BF16), ((8, 128), F32), means],
        (intensity, edge_core, edge_chip, inner, outer, operator, coords_chip),
        hbm_outs=(0,),
        scratch=[pltpu.VMEM((tile_rows, tile_cols), F32), pltpu.SemaphoreType.DMA],
        name="resist",
    )
    back_chip = swap_chips(mean_chip)
    (mean_core,) = call(mean_kernel, [means], (table, middle, coords_core), name="mean_core")
    back_core = swap_cores(mean_core)
    (mean_own,) = call(mean_kernel, [means], (table, middle, packed_own), name="mean_own")
    (new_bias,) = call(
        bias_kernel,
        [((1, frags), F32)],
        (level, chosen, mean_own, back_core, back_chip, bias_steps.reshape(1, frags)),
        name="bias",
    )
    return resist, new_bias.reshape(frags)


def solution(mesh):
    placed = (
        P(("groups", "tx"), None),
        P(),
        P(),
        P(),
        P(("groups", "tx")),
        P(None, None, ("groups", "tx")),
        P(("groups", "tx")),
    )
    return jax.shard_map(
        shards,
        mesh=mesh,
        in_specs=placed,
        out_specs=(P(("groups", "tx"), None), P(("groups", "tx"))),
        check_vma=False,
    )
```

```python
import functools
import math

import jax
import jax.numpy as jnp
import ml_dtypes
import numpy as np
from jax import lax
from jax.experimental import pallas as pl
from jax.experimental.pallas import tpu as pltpu
from jax.sharding import PartitionSpec as P

HALO = 256
BLUR_REACH = 8
SITES = 16

blur_sigma = 3.0
bias_step = 0.5
bias_gain = 2.0

F32 = jnp.float32
BF16 = jnp.bfloat16
SINE = (1.57079628989, -0.645963358138, 0.0796884742403, -0.0046722194159, 0.000150816735945)
COSINE = (0.99999999978, -1.23370053428, 0.253669322509, -0.0208626876045, 0.000917723911039, -2.38245358719e-05)
VMEM_BYTES = 32 * 1024 * 1024


def rounded(table):
    return np.asarray(table, np.float32).astype(ml_dtypes.bfloat16)


def halves(table):
    high = rounded(table)
    low = rounded(np.asarray(table, np.float64) - high.astype(np.float64))
    return high, low


def twiddle(position, frequency, period, amplitude):
    phase_index = (position[:, None] * frequency[None, :]) % period
    phase_angle = phase_index * (2.0 * math.pi / period)
    return np.cos(phase_angle) * amplitude, np.sin(phase_angle) * amplitude


def centered(count):
    return np.arange(count) - count // 2


def imaging_tables(tile_rows, tile_cols, row_freqs, col_freqs):
    window_rows = tile_rows + 2 * HALO
    col_cos, col_sin = twiddle(
        np.arange(tile_cols), centered(col_freqs), tile_cols, 1.0 / math.sqrt(tile_cols)
    )
    col_forward = rounded(np.concatenate([col_cos, -col_sin], axis=1))
    row_cos, row_sin = twiddle(
        centered(row_freqs), np.arange(window_rows), window_rows, 1.0 / math.sqrt(window_rows)
    )
    row_forward = rounded(np.concatenate([row_cos, -row_sin], axis=0))
    row_blocks = np.concatenate(
        [row_forward[:, i * tile_rows : (i + 1) * tile_rows] for i in range(3)], axis=0
    )
    back_cos, back_sin = twiddle(
        np.arange(tile_rows) + HALO, centered(row_freqs), window_rows, 1.0 / math.sqrt(row_freqs)
    )
    row_inverse = rounded(
        np.block([[back_cos, -back_sin], [back_sin, back_cos]])
    )
    samples = 2 * col_freqs
    step = tile_cols // samples
    out_cos, out_sin = twiddle(
        centered(col_freqs), np.arange(samples) * step, tile_cols, 1.0 / math.sqrt(col_freqs)
    )
    col_inverse = rounded(np.block([[out_cos, out_sin], [-out_sin, out_cos]]))
    return col_forward, row_blocks, row_inverse, col_inverse


def blur_weight(offset, reach):
    every = np.arange(-reach, reach + 1).astype(np.float64)
    norm = np.sum(np.exp(-every * every / (2.0 * blur_sigma * blur_sigma)))
    weight = np.exp(-offset.astype(np.float64) ** 2 / (2.0 * blur_sigma * blur_sigma)) / norm
    return np.where(np.abs(offset) <= reach, weight, 0.0)


def blur_tables(tile_rows, tile_cols, col_freqs, reach):
    line = np.arange(tile_cols)
    col_blur = rounded(blur_weight(line[None, :] - line[:, None], reach))
    samples = 2 * col_freqs
    step = tile_cols // samples
    offset = (line[None, :] - step * np.arange(samples)[:, None]).astype(np.float64)
    half = np.where(offset == 0, 1.0, np.sin(math.pi * offset / tile_cols))
    spread = np.where(
        offset == 0,
        (samples - 1) / samples,
        np.sin((samples - 1) * math.pi * offset / tile_cols) / (samples * half),
    )
    spread_blur = spread @ col_blur.astype(np.float64)
    row_diff = (
        np.arange(tile_rows + 2 * reach)[None, :] - reach - np.arange(tile_rows)[:, None]
    )
    row_blur = rounded(blur_weight(row_diff, reach))
    inner = row_blur[:, reach : reach + tile_rows]
    outer = np.concatenate([row_blur[:, :reach], row_blur[:, reach + tile_rows :]], axis=1)
    high, low = halves(spread_blur)
    operator = np.concatenate([high, high, low], axis=0)

    freqs = np.arange(col_freqs)
    gauss = blur_weight(np.arange(-reach, reach + 1), reach)
    gauss = rounded(gauss).astype(np.float64)
    theta = 2.0 * math.pi * freqs / tile_cols
    gain = np.cos(theta[:, None] * np.arange(-reach, reach + 1)[None, :]) @ gauss
    gain = gain * np.where(freqs == 0, 1.0, 2.0) / samples * np.cos(theta / 2.0)
    cosines, sines = twiddle(freqs, np.arange(samples), samples, 1.0)
    ring = np.zeros((tile_cols, tile_cols))
    for shift in range(-reach, reach + 1):
        ring[line, (line + shift) % tile_cols] = gauss[shift + reach]
    edge = np.concatenate([line[:reach], line[tile_cols - reach :]])
    cut = (spread @ (col_blur.astype(np.float64) - ring)[:, edge]).T
    waves = np.concatenate([gain[:, None] * cosines, -gain[:, None] * sines, cut], axis=0)
    high, low = halves(waves)
    waves = np.concatenate([high, high, low], axis=1)
    slope = np.broadcast_to(np.tan(theta / 2.0)[:, None], (col_freqs, 128)).astype(np.float32)
    return operator, waves, np.ascontiguousarray(slope), np.ascontiguousarray(inner), np.ascontiguousarray(outer)


def parity():
    return lax.rem(lax.axis_index("tx"), 2)


def has_chip_side():
    me = lax.axis_index("tx")
    return jnp.logical_and(me != 0, me != lax.axis_size("tx") - 1)


def three_parts(values):
    first = values.astype(BF16)
    rest = values - first.astype(F32)
    second = rest.astype(BF16)
    third = (rest - second.astype(F32)).astype(BF16)
    return first, second, third


def transposed_dot(left, right):
    return lax.dot_general(left, right, (((1,), (1,)), ((), ())), preferred_element_type=F32)


def started(sems, first, *moves):
    copies = []
    for source, target, pieces in moves:
        rows = source.shape[0] // pieces
        for i in range(pieces):
            part = pl.ds(i * rows, rows)
            copies.append(
                pltpu.make_async_copy(
                    source.at[part], target.at[part], sems.at[first + len(copies)]
                )
            )
            copies[-1].start()
    return copies


def load_kernel(
    cols, coords_ref, threshold_ref, kern_hbm, inverse_hbm, spread_hbm,
    level_ref, kern_ref, inverse_ref, spread_ref, tents_ref, spin_ref, ends_ref, sems,
):
    copies = started(
        sems, 0, (kern_hbm, kern_ref, 2), (inverse_hbm, inverse_ref, 1), (spread_hbm, spread_ref, 1)
    )
    level_ref[...] = jnp.full(level_ref.shape, threshold_ref[0], F32)
    site_tables(coords_ref[...], tents_ref, spin_ref, ends_ref, cols)
    for copy in copies:
        copy.wait()


def front_kernel(
    eval_hbm, records_hbm, mask_hbm, forward_hbm, rows_hbm,
    own_ref, core_ref, chip_ref, packed_core_ref, packed_chip_ref, packed_own_ref, chosen_ref,
    eval_ref, records_ref, mask_ref, forward_ref, rows_ref, sems,
):
    small = started(sems, 0, (eval_hbm, eval_ref, 1), (records_hbm, records_ref, 1))
    large = started(
        sems, 2, (mask_hbm, mask_ref, 2), (forward_hbm, forward_ref, 2), (rows_hbm, rows_ref, 1)
    )
    me = lax.axis_index("tx")
    odd = parity()
    frags = eval_ref.shape[1]
    capacity = frags // 2
    count = records_ref.shape[0]
    before = lax.broadcasted_iota(jnp.int32, (frags, frags), 0)
    after = lax.broadcasted_iota(jnp.int32, (frags, frags), 1)
    upper = (before <= after).astype(F32).astype(BF16)
    slots = lax.broadcasted_iota(jnp.int32, (capacity, frags), 0).astype(F32).astype(BF16)
    for copy in small:
        copy.wait()
    member = lax.broadcasted_iota(jnp.int32, (8, frags), 0) == eval_ref[...] - me + 1
    counts = jnp.dot(member.astype(F32).astype(BF16), upper, preferred_element_type=F32)
    code = jnp.where(member, counts - 1.0, -1.0)
    for side in range(3):
        row = jnp.broadcast_to(code[side : side + 1].astype(BF16), (capacity, frags))
        chosen_ref[pl.ds(side * capacity, capacity)] = jnp.where(slots == row, jnp.ones_like(slots), jnp.zeros_like(slots))
    pieces = jnp.concatenate(three_parts(records_ref[...]), axis=0)

    def packed(side, out_ref):
        chosen = chosen_ref[pl.ds(pl.multiple_of(side * capacity, capacity), capacity)]
        got = transposed_dot(pieces, chosen)
        out_ref[...] = got[:count] + got[count : 2 * count] + got[2 * count :]

    packed(2 - 2 * odd, packed_core_ref)
    packed(2 * odd, packed_chip_ref)
    packed(1, packed_own_ref)

    for copy in large:
        copy.wait()
    col_spectra = jnp.dot(mask_ref[...], forward_ref[...], preferred_element_type=F32).astype(BF16)
    product = jnp.dot(rows_ref[...], col_spectra, preferred_element_type=F32)
    freqs, cols = own_ref.shape[0] // 2, own_ref.shape[1]

    def partial(block):
        part = product[2 * freqs * block : 2 * freqs * (block + 1)]
        real = part[:freqs, :cols] - part[freqs:, cols:]
        imag = part[:freqs, cols:] + part[freqs:, :cols]
        return jnp.concatenate([real, imag], axis=0)

    upper_side, own, lower_side = partial(0), partial(1), partial(2)
    chip_ref[...] = jnp.where(odd == 1, upper_side, lower_side)
    core_ref[...] = jnp.where(odd == 1, lower_side, upper_side)
    own_ref[...] = own


def stacked_pairs(half, rows, kernels, cols):
    pairs = []
    for k in range(kernels):
        lanes = slice(k * cols, (k + 1) * cols)
        pairs.append(jnp.concatenate([half[:rows, lanes], half[rows:, lanes]], axis=1))
    return jnp.concatenate(pairs, axis=0)


def edge_kernel(
    weights_ref, own_ref, core_ref, chip_ref, kern_ref, inverse_ref, spread_ref,
    product_ref, edge_core_ref, edge_chip_ref,
):
    freqs, cols = own_ref.shape[0] // 2, own_ref.shape[1]
    rows = inverse_ref.shape[0] // 2
    kernels = kern_ref.shape[1]
    odd = parity()
    chip = jnp.where(has_chip_side(), chip_ref[...], 0.0)
    spectrum = own_ref[...] + core_ref[...] + chip
    spec_real, spec_imag = spectrum[:freqs], spectrum[freqs:]
    for k in range(kernels):
        kern_real, kern_imag = kern_ref[0, k], kern_ref[1, k]
        lanes = slice(k * cols, (k + 1) * cols)
        product_ref[:freqs, lanes] = (kern_real * spec_real - kern_imag * spec_imag).astype(BF16)
        product_ref[freqs:, lanes] = (kern_real * spec_imag + kern_imag * spec_real).astype(BF16)
    reach = BLUR_REACH
    lines = jnp.concatenate(
        [
            inverse_ref[:reach], inverse_ref[rows - reach : rows],
            inverse_ref[rows : rows + reach], inverse_ref[2 * rows - reach :],
        ],
        axis=0,
    )
    half = jnp.dot(lines, product_ref[...], preferred_element_type=F32).astype(BF16)
    pairs = stacked_pairs(half, 2 * reach, kernels, cols)
    field = jnp.dot(pairs, spread_ref[...], preferred_element_type=F32)
    total = jnp.zeros((2 * reach, 2 * cols), F32)
    for k in range(kernels):
        part = field[2 * reach * k : 2 * reach * (k + 1)]
        real, imag = part[:, : 2 * cols], part[:, 2 * cols :]
        total = total + weights_ref[:, k : k + 1] * (real * real + imag * imag)
    values = total.astype(BF16).astype(F32)
    top, bottom = values[:reach], values[reach:]
    edge_core_ref[...] = jnp.where(odd == 1, top, bottom)
    edge_chip_ref[...] = jnp.where(odd == 1, bottom, top)


def imaging_kernel(
    tile_cols, weights_ref, product_ref, inverse_ref, spread_ref, chip_coords_ref, core_coords_ref,
    intensity_ref, chip_tents_ref, chip_spin_ref, chip_ends_ref,
    core_tents_ref, core_spin_ref, core_ends_ref,
):
    rows, samples = intensity_ref.shape
    cols = samples // 2
    kernels = product_ref.shape[1] // cols
    half = jnp.dot(inverse_ref[...], product_ref[...], preferred_element_type=F32).astype(BF16)
    fields = jnp.dot(
        stacked_pairs(half, rows, kernels, cols), spread_ref[...], preferred_element_type=F32
    )
    total = jnp.zeros((rows, samples), F32)
    for k in range(kernels):
        field = fields[k * rows : (k + 1) * rows]
        real, imag = field[:, :samples], field[:, samples:]
        total = total + weights_ref[:, k : k + 1] * (real * real + imag * imag)
    intensity_ref[...] = total.astype(BF16)
    site_tables(chip_coords_ref[...], chip_tents_ref, chip_spin_ref, chip_ends_ref, tile_cols)
    site_tables(core_coords_ref[...], core_tents_ref, core_spin_ref, core_ends_ref, tile_cols)


def turned(index, period):
    turns = index * (1.0 / period)
    part = 2.0 * (turns - jnp.round(turns))
    square = part * part
    sine = SINE[-1]
    for term in SINE[-2::-1]:
        sine = sine * square + term
    sine = sine * part
    cosine = COSINE[-1]
    for term in COSINE[-2::-1]:
        cosine = cosine * square + term
    return 1.0 - 2.0 * sine * sine, 2.0 * sine * cosine


def site_tables(coords, tents_ref, spin_ref, ends_ref, tile_cols):
    tile_rows, slots = tents_ref.shape[1:]
    groups = spin_ref.shape[1] // 2
    eight = lax.broadcasted_iota(jnp.int32, (8, slots), 0).astype(F32)
    group = lax.broadcasted_iota(jnp.int32, (groups, slots), 0).astype(F32)
    line = lax.broadcasted_iota(jnp.int32, (tile_rows, slots), 0).astype(F32).astype(BF16)
    none = jnp.zeros((tile_rows, slots), BF16)
    edge = lax.broadcasted_iota(jnp.int32, (2 * BLUR_REACH, slots), 0).astype(F32)
    edge = jnp.where(edge < BLUR_REACH, edge, edge + (tile_cols - 2.0 * BLUR_REACH))

    def wide(row, dtype=F32):
        return jnp.broadcast_to(row.astype(dtype), (tile_rows, slots))

    for site in range(SITES):
        position = coords[site : site + 1] * (tile_rows - 1)
        low = jnp.minimum(jnp.floor(position), tile_rows - 2.0)
        part = position - low
        high_tent = jnp.where(line == wide(low + 1.0, BF16), wide(part, BF16), none)
        tents_ref[site] = jnp.where(line == wide(low, BF16), wide(1.0 - part, BF16), high_tent)
        position = coords[SITES + site : SITES + site + 1] * (tile_cols - 1)
        low = jnp.minimum(jnp.floor(position), tile_cols - 2.0)
        tilt = 2.0 * (position - low) - 1.0
        center = 2.0 * low + 1.0
        spin_ref[site, :groups], spin_ref[site, groups:] = turned(center * (8.0 * group), 2 * tile_cols)
        cosine, sine = turned(center * eight, 2 * tile_cols)
        ends_ref[site, :8] = cosine
        ends_ref[site, 8:16] = sine
        ends_ref[site, 16:24] = tilt * sine
        ends_ref[site, 24:32] = tilt * cosine
        ends_ref[site, 32:] = jnp.maximum(1.0 - jnp.abs(position - edge), 0.0)


def site_means(table_ref, slope_ref, tents_ref, spin_ref, ends_ref, middle):
    slots = tents_ref.shape[2]
    groups = spin_ref.shape[1] // 2
    freqs = 8 * groups
    none = jnp.zeros((8, slots), F32)
    slopes = [
        jnp.concatenate([slope_ref[8 * g : 8 * g + 8]] * (slots // slope_ref.shape[1]), axis=1)
        for g in range(groups)
    ]
    total = none
    for site in range(SITES):
        picked = jnp.dot(table_ref[...], tents_ref[site], preferred_element_type=F32)
        real = imag = tilted_real = tilted_imag = none
        for g in range(groups):
            part_real = picked[8 * g : 8 * g + 8]
            part_imag = picked[freqs + 8 * g : freqs + 8 * g + 8]
            cosine = jnp.broadcast_to(spin_ref[site, g : g + 1], (8, slots))
            sine = jnp.broadcast_to(spin_ref[site, groups + g : groups + g + 1], (8, slots))
            turn_real = part_real * cosine - part_imag * sine
            turn_imag = part_real * sine + part_imag * cosine
            real += turn_real
            imag += turn_imag
            tilted_real += slopes[g] * turn_real
            tilted_imag += slopes[g] * turn_imag
        total += real * ends_ref[site, :8] - imag * ends_ref[site, 8:16]
        total -= tilted_real * ends_ref[site, 16:24] + tilted_imag * ends_ref[site, 24:32]
        edge = picked[2 * freqs :] * ends_ref[site, 32:]
        total += edge[:8] + edge[8:]
    mean = middle + jnp.sum(total, axis=0, keepdims=True) * (1.0 / SITES)
    return jnp.broadcast_to(mean, (8, slots))


def resist_kernel(
    intensity_ref, core_ref, chip_ref, inner_ref, outer_ref, waves_ref, slope_ref,
    tents_ref, spin_ref, ends_ref,
    parts_ref, table_ref, middle_ref, mean_ref,
):
    odd = parity()
    chip_edge = jnp.where(has_chip_side(), chip_ref[...], 0.0)
    core_edge = core_ref[...]
    above = jnp.where(odd == 1, core_edge, chip_edge)
    below = jnp.where(odd == 1, chip_edge, core_edge)
    edges = jnp.concatenate([above, below], axis=0).astype(BF16)
    blurred = jnp.dot(inner_ref[...], intensity_ref[...], preferred_element_type=F32)
    blurred += jnp.dot(outer_ref[...], edges, preferred_element_type=F32)
    middle = jnp.sum(jnp.sum(blurred, axis=0, keepdims=True), axis=1, keepdims=True)
    middle = middle * (1.0 / (blurred.shape[0] * blurred.shape[1]))
    high = blurred.astype(BF16)
    low = (blurred - high.astype(F32)).astype(BF16)
    parts = jnp.concatenate([high, low, high], axis=1)
    parts_ref[...] = parts
    table = transposed_dot(waves_ref[...], parts)
    first = lax.broadcasted_iota(jnp.int32, table.shape, 0) == 0
    table_ref[...] = jnp.where(first, table - middle, table).astype(BF16)
    middle_ref[...] = jnp.broadcast_to(middle, middle_ref.shape)
    mean_ref[...] = site_means(
        table_ref, slope_ref, tents_ref, spin_ref, ends_ref, middle_ref[:1, :1]
    )


def core_kernel(table_ref, slope_ref, tents_ref, spin_ref, ends_ref, middle_ref, mean_ref):
    mean_ref[...] = site_means(
        table_ref, slope_ref, tents_ref, spin_ref, ends_ref, middle_ref[:1, :1]
    )


def own_kernel(
    parts_ref, operator_ref, table_ref, slope_ref, tents_ref, spin_ref, ends_ref, middle_ref,
    resist_hbm, mean_ref, resist_ref, sem,
):
    resist_ref[...] = jnp.dot(parts_ref[...], operator_ref[...], preferred_element_type=F32)
    copy = pltpu.make_async_copy(resist_ref, resist_hbm, sem)
    copy.start()
    mean_ref[...] = site_means(
        table_ref, slope_ref, tents_ref, spin_ref, ends_ref, middle_ref[:1, :1]
    )
    copy.wait()


def bias_kernel(level_ref, chosen_ref, own_ref, core_ref, chip_ref, steps_ref, out_ref):
    odd = parity() == 1
    core, chip = core_ref[...], chip_ref[...]
    means = jnp.concatenate(
        [jnp.where(odd, core, chip), own_ref[...], jnp.where(odd, chip, core)], axis=1
    )
    lines = lax.broadcasted_iota(jnp.int32, means.shape, 0)
    first, second, third = (part.astype(F32) for part in three_parts(means))
    parts = jnp.where(lines == 0, first, jnp.where(lines == 1, second, third))
    parts = jnp.where(lines < 3, parts, 0.0).astype(BF16)
    found = jnp.dot(parts, chosen_ref[...], preferred_element_type=F32)
    site_mean = jnp.sum(found, axis=0, keepdims=True)
    out_ref[...] = bias_step * steps_ref[...].astype(F32) - bias_gain * (
        site_mean - level_ref[:1, :1]
    )


def chip_pairs(groups, count):
    pairs = []
    for group in range(groups):
        first = group * count
        for i in range(1, count - 1, 2):
            pairs += [(first + i, first + i + 1), (first + i + 1, first + i)]
    if groups % 2:
        for group in range(groups):
            pairs += [(group * count, (group + 1) * count - 1), ((group + 1) * count - 1, group * count)]
    else:
        for group in range(groups):
            for end in (0, count - 1):
                pairs.append((group * count + end, (group ^ 1) * count + end))
    return pairs


def swap_chips(to_chip):
    pairs = chip_pairs(lax.axis_size("groups"), lax.axis_size("tx"))
    return lax.ppermute(to_chip, ("groups", "tx"), pairs)


def swap_cores(to_core):
    return lax.ppermute(to_core, "tx", [(i, i ^ 1) for i in range(lax.axis_size("tx"))])


def call(kernel, outs, args, smem=(), hbm=(), hbm_outs=(), scratch=(), name=None):
    specs = [
        pl.BlockSpec(
            memory_space=pltpu.SMEM if i in smem else pltpu.HBM if i in hbm else pltpu.VMEM
        )
        for i in range(len(args))
    ]
    args = [
        pltpu.with_memory_space_constraint(arg, pltpu.HBM) if i in hbm else arg
        for i, arg in enumerate(args)
    ]
    return pl.pallas_call(
        kernel,
        out_shape=[jax.ShapeDtypeStruct(s, d) for s, d in outs],
        in_specs=specs,
        out_specs=[
            pl.BlockSpec(memory_space=pltpu.HBM if i in hbm_outs else pltpu.VMEM)
            for i in range(len(outs))
        ],
        scratch_shapes=list(scratch),
        compiler_params=pltpu.CompilerParams(vmem_limit_bytes=VMEM_BYTES),
        name=name,
    )(*args)


def shards(mask, kernel_spectra, kernel_weights, threshold, eval_tile, site_coords, bias_steps):
    tile_rows, tile_cols = mask.shape
    _, row_freqs, kernels, col_freqs = kernel_spectra.shape
    frags = eval_tile.shape[0]
    capacity = frags // 2
    samples = 2 * col_freqs
    flat = kernels * col_freqs
    records = 2 * SITES
    col_forward, row_blocks, row_inverse, col_inverse = imaging_tables(
        tile_rows, tile_cols, row_freqs, col_freqs
    )
    operator, waves, slope, inner, outer = blur_tables(tile_rows, tile_cols, col_freqs, BLUR_REACH)
    spectrum = ((2 * row_freqs, col_freqs), F32)
    packed = ((records, capacity), F32)
    edge = ((BLUR_REACH, samples), F32)
    means = ((8, capacity), F32)
    site_shapes = [
        ((SITES, tile_rows, capacity), BF16),
        ((SITES, col_freqs // 4, capacity), F32),
        ((SITES, 32 + 2 * BLUR_REACH, capacity), F32),
    ]
    weights = kernel_weights.reshape(1, kernels)

    own, to_core, to_chip, packed_core, packed_chip, packed_own, chosen = call(
        front_kernel,
        [spectrum] * 3
        + [packed] * 3
        + [((3 * capacity, frags), BF16)],
        (
            eval_tile.reshape(1, frags), site_coords.reshape(records, frags),
            mask, col_forward, row_blocks,
        ),
        hbm=range(5),
        scratch=[
            pltpu.VMEM((1, frags), jnp.int32),
            pltpu.VMEM((records, frags), F32),
            pltpu.VMEM(mask.shape, BF16),
            pltpu.VMEM(col_forward.shape, BF16),
            pltpu.VMEM(row_blocks.shape, BF16),
            pltpu.SemaphoreType.DMA((7,)),
        ],
        name="front",
    )
    got_chip = swap_chips(to_chip)
    got_core = swap_cores(to_core)
    coords_chip = swap_chips(packed_chip)
    coords_core = swap_cores(packed_core)
    kern = jnp.transpose(kernel_spectra, (0, 2, 1, 3))
    level, kern, inverse, spread, *own_sites = call(
        functools.partial(load_kernel, tile_cols),
        [((8, 128), F32), (kern.shape, F32), (row_inverse.shape, BF16), (col_inverse.shape, BF16)]
        + site_shapes,
        (packed_own, threshold, kern, row_inverse, col_inverse),
        smem=(1,),
        hbm=(2, 3, 4),
        scratch=[pltpu.SemaphoreType.DMA((4,))],
        name="load",
    )
    product, edge_core, edge_chip = call(
        edge_kernel,
        [((2 * row_freqs, flat), BF16), edge, edge],
        (
            weights, own, got_core, got_chip, kern, inverse, spread,
        ),
        name="edges",
    )
    edge_chip = swap_chips(edge_chip)
    edge_core = swap_cores(edge_core)
    intensity, *other_sites = call(
        functools.partial(imaging_kernel, tile_cols),
        [((tile_rows, samples), BF16)] + site_shapes * 2,
        (weights, product, inverse, spread, coords_chip, coords_core),
        name="imaging",
    )
    chip_sites, core_sites = other_sites[:3], other_sites[3:]
    parts, table, middle, mean_chip = call(
        resist_kernel,
        [((tile_rows, 3 * samples), BF16), ((waves.shape[0], tile_rows), BF16), ((8, 128), F32), means],
        (intensity, edge_core, edge_chip, inner, outer, waves, slope, *chip_sites),
        name="resist",
    )
    back_chip = swap_chips(mean_chip)
    (mean_core,) = call(core_kernel, [means], (table, slope, *core_sites, middle), name="mean_core")
    back_core = swap_cores(mean_core)
    resist, mean_own = call(
        own_kernel,
        [((tile_rows, tile_cols), F32), means],
        (parts, operator, table, slope, *own_sites, middle),
        hbm_outs=(0,),
        scratch=[pltpu.VMEM((tile_rows, tile_cols), F32), pltpu.SemaphoreType.DMA],
        name="mean_own",
    )
    (new_bias,) = call(
        bias_kernel,
        [((1, frags), F32)],
        (level, chosen, mean_own, back_core, back_chip, bias_steps.reshape(1, frags)),
        name="bias",
    )
    return resist, new_bias.reshape(frags)


def solution(mesh):
    placed = (
        P(("groups", "tx"), None),
        P(),
        P(),
        P(),
        P(("groups", "tx")),
        P(None, None, ("groups", "tx")),
        P(("groups", "tx")),
    )
    return jax.shard_map(
        shards,
        mesh=mesh,
        in_specs=placed,
        out_specs=(P(("groups", "tx"), None), P(("groups", "tx"))),
        check_vma=False,
    )
```

```python
import functools
import math

import jax
import jax.numpy as jnp
import ml_dtypes
import numpy as np
from jax import lax
from jax.experimental import pallas as pl
from jax.experimental.pallas import tpu as pltpu
from jax.sharding import PartitionSpec as P

HALO = 256
BLUR_REACH = 8
SITES = 16

blur_sigma = 3.0
bias_step = 0.5
bias_gain = 2.0

F32 = jnp.float32
BF16 = jnp.bfloat16
SINE = (1.57079628989, -0.645963358138, 0.0796884742403, -0.0046722194159, 0.000150816735945)
COSINE = (0.99999999978, -1.23370053428, 0.253669322509, -0.0208626876045, 0.000917723911039, -2.38245358719e-05)
VMEM_BYTES = 32 * 1024 * 1024


def rounded(table):
    return np.asarray(table, np.float32).astype(ml_dtypes.bfloat16)


def halves(table):
    high = rounded(table)
    low = rounded(np.asarray(table, np.float64) - high.astype(np.float64))
    return high, low


def twiddle(position, frequency, period, amplitude):
    phase_index = (position[:, None] * frequency[None, :]) % period
    phase_angle = phase_index * (2.0 * math.pi / period)
    return np.cos(phase_angle) * amplitude, np.sin(phase_angle) * amplitude


def centered(count):
    return np.arange(count) - count // 2


def imaging_tables(tile_rows, tile_cols, row_freqs, col_freqs):
    window_rows = tile_rows + 2 * HALO
    col_cos, col_sin = twiddle(
        np.arange(tile_cols), centered(col_freqs), tile_cols, 1.0 / math.sqrt(tile_cols)
    )
    col_forward = rounded(np.concatenate([col_cos, -col_sin], axis=1))
    row_cos, row_sin = twiddle(
        centered(row_freqs), np.arange(window_rows), window_rows, 1.0 / math.sqrt(window_rows)
    )
    row_forward = rounded(np.concatenate([row_cos, -row_sin], axis=0))
    row_blocks = [row_forward[:, i * tile_rows : (i + 1) * tile_rows] for i in range(3)]
    side_rows = np.concatenate([row_blocks[0], row_blocks[2]], axis=0)
    own_rows = np.ascontiguousarray(row_blocks[1])
    back_cos, back_sin = twiddle(
        np.arange(tile_rows) + HALO, centered(row_freqs), window_rows, 1.0 / math.sqrt(row_freqs)
    )
    row_inverse = rounded(
        np.block([[back_cos, -back_sin], [back_sin, back_cos]])
    )
    samples = 2 * col_freqs
    step = tile_cols // samples
    out_cos, out_sin = twiddle(
        centered(col_freqs), np.arange(samples) * step, tile_cols, 1.0 / math.sqrt(col_freqs)
    )
    col_inverse = rounded(np.block([[out_cos, out_sin], [-out_sin, out_cos]]))
    return col_forward, side_rows, own_rows, row_inverse, col_inverse


def blur_weight(offset, reach):
    every = np.arange(-reach, reach + 1).astype(np.float64)
    norm = np.sum(np.exp(-every * every / (2.0 * blur_sigma * blur_sigma)))
    weight = np.exp(-offset.astype(np.float64) ** 2 / (2.0 * blur_sigma * blur_sigma)) / norm
    return np.where(np.abs(offset) <= reach, weight, 0.0)


def blur_tables(tile_rows, tile_cols, col_freqs, reach):
    line = np.arange(tile_cols)
    col_blur = rounded(blur_weight(line[None, :] - line[:, None], reach))
    samples = 2 * col_freqs
    step = tile_cols // samples
    offset = (line[None, :] - step * np.arange(samples)[:, None]).astype(np.float64)
    half = np.where(offset == 0, 1.0, np.sin(math.pi * offset / tile_cols))
    spread = np.where(
        offset == 0,
        (samples - 1) / samples,
        np.sin((samples - 1) * math.pi * offset / tile_cols) / (samples * half),
    )
    spread_blur = spread @ col_blur.astype(np.float64)
    row_diff = (
        np.arange(tile_rows + 2 * reach)[None, :] - reach - np.arange(tile_rows)[:, None]
    )
    row_blur = rounded(blur_weight(row_diff, reach))
    inner = row_blur[:, reach : reach + tile_rows]
    outer = np.concatenate([row_blur[:, :reach], row_blur[:, reach + tile_rows :]], axis=1)
    high, low = halves(spread_blur)
    operator = np.concatenate([high, high, low], axis=0)

    freqs = np.arange(col_freqs)
    gauss = blur_weight(np.arange(-reach, reach + 1), reach)
    gauss = rounded(gauss).astype(np.float64)
    theta = 2.0 * math.pi * freqs / tile_cols
    gain = np.cos(theta[:, None] * np.arange(-reach, reach + 1)[None, :]) @ gauss
    gain = gain * np.where(freqs == 0, 1.0, 2.0) / samples
    cosines, sines = twiddle(freqs, np.arange(samples), samples, 1.0)
    real = (gain[:, None] * cosines).reshape(-1, 8, samples)
    imag = (-gain[:, None] * sines).reshape(-1, 8, samples)
    mid = col_freqs // 16
    above, below = slice(mid + 1, None), slice(mid - 1, 0, -1)
    paired = [
        real[above] + real[below], imag[above] - imag[below],
        imag[above] + imag[below], real[above] - real[below],
        real[mid : mid + 1], imag[mid : mid + 1], real[:1], imag[:1],
    ]
    paired = np.concatenate(paired, axis=0).reshape(-1, samples)
    ring = np.zeros((tile_cols, tile_cols))
    for shift in range(-reach, reach + 1):
        ring[line, (line + shift) % tile_cols] = gauss[shift + reach]
    edge = np.concatenate([line[:reach], line[tile_cols - reach :]])
    cut = (spread @ (col_blur.astype(np.float64) - ring)[:, edge]).T
    waves = np.concatenate([paired, cut], axis=0)
    high, low = halves(waves)
    waves = np.concatenate([high, high, low], axis=1)
    return operator, waves, np.ascontiguousarray(inner), np.ascontiguousarray(outer)


def parity():
    return lax.rem(lax.axis_index("tx"), 2)


def has_chip_side():
    me = lax.axis_index("tx")
    return jnp.logical_and(me != 0, me != lax.axis_size("tx") - 1)


def three_parts(values):
    first = values.astype(BF16)
    rest = values - first.astype(F32)
    second = rest.astype(BF16)
    third = (rest - second.astype(F32)).astype(BF16)
    return first, second, third


def transposed_dot(left, right):
    return lax.dot_general(left, right, (((1,), (1,)), ((), ())), preferred_element_type=F32)


def started(sems, *moves):
    copies = [
        pltpu.make_async_copy(source, target, sems.at[i])
        for i, (source, target) in enumerate(moves)
    ]
    for copy in copies:
        copy.start()
    return copies


def part_spectrum(product, freqs, cols):
    real = product[:freqs, :cols] - product[freqs:, cols:]
    imag = product[:freqs, cols:] + product[freqs:, :cols]
    return jnp.concatenate([real, imag], axis=0)


def front_kernel(
    mask_hbm, forward_hbm, rows_hbm, eval_hbm, records_hbm,
    spectra_ref, core_ref, chip_ref, eval_ref, records_ref,
    mask_ref, forward_ref, rows_ref, sems,
):
    depth = mask_ref.shape[1] // 2
    parts = [pl.ds(i * depth, depth) for i in range(2)]
    copies = started(
        sems,
        (mask_hbm, mask_ref),
        (forward_hbm, forward_ref),
        (rows_hbm, rows_ref),
        (eval_hbm, eval_ref),
        (records_hbm, records_ref),
    )
    copies[0].wait()
    copies[1].wait()
    spectra = jnp.dot(mask_ref[...], forward_ref[...], preferred_element_type=F32).astype(BF16)
    spectra_ref[...] = spectra
    copies[2].wait()
    product = jnp.dot(rows_ref[...], spectra, preferred_element_type=F32)
    freqs, cols = core_ref.shape[0] // 2, core_ref.shape[1]
    upper_side = part_spectrum(product[: 2 * freqs], freqs, cols)
    lower_side = part_spectrum(product[2 * freqs :], freqs, cols)
    odd = parity()
    chip_ref[...] = jnp.where(odd == 1, upper_side, lower_side)
    core_ref[...] = jnp.where(odd == 1, lower_side, upper_side)
    copies[3].wait()
    copies[4].wait()


def pack_kernel(
    after_ref, eval_ref, records_ref, packed_core_ref, packed_chip_ref, packed_own_ref, places_ref,
    chosen_ref,
):
    me = lax.axis_index("tx")
    odd = parity()
    frags = eval_ref.shape[1]
    capacity = frags // 2
    count = records_ref.shape[0]
    before = lax.broadcasted_iota(jnp.int32, (frags, frags), 0)
    after = lax.broadcasted_iota(jnp.int32, (frags, frags), 1)
    upper = (before <= after).astype(F32).astype(BF16)
    slots = lax.broadcasted_iota(jnp.int32, (capacity, frags), 0).astype(F32).astype(BF16)
    member = lax.broadcasted_iota(jnp.int32, (8, frags), 0) == eval_ref[...] - me + 1
    counts = jnp.dot(member.astype(F32).astype(BF16), upper, preferred_element_type=F32)
    code = jnp.where(member, counts - 1.0, -1.0)
    side = lax.broadcasted_iota(jnp.int32, (8, frags), 0) * capacity
    place = jnp.where(member, side + counts.astype(jnp.int32) - 1, 0)
    places_ref[...] = jnp.sum(place, axis=0, keepdims=True)
    for side in range(3):
        row = jnp.broadcast_to(code[side : side + 1].astype(BF16), (capacity, frags))
        chosen_ref[pl.ds(side * capacity, capacity)] = jnp.where(
            slots == row, jnp.ones_like(slots), jnp.zeros_like(slots)
        )
    pieces = jnp.concatenate(three_parts(records_ref[...]), axis=0)

    def packed(side, out_ref):
        chosen = chosen_ref[pl.ds(pl.multiple_of(side * capacity, capacity), capacity)]
        got = transposed_dot(pieces, chosen)
        out_ref[...] = got[:count] + got[count : 2 * count] + got[2 * count :]

    packed(2 - 2 * odd, packed_core_ref)
    packed(2 * odd, packed_chip_ref)
    packed(1, packed_own_ref)


def load_kernel(
    cols, spectra_ref, coords_ref, threshold_ref, rows_hbm, inverse_hbm, spread_hbm,
    level_ref, own_ref, inverse_ref, spread_ref, tents_ref, spin_ref, ends_ref,
    rows_ref, sems,
):
    copies = started(
        sems, (rows_hbm, rows_ref), (inverse_hbm, inverse_ref), (spread_hbm, spread_ref)
    )
    level_ref[...] = jnp.full(level_ref.shape, threshold_ref[0], F32)
    site_tables(coords_ref[...], tents_ref, spin_ref, ends_ref, cols)
    copies[0].wait()
    product = jnp.dot(rows_ref[...], spectra_ref[...], preferred_element_type=F32)
    own_ref[...] = part_spectrum(product, own_ref.shape[0] // 2, own_ref.shape[1])
    copies[1].wait()
    copies[2].wait()


def stacked_pairs(half, rows, kernels, cols):
    pairs = []
    for k in range(kernels):
        lanes = slice(k * cols, (k + 1) * cols)
        pairs.append(jnp.concatenate([half[:rows, lanes], half[rows:, lanes]], axis=1))
    return jnp.concatenate(pairs, axis=0)


def edge_kernel(
    weights_ref, own_ref, core_ref, chip_ref, kern_ref, inverse_ref, spread_ref,
    product_ref, edge_core_ref, edge_chip_ref,
):
    freqs, cols = own_ref.shape[0] // 2, own_ref.shape[1]
    rows = inverse_ref.shape[0] // 2
    kernels = kern_ref.shape[1]
    odd = parity()
    chip = jnp.where(has_chip_side(), chip_ref[...], 0.0)
    spectrum = own_ref[...] + core_ref[...] + chip
    spec_real, spec_imag = spectrum[:freqs], spectrum[freqs:]
    for k in range(kernels):
        kern_real, kern_imag = kern_ref[0, k], kern_ref[1, k]
        lanes = slice(k * cols, (k + 1) * cols)
        product_ref[:freqs, lanes] = (kern_real * spec_real - kern_imag * spec_imag).astype(BF16)
        product_ref[freqs:, lanes] = (kern_real * spec_imag + kern_imag * spec_real).astype(BF16)
    reach = BLUR_REACH
    lines = jnp.concatenate(
        [
            inverse_ref[:reach], inverse_ref[rows - reach : rows],
            inverse_ref[rows : rows + reach], inverse_ref[2 * rows - reach :],
        ],
        axis=0,
    )
    half = jnp.dot(lines, product_ref[...], preferred_element_type=F32).astype(BF16)
    pairs = stacked_pairs(half, 2 * reach, kernels, cols)
    field = jnp.dot(pairs, spread_ref[...], preferred_element_type=F32)
    total = jnp.zeros((2 * reach, 2 * cols), F32)
    for k in range(kernels):
        part = field[2 * reach * k : 2 * reach * (k + 1)]
        real, imag = part[:, : 2 * cols], part[:, 2 * cols :]
        total = total + weights_ref[:, k : k + 1] * (real * real + imag * imag)
    values = total.astype(BF16).astype(F32)
    top, bottom = values[:reach], values[reach:]
    edge_core_ref[...] = jnp.where(odd == 1, top, bottom)
    edge_chip_ref[...] = jnp.where(odd == 1, bottom, top)


def prepare_kernel(
    tile_cols, chip_coords_ref, core_coords_ref,
    chip_tents_ref, chip_spin_ref, chip_ends_ref, core_tents_ref, core_spin_ref, core_ends_ref,
):
    site_tables(chip_coords_ref[...], chip_tents_ref, chip_spin_ref, chip_ends_ref, tile_cols)
    site_tables(core_coords_ref[...], core_tents_ref, core_spin_ref, core_ends_ref, tile_cols)


def imaging_kernel(weights_ref, product_ref, inverse_ref, spread_ref, intensity_ref):
    rows, samples = intensity_ref.shape
    cols = samples // 2
    kernels = product_ref.shape[1] // cols
    half = jnp.dot(inverse_ref[...], product_ref[...], preferred_element_type=F32).astype(BF16)
    fields = jnp.dot(
        stacked_pairs(half, rows, kernels, cols), spread_ref[...], preferred_element_type=F32
    )
    total = jnp.zeros((rows, samples), F32)
    for k in range(kernels):
        field = fields[k * rows : (k + 1) * rows]
        real, imag = field[:, :samples], field[:, samples:]
        total = total + weights_ref[:, k : k + 1] * (real * real + imag * imag)
    intensity_ref[...] = total.astype(BF16)


def turned(index, period):
    turns = index * (1.0 / period)
    part = 2.0 * (turns - jnp.floor(turns + 0.5))
    square = part * part
    sine = SINE[-1]
    for term in SINE[-2::-1]:
        sine = sine * square + term
    sine = sine * part
    cosine = COSINE[-1]
    for term in COSINE[-2::-1]:
        cosine = cosine * square + term
    return 1.0 - 2.0 * sine * sine, 2.0 * sine * cosine


def site_tables(coords, tents_ref, spin_ref, ends_ref, tile_cols):
    tile_rows, slots = tents_ref.shape[1:]
    eight = lax.broadcasted_iota(jnp.int32, (8, slots), 0).astype(F32)
    count = spin_ref.shape[1] // 4
    steps = jnp.concatenate([8.0 * eight + 8.0, eight + 8.0 * count], axis=0)
    one_cosine, one_sine = turned(steps, tile_cols)
    line = lax.broadcasted_iota(jnp.int32, (tile_rows, slots), 0).astype(F32).astype(BF16)
    none = jnp.zeros((tile_rows, slots), BF16)
    edge = lax.broadcasted_iota(jnp.int32, (2 * BLUR_REACH, slots), 0).astype(F32)
    edge = jnp.where(edge < BLUR_REACH, edge, edge + (tile_cols - 2.0 * BLUR_REACH))

    def wide(row, dtype=F32):
        return jnp.broadcast_to(row.astype(dtype), (tile_rows, slots))

    for site in range(SITES):
        position = coords[site : site + 1] * (tile_rows - 1)
        low = jnp.minimum(jnp.floor(position), tile_rows - 2.0)
        part = position - low
        high_tent = jnp.where(line == wide(low + 1.0, BF16), wide(part, BF16), none)
        tents_ref[site] = jnp.where(line == wide(low, BF16), wide(1.0 - part, BF16), high_tent)
        position = coords[SITES + site : SITES + site + 1] * (tile_cols - 1)
        low = jnp.minimum(jnp.floor(position), tile_cols - 2.0)
        part = position - low
        cosine, sine = turned(low * steps, tile_cols)
        next_cosine = cosine * one_cosine - sine * one_sine
        next_sine = sine * one_cosine + cosine * one_sine
        spin_ref[site, :8] = cosine[:8]
        spin_ref[site, 8:16] = sine[:8]
        spin_ref[site, 16:24] = next_cosine[:8]
        spin_ref[site, 24:] = next_sine[:8]
        ends_ref[site, :8] = (1.0 - part) * cosine[8:]
        ends_ref[site, 8:16] = (1.0 - part) * sine[8:]
        ends_ref[site, 16:24] = part * next_cosine[8:]
        ends_ref[site, 24:32] = part * next_sine[8:]
        ends_ref[site, 32:] = jnp.maximum(1.0 - jnp.abs(position - edge), 0.0)


def site_means(table_ref, tents_ref, spin_ref, ends_ref, middle):
    slots = tents_ref.shape[2]
    count = spin_ref.shape[1] // 4
    pairs = count - 1
    none = jnp.zeros((8, slots), F32)
    total = none
    for site in range(SITES):
        picked = jnp.dot(table_ref[...], tents_ref[site], preferred_element_type=F32)
        rows = [picked[8 * i : 8 * i + 8] for i in range(4 * pairs + 6)]

        def spin(i):
            return jnp.broadcast_to(spin_ref[site, i : i + 1], (8, slots))

        for side in range(2):
            first = 2 * count * side
            cosine, sine = spin(first + pairs), spin(first + count + pairs)
            low_real, low_imag = rows[4 * pairs + 2], rows[4 * pairs + 3]
            real = rows[4 * pairs] + low_real * cosine + low_imag * sine
            imag = rows[4 * pairs + 1] + low_imag * cosine - low_real * sine
            for k in range(pairs):
                cosine, sine = spin(first + k), spin(first + count + k)
                real += rows[k] * cosine - rows[pairs + k] * sine
                imag += rows[2 * pairs + k] * cosine + rows[3 * pairs + k] * sine
            total += real * ends_ref[site, 16 * side : 16 * side + 8]
            total -= imag * ends_ref[site, 16 * side + 8 : 16 * side + 16]
        total += rows[4 * pairs + 4] * ends_ref[site, 32:40] + rows[4 * pairs + 5] * ends_ref[site, 40:]
    mean = middle + jnp.sum(total, axis=0, keepdims=True) * (1.0 / SITES)
    return jnp.broadcast_to(mean, (8, slots))


def resist_kernel(
    intensity_ref, core_ref, chip_ref, inner_ref, outer_ref, waves_ref,
    tents_ref, spin_ref, ends_ref,
    parts_ref, table_ref, middle_ref, mean_ref,
):
    odd = parity()
    chip_edge = jnp.where(has_chip_side(), chip_ref[...], 0.0)
    core_edge = core_ref[...]
    above = jnp.where(odd == 1, core_edge, chip_edge)
    below = jnp.where(odd == 1, chip_edge, core_edge)
    edges = jnp.concatenate([above, below], axis=0).astype(BF16)
    blurred = jnp.dot(inner_ref[...], intensity_ref[...], preferred_element_type=F32)
    blurred += jnp.dot(outer_ref[...], edges, preferred_element_type=F32)
    middle = jnp.sum(jnp.sum(blurred, axis=0, keepdims=True), axis=1, keepdims=True)
    middle = middle * (1.0 / (blurred.shape[0] * blurred.shape[1]))
    high = blurred.astype(BF16)
    low = (blurred - high.astype(F32)).astype(BF16)
    parts = jnp.concatenate([high, low, high], axis=1)
    parts_ref[...] = parts
    table = transposed_dot(waves_ref[...], parts)
    lowest = table.shape[0] - 2 * BLUR_REACH - 16
    first = lax.broadcasted_iota(jnp.int32, table.shape, 0) == lowest
    table_ref[...] = jnp.where(first, table - middle, table).astype(BF16)
    middle_ref[...] = jnp.broadcast_to(middle, middle_ref.shape)
    mean_ref[...] = site_means(
        table_ref, tents_ref, spin_ref, ends_ref, middle_ref[:1, :1]
    )


def core_kernel(table_ref, tents_ref, spin_ref, ends_ref, middle_ref, mean_ref):
    mean_ref[...] = site_means(
        table_ref, tents_ref, spin_ref, ends_ref, middle_ref[:1, :1]
    )


def own_kernel(
    parts_ref, operator_ref, table_ref, tents_ref, spin_ref, ends_ref, middle_ref,
    resist_hbm, mean_ref, resist_ref, sem,
):
    resist_ref[...] = jnp.dot(parts_ref[...], operator_ref[...], preferred_element_type=F32)
    copy = pltpu.make_async_copy(resist_ref, resist_hbm, sem)
    copy.start()
    mean_ref[...] = site_means(
        table_ref, tents_ref, spin_ref, ends_ref, middle_ref[:1, :1]
    )
    copy.wait()


def bias_kernel(level_ref, places_ref, own_ref, core_ref, chip_ref, steps_ref, out_ref):
    odd = parity() == 1
    core, chip = core_ref[...], chip_ref[...]
    means = (jnp.where(odd, core, chip), own_ref[...], jnp.where(odd, chip, core))
    means = [part[:, i : i + 128] for part in means for i in range(0, part.shape[1], 128)]
    found = []
    for start in range(0, out_ref.shape[1], 128):
        place = jnp.broadcast_to(places_ref[:, start : start + 128], (8, 128))
        tile, lane = place // 128, place % 128
        site_mean = jnp.zeros((8, 128), F32)
        for i, part in enumerate(means):
            site_mean = jnp.where(tile == i, jnp.take_along_axis(part, lane, axis=1), site_mean)
        found.append(site_mean[:1])
    site_mean = jnp.concatenate(found, axis=1)
    out_ref[...] = bias_step * steps_ref[...].astype(F32) - bias_gain * (
        site_mean - level_ref[:1, :1]
    )


def chip_pairs(groups, count):
    pairs = []
    for group in range(groups):
        first = group * count
        for i in range(1, count - 1, 2):
            pairs += [(first + i, first + i + 1), (first + i + 1, first + i)]
    if groups % 2:
        for group in range(groups):
            pairs += [(group * count, (group + 1) * count - 1), ((group + 1) * count - 1, group * count)]
    else:
        for group in range(groups):
            for end in (0, count - 1):
                pairs.append((group * count + end, (group ^ 1) * count + end))
    return pairs


def swap_chips(to_chip):
    pairs = chip_pairs(lax.axis_size("groups"), lax.axis_size("tx"))
    return lax.ppermute(to_chip, ("groups", "tx"), pairs)


def swap_cores(to_core):
    return lax.ppermute(to_core, "tx", [(i, i ^ 1) for i in range(lax.axis_size("tx"))])


def call(kernel, outs, args, smem=(), hbm=(), hbm_outs=(), scratch=(), name=None):
    specs = [
        pl.BlockSpec(
            memory_space=pltpu.SMEM if i in smem else pltpu.HBM if i in hbm else pltpu.VMEM
        )
        for i in range(len(args))
    ]
    args = [
        pltpu.with_memory_space_constraint(arg, pltpu.HBM) if i in hbm else arg
        for i, arg in enumerate(args)
    ]
    return pl.pallas_call(
        kernel,
        out_shape=[jax.ShapeDtypeStruct(s, d) for s, d in outs],
        in_specs=specs,
        out_specs=[
            pl.BlockSpec(memory_space=pltpu.HBM if i in hbm_outs else pltpu.VMEM)
            for i in range(len(outs))
        ],
        scratch_shapes=list(scratch),
        compiler_params=pltpu.CompilerParams(vmem_limit_bytes=VMEM_BYTES),
        name=name,
    )(*args)


def shards(mask, kernel_spectra, kernel_weights, threshold, eval_tile, site_coords, bias_steps):
    tile_rows, tile_cols = mask.shape
    _, row_freqs, kernels, col_freqs = kernel_spectra.shape
    frags = eval_tile.shape[0]
    capacity = frags // 2
    samples = 2 * col_freqs
    flat = kernels * col_freqs
    records = 2 * SITES
    col_forward, side_rows, own_rows, row_inverse, col_inverse = imaging_tables(
        tile_rows, tile_cols, row_freqs, col_freqs
    )
    operator, waves, inner, outer = blur_tables(tile_rows, tile_cols, col_freqs, BLUR_REACH)
    spectrum = ((2 * row_freqs, col_freqs), F32)
    packed = ((records, capacity), F32)
    edge = ((BLUR_REACH, samples), F32)
    means = ((8, capacity), F32)
    site_shapes = [
        ((SITES, tile_rows, capacity), BF16),
        ((SITES, col_freqs // 4, capacity), F32),
        ((SITES, 32 + 2 * BLUR_REACH, capacity), F32),
    ]
    weights = kernel_weights.reshape(1, kernels)

    spectra, to_core, to_chip, targets, coords = call(
        front_kernel,
        [((tile_rows, 2 * col_freqs), BF16), spectrum, spectrum]
        + [((1, frags), jnp.int32), ((records, frags), F32)],
        (
            mask, col_forward, side_rows,
            eval_tile.reshape(1, frags), site_coords.reshape(records, frags),
        ),
        hbm=range(5),
        scratch=[
            pltpu.VMEM(mask.shape, BF16),
            pltpu.VMEM(col_forward.shape, BF16),
            pltpu.VMEM(side_rows.shape, BF16),
            pltpu.SemaphoreType.DMA((5,)),
        ],
        name="front",
    )
    got_chip = swap_chips(to_chip)
    got_core = swap_cores(to_core)
    packed_core, packed_chip, packed_own, places = call(
        pack_kernel,
        [packed] * 3 + [((1, frags), jnp.int32)],
        (spectra, targets, coords),
        scratch=[pltpu.VMEM((3 * capacity, frags), BF16)],
        name="pack",
    )
    coords_chip = swap_chips(packed_chip)
    coords_core = swap_cores(packed_core)
    level, own, inverse, spread, *own_sites = call(
        functools.partial(load_kernel, tile_cols),
        [((8, 128), F32), spectrum, (row_inverse.shape, BF16), (col_inverse.shape, BF16)]
        + site_shapes,
        (spectra, packed_own, threshold, own_rows, row_inverse, col_inverse),
        smem=(2,),
        hbm=(3, 4, 5),
        scratch=[pltpu.VMEM(own_rows.shape, BF16), pltpu.SemaphoreType.DMA((3,))],
        name="load",
    )
    kern = jnp.transpose(kernel_spectra, (0, 2, 1, 3))
    product, edge_core, edge_chip = call(
        edge_kernel,
        [((2 * row_freqs, flat), BF16), edge, edge],
        (
            weights, own, got_core, got_chip, kern, inverse, spread,
        ),
        name="edges",
    )
    edge_chip = swap_chips(edge_chip)
    edge_core = swap_cores(edge_core)
    (intensity,) = call(
        imaging_kernel,
        [((tile_rows, samples), BF16)],
        (weights, product, inverse, spread),
        name="imaging",
    )
    other_sites = call(
        functools.partial(prepare_kernel, tile_cols),
        site_shapes * 2,
        (coords_chip, coords_core),
        name="prepare",
    )
    chip_sites, core_sites = other_sites[:3], other_sites[3:]
    parts, table, middle, mean_chip = call(
        resist_kernel,
        [((tile_rows, 3 * samples), BF16), ((waves.shape[0], tile_rows), BF16), ((8, 128), F32), means],
        (intensity, edge_core, edge_chip, inner, outer, waves, *chip_sites),
        name="resist",
    )
    back_chip = swap_chips(mean_chip)
    (mean_core,) = call(core_kernel, [means], (table, *core_sites, middle), name="mean_core")
    back_core = swap_cores(mean_core)
    resist, mean_own = call(
        own_kernel,
        [((tile_rows, tile_cols), F32), means],
        (parts, operator, table, *own_sites, middle),
        hbm_outs=(0,),
        scratch=[pltpu.VMEM((tile_rows, tile_cols), F32), pltpu.SemaphoreType.DMA],
        name="mean_own",
    )
    (new_bias,) = call(
        bias_kernel,
        [((1, frags), F32)],
        (level, places, mean_own, back_core, back_chip, bias_steps.reshape(1, frags)),
        name="bias",
    )
    return resist, new_bias.reshape(frags)


def solution(mesh):
    placed = (
        P(("groups", "tx"), None),
        P(),
        P(),
        P(),
        P(("groups", "tx")),
        P(None, None, ("groups", "tx")),
        P(("groups", "tx")),
    )
    return jax.shard_map(
        shards,
        mesh=mesh,
        in_specs=placed,
        out_specs=(P(("groups", "tx"), None), P(("groups", "tx"))),
        check_vma=False,
    )
```

```python
import functools
import math

import jax
import jax.numpy as jnp
import ml_dtypes
import numpy as np
from jax import lax
from jax.experimental import pallas as pl
from jax.experimental.pallas import tpu as pltpu
from jax.sharding import PartitionSpec as P

HALO = 256
BLUR_REACH = 8
SITES = 16

blur_sigma = 3.0
bias_step = 0.5
bias_gain = 2.0

F32 = jnp.float32
BF16 = jnp.bfloat16
SINE = (1.57079628989, -0.645963358138, 0.0796884742403, -0.0046722194159, 0.000150816735945)
COSINE = (0.99999999978, -1.23370053428, 0.253669322509, -0.0208626876045, 0.000917723911039, -2.38245358719e-05)
VMEM_BYTES = 32 * 1024 * 1024


def rounded(table):
    return np.asarray(table, np.float32).astype(ml_dtypes.bfloat16)


def shaped(table):
    result = np.zeros(table.shape, ml_dtypes.bfloat16)
    carry = np.zeros(table.shape[:-1])
    for i in range(table.shape[-1]):
        wanted = table[..., i] + carry
        result[..., i] = rounded(wanted)
        carry = wanted - result[..., i].astype(np.float64)
    return result


def twiddle(position, frequency, period, amplitude):
    phase_index = (position[:, None] * frequency[None, :]) % period
    phase_angle = phase_index * (2.0 * math.pi / period)
    return np.cos(phase_angle) * amplitude, np.sin(phase_angle) * amplitude


def centered(count):
    return np.arange(count) - count // 2


def imaging_tables(tile_rows, tile_cols, row_freqs, col_freqs):
    window_rows = tile_rows + 2 * HALO
    col_cos, col_sin = twiddle(
        np.arange(tile_cols), centered(col_freqs), tile_cols, 1.0 / math.sqrt(tile_cols)
    )
    col_forward = rounded(np.concatenate([col_cos, -col_sin], axis=1))
    row_cos, row_sin = twiddle(
        centered(row_freqs), np.arange(window_rows), window_rows, 1.0 / math.sqrt(window_rows)
    )
    row_forward = rounded(np.concatenate([row_cos, -row_sin], axis=0))
    row_blocks = [row_forward[:, i * tile_rows : (i + 1) * tile_rows] for i in range(3)]
    side_rows = np.concatenate([row_blocks[0], row_blocks[2]], axis=0)
    own_rows = np.ascontiguousarray(row_blocks[1])
    back_cos, back_sin = twiddle(
        np.arange(tile_rows) + HALO, centered(row_freqs), window_rows, 1.0 / math.sqrt(row_freqs)
    )
    row_inverse = rounded(
        np.block([[back_cos, -back_sin], [back_sin, back_cos]])
    )
    samples = 2 * col_freqs
    step = tile_cols // samples
    out_cos, out_sin = twiddle(
        centered(col_freqs), np.arange(samples) * step, tile_cols, 1.0 / math.sqrt(col_freqs)
    )
    col_inverse = rounded(np.block([[out_cos, out_sin], [-out_sin, out_cos]]))
    return col_forward, side_rows, own_rows, row_inverse, col_inverse


def blur_weight(offset, reach):
    every = np.arange(-reach, reach + 1).astype(np.float64)
    norm = np.sum(np.exp(-every * every / (2.0 * blur_sigma * blur_sigma)))
    weight = np.exp(-offset.astype(np.float64) ** 2 / (2.0 * blur_sigma * blur_sigma)) / norm
    return np.where(np.abs(offset) <= reach, weight, 0.0)


def blur_tables(tile_rows, tile_cols, col_freqs, reach):
    line = np.arange(tile_cols)
    col_blur = rounded(blur_weight(line[None, :] - line[:, None], reach))
    samples = 2 * col_freqs
    step = tile_cols // samples
    offset = (line[None, :] - step * np.arange(samples)[:, None]).astype(np.float64)
    half = np.where(offset == 0, 1.0, np.sin(math.pi * offset / tile_cols))
    spread = np.where(
        offset == 0,
        (samples - 1) / samples,
        np.sin((samples - 1) * math.pi * offset / tile_cols) / (samples * half),
    )
    spread_blur = spread @ col_blur.astype(np.float64)
    row_diff = (
        np.arange(tile_rows + 2 * reach)[None, :] - reach - np.arange(tile_rows)[:, None]
    )
    row_blur = rounded(blur_weight(row_diff, reach))
    inner = row_blur[:, reach : reach + tile_rows]
    outer = np.concatenate([row_blur[:, :reach], row_blur[:, reach + tile_rows :]], axis=1)
    operator = np.ascontiguousarray(shaped(spread_blur.T).T)

    freqs = np.arange(col_freqs)
    gauss = blur_weight(np.arange(-reach, reach + 1), reach)
    gauss = rounded(gauss).astype(np.float64)
    theta = 2.0 * math.pi * freqs / tile_cols
    gain = np.cos(theta[:, None] * np.arange(-reach, reach + 1)[None, :]) @ gauss
    gain = gain * np.where(freqs == 0, 1.0, 2.0) / samples
    cosines, sines = twiddle(freqs, np.arange(samples), samples, 1.0)
    real = (gain[:, None] * cosines).reshape(-1, 8, samples)
    imag = (-gain[:, None] * sines).reshape(-1, 8, samples)
    mid = col_freqs // 16
    above, below = slice(mid + 1, None), slice(mid - 1, 0, -1)
    sides = [
        real[above] + real[below], imag[above] - imag[below],
        imag[above] + imag[below], real[above] - real[below],
    ]
    paired = np.concatenate(
        [np.stack([real[mid], imag[mid], real[0], imag[0]]).reshape(-1, samples)]
        + [np.stack(sides, axis=1).reshape(-1, samples)]
    )
    ring = np.zeros((tile_cols, tile_cols))
    for shift in range(-reach, reach + 1):
        ring[line, (line + shift) % tile_cols] = gauss[shift + reach]
    edge = np.concatenate([line[:reach], line[tile_cols - reach :]])
    cut = (spread @ (col_blur.astype(np.float64) - ring)[:, edge]).T
    waves = np.concatenate([paired, cut], axis=0)
    waves = shaped(waves)
    waves = np.concatenate([waves, waves], axis=1)
    return operator, waves, np.ascontiguousarray(inner), np.ascontiguousarray(outer)


def parity():
    return lax.rem(lax.axis_index("tx"), 2)


def has_chip_side():
    me = lax.axis_index("tx")
    return jnp.logical_and(me != 0, me != lax.axis_size("tx") - 1)


def three_parts(values):
    first = values.astype(BF16)
    rest = values - first.astype(F32)
    second = rest.astype(BF16)
    third = (rest - second.astype(F32)).astype(BF16)
    return first, second, third


def transposed_dot(left, right):
    return lax.dot_general(left, right, (((1,), (1,)), ((), ())), preferred_element_type=F32)


def started(sems, *moves):
    copies = [
        pltpu.make_async_copy(source, target, sems.at[i])
        for i, (source, target) in enumerate(moves)
    ]
    for copy in copies:
        copy.start()
    return copies


def part_spectrum(product, freqs, cols):
    real = product[:freqs, :cols] - product[freqs:, cols:]
    imag = product[:freqs, cols:] + product[freqs:, :cols]
    return jnp.concatenate([real, imag], axis=0)


def front_kernel(
    mask_hbm, forward_hbm, rows_hbm, eval_hbm, records_hbm,
    spectra_ref, core_ref, chip_ref, eval_ref, records_ref,
    mask_ref, forward_ref, rows_ref, sems,
):
    depth = mask_ref.shape[1] // 2
    parts = [pl.ds(i * depth, depth) for i in range(2)]
    copies = started(
        sems,
        (mask_hbm, mask_ref),
        (forward_hbm, forward_ref),
        (rows_hbm, rows_ref),
        (eval_hbm, eval_ref),
        (records_hbm, records_ref),
    )
    copies[0].wait()
    copies[1].wait()
    spectra = jnp.dot(mask_ref[...], forward_ref[...], preferred_element_type=F32).astype(BF16)
    spectra_ref[...] = spectra
    copies[2].wait()
    product = jnp.dot(rows_ref[...], spectra, preferred_element_type=F32)
    freqs, cols = core_ref.shape[0] // 2, core_ref.shape[1]
    upper_side = part_spectrum(product[: 2 * freqs], freqs, cols)
    lower_side = part_spectrum(product[2 * freqs :], freqs, cols)
    odd = parity()
    chip_ref[...] = jnp.where(odd == 1, upper_side, lower_side)
    core_ref[...] = jnp.where(odd == 1, lower_side, upper_side)
    copies[3].wait()
    copies[4].wait()


def pack_kernel(
    after_ref, eval_ref, records_ref, packed_core_ref, packed_chip_ref, packed_own_ref, places_ref,
    chosen_ref,
):
    me = lax.axis_index("tx")
    odd = parity()
    frags = eval_ref.shape[1]
    capacity = frags // 2
    count = records_ref.shape[0]
    before = lax.broadcasted_iota(jnp.int32, (frags, frags), 0)
    after = lax.broadcasted_iota(jnp.int32, (frags, frags), 1)
    upper = (before <= after).astype(F32).astype(BF16)
    slots = lax.broadcasted_iota(jnp.int32, (capacity, frags), 0).astype(F32).astype(BF16)
    member = lax.broadcasted_iota(jnp.int32, (8, frags), 0) == eval_ref[...] - me + 1
    counts = jnp.dot(member.astype(F32).astype(BF16), upper, preferred_element_type=F32)
    code = jnp.where(member, counts - 1.0, -1.0)
    side = lax.broadcasted_iota(jnp.int32, (8, frags), 0) * capacity
    place = jnp.where(member, side + counts.astype(jnp.int32) - 1, 0)
    places_ref[...] = jnp.sum(place, axis=0, keepdims=True)
    for side in range(3):
        row = jnp.broadcast_to(code[side : side + 1].astype(BF16), (capacity, frags))
        chosen_ref[pl.ds(side * capacity, capacity)] = jnp.where(
            slots == row, jnp.ones_like(slots), jnp.zeros_like(slots)
        )
    pieces = jnp.concatenate(three_parts(records_ref[...]), axis=0)

    def packed(side, out_ref):
        chosen = chosen_ref[pl.ds(pl.multiple_of(side * capacity, capacity), capacity)]
        got = transposed_dot(pieces, chosen)
        out_ref[...] = got[:count] + got[count : 2 * count] + got[2 * count :]

    packed(2 - 2 * odd, packed_core_ref)
    packed(2 * odd, packed_chip_ref)
    packed(1, packed_own_ref)


def load_kernel(
    cols, spectra_ref, coords_ref, threshold_ref, rows_hbm, inverse_hbm, spread_hbm,
    level_ref, own_ref, inverse_ref, spread_ref, tents_ref, spin_ref, ends_ref,
    rows_ref, sems,
):
    copies = started(
        sems, (rows_hbm, rows_ref), (inverse_hbm, inverse_ref), (spread_hbm, spread_ref)
    )
    level_ref[...] = jnp.full(level_ref.shape, threshold_ref[0], F32)
    site_tables(coords_ref[...], tents_ref, spin_ref, ends_ref, cols)
    copies[0].wait()
    product = jnp.dot(rows_ref[...], spectra_ref[...], preferred_element_type=F32)
    own_ref[...] = part_spectrum(product, own_ref.shape[0] // 2, own_ref.shape[1])
    copies[1].wait()
    copies[2].wait()


def stacked_pairs(half, rows, kernels, cols):
    pairs = []
    for k in range(kernels):
        lanes = slice(k * cols, (k + 1) * cols)
        pairs.append(jnp.concatenate([half[:rows, lanes], half[rows:, lanes]], axis=1))
    return jnp.concatenate(pairs, axis=0)


def edge_kernel(
    weights_ref, own_ref, core_ref, chip_ref, kern_ref, inverse_ref, spread_ref,
    product_ref, edge_core_ref, edge_chip_ref,
):
    freqs, cols = own_ref.shape[0] // 2, own_ref.shape[1]
    rows = inverse_ref.shape[0] // 2
    kernels = kern_ref.shape[1]
    odd = parity()
    chip = jnp.where(has_chip_side(), chip_ref[...], 0.0)
    spectrum = own_ref[...] + core_ref[...] + chip
    spec_real, spec_imag = spectrum[:freqs], spectrum[freqs:]
    for k in range(kernels):
        kern_real, kern_imag = kern_ref[0, k], kern_ref[1, k]
        lanes = slice(k * cols, (k + 1) * cols)
        product_ref[:freqs, lanes] = (kern_real * spec_real - kern_imag * spec_imag).astype(BF16)
        product_ref[freqs:, lanes] = (kern_real * spec_imag + kern_imag * spec_real).astype(BF16)
    reach = BLUR_REACH
    lines = jnp.concatenate(
        [
            inverse_ref[:reach], inverse_ref[rows - reach : rows],
            inverse_ref[rows : rows + reach], inverse_ref[2 * rows - reach :],
        ],
        axis=0,
    )
    half = jnp.dot(lines, product_ref[...], preferred_element_type=F32).astype(BF16)
    pairs = stacked_pairs(half, 2 * reach, kernels, cols)
    field = jnp.dot(pairs, spread_ref[...], preferred_element_type=F32)
    total = jnp.zeros((2 * reach, 2 * cols), F32)
    for k in range(kernels):
        part = field[2 * reach * k : 2 * reach * (k + 1)]
        real, imag = part[:, : 2 * cols], part[:, 2 * cols :]
        total = total + weights_ref[:, k : k + 1] * (real * real + imag * imag)
    values = total.astype(BF16).astype(F32)
    top, bottom = values[:reach], values[reach:]
    edge_core_ref[...] = jnp.where(odd == 1, top, bottom)
    edge_chip_ref[...] = jnp.where(odd == 1, bottom, top)


def prepare_kernel(
    tile_cols, chip_coords_ref, core_coords_ref,
    chip_tents_ref, chip_spin_ref, chip_ends_ref, core_tents_ref, core_spin_ref, core_ends_ref,
):
    site_tables(chip_coords_ref[...], chip_tents_ref, chip_spin_ref, chip_ends_ref, tile_cols)
    site_tables(core_coords_ref[...], core_tents_ref, core_spin_ref, core_ends_ref, tile_cols)


def imaging_kernel(weights_ref, product_ref, inverse_ref, spread_ref, intensity_ref):
    rows, samples = intensity_ref.shape
    cols = samples // 2
    kernels = product_ref.shape[1] // cols
    half = jnp.dot(inverse_ref[...], product_ref[...], preferred_element_type=F32).astype(BF16)
    fields = jnp.dot(
        stacked_pairs(half, rows, kernels, cols), spread_ref[...], preferred_element_type=F32
    )
    total = jnp.zeros((rows, samples), F32)
    for k in range(kernels):
        field = fields[k * rows : (k + 1) * rows]
        real, imag = field[:, :samples], field[:, samples:]
        total = total + weights_ref[:, k : k + 1] * (real * real + imag * imag)
    intensity_ref[...] = total.astype(BF16)


def turned(index, period):
    turns = index * (1.0 / period)
    part = 2.0 * (turns - jnp.floor(turns + 0.5))
    square = part * part
    sine = SINE[-1]
    for term in SINE[-2::-1]:
        sine = sine * square + term
    sine = sine * part
    cosine = COSINE[-1]
    for term in COSINE[-2::-1]:
        cosine = cosine * square + term
    return 1.0 - 2.0 * sine * sine, 2.0 * sine * cosine


def site_tables(coords, tents_ref, spin_ref, ends_ref, tile_cols):
    tile_rows, slots = tents_ref.shape[1:]
    eight = lax.broadcasted_iota(jnp.int32, (8, slots), 0).astype(F32)
    count = spin_ref.shape[1] // 4
    steps = jnp.concatenate([8.0 * eight + 8.0, eight + 8.0 * count], axis=0)
    one_cosine, one_sine = turned(steps, tile_cols)
    line = lax.broadcasted_iota(jnp.int32, (tile_rows, slots), 0).astype(F32).astype(BF16)
    none = jnp.zeros((tile_rows, slots), BF16)
    edge = lax.broadcasted_iota(jnp.int32, (2 * BLUR_REACH, slots), 0).astype(F32)
    edge = jnp.where(edge < BLUR_REACH, edge, edge + (tile_cols - 2.0 * BLUR_REACH))

    def wide(row, dtype=F32):
        return jnp.broadcast_to(row.astype(dtype), (tile_rows, slots))

    for site in range(SITES):
        position = coords[site : site + 1] * (tile_rows - 1)
        low = jnp.minimum(jnp.floor(position), tile_rows - 2.0)
        part = position - low
        high_tent = jnp.where(line == wide(low + 1.0, BF16), wide(part, BF16), none)
        tents_ref[site] = jnp.where(line == wide(low, BF16), wide(1.0 - part, BF16), high_tent)
        position = coords[SITES + site : SITES + site + 1] * (tile_cols - 1)
        low = jnp.minimum(jnp.floor(position), tile_cols - 2.0)
        part = position - low
        cosine, sine = turned(low * steps, tile_cols)
        next_cosine = cosine * one_cosine - sine * one_sine
        next_sine = sine * one_cosine + cosine * one_sine
        spin_ref[site, :8] = cosine[:8]
        spin_ref[site, 8:16] = sine[:8]
        spin_ref[site, 16:24] = next_cosine[:8]
        spin_ref[site, 24:] = next_sine[:8]
        ends_ref[site, :8] = (1.0 - part) * cosine[8:]
        ends_ref[site, 8:16] = (1.0 - part) * sine[8:]
        ends_ref[site, 16:24] = part * next_cosine[8:]
        ends_ref[site, 24:32] = part * next_sine[8:]
        ends_ref[site, 32:] = jnp.maximum(1.0 - jnp.abs(position - edge), 0.0)


def site_means(table_ref, tents_ref, spin_ref, ends_ref, middle, beside=None):
    slots = tents_ref.shape[2]
    count = spin_ref.shape[1] // 4
    pairs = count - 1
    none = jnp.zeros((8, slots), F32)
    total = none
    for site in range(SITES):
        if beside is not None:
            beside(site)
        picked = jnp.dot(table_ref[...], tents_ref[site], preferred_element_type=F32)
        rows = [picked[8 * i : 8 * i + 8] for i in range(4 * pairs + 6)]

        def spin(i):
            return jnp.broadcast_to(spin_ref[site, i : i + 1], (8, slots))

        def ends(i):
            return ends_ref[site, 8 * i : 8 * i + 8]

        sums = []
        for first in (0, 2 * count):
            cosine, sine = spin(first + pairs), spin(first + count + pairs)
            sums.append(rows[0] + rows[2] * cosine + rows[3] * sine)
            sums.append(rows[1] + rows[3] * cosine - rows[2] * sine)
        for k in range(pairs):
            here = rows[4 * k + 4 : 4 * k + 8]
            for side in range(2):
                first = 2 * count * side
                cosine, sine = spin(first + k), spin(first + count + k)
                sums[2 * side] += here[0] * cosine - here[1] * sine
                sums[2 * side + 1] += here[2] * cosine + here[3] * sine
        total += (sums[0] * ends(0) - sums[1] * ends(1)) + (sums[2] * ends(2) - sums[3] * ends(3))
        total += rows[4 * pairs + 4] * ends(4) + rows[4 * pairs + 5] * ends(5)
    mean = middle + jnp.sum(total, axis=0, keepdims=True) * (1.0 / SITES)
    return jnp.broadcast_to(mean, (8, slots))


def resist_kernel(
    intensity_ref, core_ref, chip_ref, inner_ref, outer_ref, waves_ref,
    tents_ref, spin_ref, ends_ref,
    parts_ref, table_ref, middle_ref, mean_ref,
):
    odd = parity()
    chip_edge = jnp.where(has_chip_side(), chip_ref[...], 0.0)
    core_edge = core_ref[...]
    above = jnp.where(odd == 1, core_edge, chip_edge)
    below = jnp.where(odd == 1, chip_edge, core_edge)
    edges = jnp.concatenate([above, below], axis=0).astype(BF16)
    blurred = jnp.dot(inner_ref[...], intensity_ref[...], preferred_element_type=F32)
    blurred += jnp.dot(outer_ref[...], edges, preferred_element_type=F32)
    middle = jnp.sum(jnp.sum(blurred, axis=0, keepdims=True), axis=1, keepdims=True)
    middle = middle * (1.0 / (blurred.shape[0] * blurred.shape[1]))
    high = blurred.astype(BF16)
    low = (blurred - high.astype(F32)).astype(BF16)
    parts = jnp.concatenate([high, low], axis=1)
    parts_ref[...] = parts
    table = transposed_dot(waves_ref[...], parts)
    first = lax.broadcasted_iota(jnp.int32, table.shape, 0) == 16
    table_ref[...] = jnp.where(first, table - middle, table).astype(BF16)
    middle_ref[...] = jnp.broadcast_to(middle, middle_ref.shape)
    mean_ref[...] = site_means(
        table_ref, tents_ref, spin_ref, ends_ref, middle_ref[:1, :1]
    )


def core_kernel(table_ref, tents_ref, spin_ref, ends_ref, middle_ref, mean_ref):
    mean_ref[...] = site_means(
        table_ref, tents_ref, spin_ref, ends_ref, middle_ref[:1, :1]
    )


def own_kernel(
    parts_ref, operator_ref, table_ref, tents_ref, spin_ref, ends_ref, middle_ref,
    resist_hbm, mean_ref, resist_ref, sem,
):
    cols = resist_ref.shape[1] // 4
    copies = []

    def beside(site):
        if site % 3 == 0 and len(copies) < 4:
            lanes = pl.ds(len(copies) * cols, cols)
            block = operator_ref[:, lanes]
            resist_ref[:, lanes] = jnp.dot(
                parts_ref[...], jnp.concatenate([block, block], axis=0), preferred_element_type=F32
            )
            copies.append(
                pltpu.make_async_copy(
                    resist_ref.at[:, lanes], resist_hbm.at[:, lanes], sem.at[len(copies)]
                )
            )
            copies[-1].start()

    mean_ref[...] = site_means(
        table_ref, tents_ref, spin_ref, ends_ref, middle_ref[:1, :1], beside
    )
    for copy in copies:
        copy.wait()


def bias_kernel(level_ref, places_ref, own_ref, core_ref, chip_ref, steps_ref, out_ref):
    odd = parity() == 1
    core, chip = core_ref[...], chip_ref[...]
    means = (jnp.where(odd, core, chip), own_ref[...], jnp.where(odd, chip, core))
    means = [part[:, i : i + 128] for part in means for i in range(0, part.shape[1], 128)]
    found = []
    for start in range(0, out_ref.shape[1], 128):
        place = jnp.broadcast_to(places_ref[:, start : start + 128], (8, 128))
        tile, lane = place // 128, place % 128
        site_mean = jnp.zeros((8, 128), F32)
        for i, part in enumerate(means):
            site_mean = jnp.where(tile == i, jnp.take_along_axis(part, lane, axis=1), site_mean)
        found.append(site_mean[:1])
    site_mean = jnp.concatenate(found, axis=1)
    out_ref[...] = bias_step * steps_ref[...].astype(F32) - bias_gain * (
        site_mean - level_ref[:1, :1]
    )


def chip_pairs(groups, count):
    pairs = []
    for group in range(groups):
        first = group * count
        for i in range(1, count - 1, 2):
            pairs += [(first + i, first + i + 1), (first + i + 1, first + i)]
    if groups % 2:
        for group in range(groups):
            pairs += [(group * count, (group + 1) * count - 1), ((group + 1) * count - 1, group * count)]
    else:
        for group in range(groups):
            for end in (0, count - 1):
                pairs.append((group * count + end, (group ^ 1) * count + end))
    return pairs


def swap_chips(to_chip):
    pairs = chip_pairs(lax.axis_size("groups"), lax.axis_size("tx"))
    return lax.ppermute(to_chip, ("groups", "tx"), pairs)


def swap_cores(to_core):
    return lax.ppermute(to_core, "tx", [(i, i ^ 1) for i in range(lax.axis_size("tx"))])


def call(kernel, outs, args, smem=(), hbm=(), hbm_outs=(), scratch=(), name=None):
    specs = [
        pl.BlockSpec(
            memory_space=pltpu.SMEM if i in smem else pltpu.HBM if i in hbm else pltpu.VMEM
        )
        for i in range(len(args))
    ]
    args = [
        pltpu.with_memory_space_constraint(arg, pltpu.HBM) if i in hbm else arg
        for i, arg in enumerate(args)
    ]
    return pl.pallas_call(
        kernel,
        out_shape=[jax.ShapeDtypeStruct(s, d) for s, d in outs],
        in_specs=specs,
        out_specs=[
            pl.BlockSpec(memory_space=pltpu.HBM if i in hbm_outs else pltpu.VMEM)
            for i in range(len(outs))
        ],
        scratch_shapes=list(scratch),
        compiler_params=pltpu.CompilerParams(vmem_limit_bytes=VMEM_BYTES),
        name=name,
    )(*args)


def shards(mask, kernel_spectra, kernel_weights, threshold, eval_tile, site_coords, bias_steps):
    tile_rows, tile_cols = mask.shape
    _, row_freqs, kernels, col_freqs = kernel_spectra.shape
    frags = eval_tile.shape[0]
    capacity = frags // 2
    samples = 2 * col_freqs
    flat = kernels * col_freqs
    records = 2 * SITES
    col_forward, side_rows, own_rows, row_inverse, col_inverse = imaging_tables(
        tile_rows, tile_cols, row_freqs, col_freqs
    )
    operator, waves, inner, outer = blur_tables(tile_rows, tile_cols, col_freqs, BLUR_REACH)
    spectrum = ((2 * row_freqs, col_freqs), F32)
    packed = ((records, capacity), F32)
    edge = ((BLUR_REACH, samples), F32)
    means = ((8, capacity), F32)
    site_shapes = [
        ((SITES, tile_rows, capacity), BF16),
        ((SITES, col_freqs // 4, capacity), F32),
        ((SITES, 32 + 2 * BLUR_REACH, capacity), F32),
    ]
    weights = kernel_weights.reshape(1, kernels)

    spectra, to_core, to_chip, targets, coords = call(
        front_kernel,
        [((tile_rows, 2 * col_freqs), BF16), spectrum, spectrum]
        + [((1, frags), jnp.int32), ((records, frags), F32)],
        (
            mask, col_forward, side_rows,
            eval_tile.reshape(1, frags), site_coords.reshape(records, frags),
        ),
        hbm=range(5),
        scratch=[
            pltpu.VMEM(mask.shape, BF16),
            pltpu.VMEM(col_forward.shape, BF16),
            pltpu.VMEM(side_rows.shape, BF16),
            pltpu.SemaphoreType.DMA((5,)),
        ],
        name="front",
    )
    got_chip = swap_chips(to_chip)
    got_core = swap_cores(to_core)
    packed_core, packed_chip, packed_own, places = call(
        pack_kernel,
        [packed] * 3 + [((1, frags), jnp.int32)],
        (spectra, targets, coords),
        scratch=[pltpu.VMEM((3 * capacity, frags), BF16)],
        name="pack",
    )
    coords_chip = swap_chips(packed_chip)
    coords_core = swap_cores(packed_core)
    level, own, inverse, spread, *own_sites = call(
        functools.partial(load_kernel, tile_cols),
        [((8, 128), F32), spectrum, (row_inverse.shape, BF16), (col_inverse.shape, BF16)]
        + site_shapes,
        (spectra, packed_own, threshold, own_rows, row_inverse, col_inverse),
        smem=(2,),
        hbm=(3, 4, 5),
        scratch=[pltpu.VMEM(own_rows.shape, BF16), pltpu.SemaphoreType.DMA((3,))],
        name="load",
    )
    kern = jnp.transpose(kernel_spectra, (0, 2, 1, 3))
    product, edge_core, edge_chip = call(
        edge_kernel,
        [((2 * row_freqs, flat), BF16), edge, edge],
        (
            weights, own, got_core, got_chip, kern, inverse, spread,
        ),
        name="edges",
    )
    edge_chip = swap_chips(edge_chip)
    edge_core = swap_cores(edge_core)
    (intensity,) = call(
        imaging_kernel,
        [((tile_rows, samples), BF16)],
        (weights, product, inverse, spread),
        name="imaging",
    )
    other_sites = call(
        functools.partial(prepare_kernel, tile_cols),
        site_shapes * 2,
        (coords_chip, coords_core),
        name="prepare",
    )
    chip_sites, core_sites = other_sites[:3], other_sites[3:]
    parts, table, middle, mean_chip = call(
        resist_kernel,
        [((tile_rows, 2 * samples), BF16), ((waves.shape[0], tile_rows), BF16), ((8, 128), F32), means],
        (intensity, edge_core, edge_chip, inner, outer, waves, *chip_sites),
        name="resist",
    )
    back_chip = swap_chips(mean_chip)
    (mean_core,) = call(core_kernel, [means], (table, *core_sites, middle), name="mean_core")
    back_core = swap_cores(mean_core)
    resist, mean_own = call(
        own_kernel,
        [((tile_rows, tile_cols), F32), means],
        (parts, operator, table, *own_sites, middle),
        hbm_outs=(0,),
        scratch=[pltpu.VMEM((tile_rows, tile_cols), F32), pltpu.SemaphoreType.DMA((4,))],
        name="mean_own",
    )
    (new_bias,) = call(
        bias_kernel,
        [((1, frags), F32)],
        (level, places, mean_own, back_core, back_chip, bias_steps.reshape(1, frags)),
        name="bias",
    )
    return resist, new_bias.reshape(frags)


def solution(mesh):
    placed = (
        P(("groups", "tx"), None),
        P(),
        P(),
        P(),
        P(("groups", "tx")),
        P(None, None, ("groups", "tx")),
        P(("groups", "tx")),
    )
    return jax.shard_map(
        shards,
        mesh=mesh,
        in_specs=placed,
        out_specs=(P(("groups", "tx"), None), P(("groups", "tx"))),
        check_vma=False,
    )
```

```python
import functools
import math

import jax
import jax.numpy as jnp
import ml_dtypes
import numpy as np
from jax import lax
from jax.experimental import pallas as pl
from jax.experimental.pallas import tpu as pltpu
from jax.sharding import PartitionSpec as P

HALO = 256
BLUR_REACH = 8
SITES = 16

blur_sigma = 3.0
bias_step = 0.5
bias_gain = 2.0

F32 = jnp.float32
BF16 = jnp.bfloat16
SINE = (1.57079628989, -0.645963358138, 0.0796884742403, -0.0046722194159, 0.000150816735945)
COSINE = (0.99999999978, -1.23370053428, 0.253669322509, -0.0208626876045, 0.000917723911039, -2.38245358719e-05)
VMEM_BYTES = 32 * 1024 * 1024


def rounded(table):
    return np.asarray(table, np.float32).astype(ml_dtypes.bfloat16)


def shaped(table):
    result = np.zeros(table.shape, ml_dtypes.bfloat16)
    carry = np.zeros(table.shape[:-1])
    for i in range(table.shape[-1]):
        wanted = table[..., i] + carry
        result[..., i] = rounded(wanted)
        carry = wanted - result[..., i].astype(np.float64)
    return result


def twiddle(position, frequency, period, amplitude):
    phase_index = (position[:, None] * frequency[None, :]) % period
    phase_angle = phase_index * (2.0 * math.pi / period)
    return np.cos(phase_angle) * amplitude, np.sin(phase_angle) * amplitude


def centered(count):
    return np.arange(count) - count // 2


def imaging_tables(tile_rows, tile_cols, row_freqs, col_freqs):
    window_rows = tile_rows + 2 * HALO
    col_cos, col_sin = twiddle(
        np.arange(tile_cols), centered(col_freqs), tile_cols, 1.0 / math.sqrt(tile_cols)
    )
    col_forward = rounded(np.concatenate([col_cos, -col_sin], axis=1))
    row_cos, row_sin = twiddle(
        centered(row_freqs), np.arange(window_rows), window_rows, 1.0 / math.sqrt(window_rows)
    )
    row_forward = rounded(np.concatenate([row_cos, -row_sin], axis=0))
    row_blocks = [row_forward[:, i * tile_rows : (i + 1) * tile_rows] for i in range(3)]
    side_rows = np.concatenate([row_blocks[0], row_blocks[2]], axis=0)
    own_rows = np.ascontiguousarray(row_blocks[1])
    back_cos, back_sin = twiddle(
        np.arange(tile_rows) + HALO, centered(row_freqs), window_rows, 1.0 / math.sqrt(row_freqs)
    )
    row_inverse = rounded(
        np.block([[back_cos, -back_sin], [back_sin, back_cos]])
    )
    reach = BLUR_REACH
    near = np.r_[:reach, tile_rows - reach : tile_rows]
    edge_inverse = np.ascontiguousarray(row_inverse[np.concatenate([near, tile_rows + near])])
    samples = 2 * col_freqs
    step = tile_cols // samples
    out_cos, out_sin = twiddle(
        centered(col_freqs), np.arange(samples) * step, tile_cols, 1.0 / math.sqrt(col_freqs)
    )
    col_inverse = rounded(np.block([[out_cos, out_sin], [-out_sin, out_cos]]))
    return col_forward, side_rows, own_rows, row_inverse, edge_inverse, col_inverse


def blur_weight(offset, reach):
    every = np.arange(-reach, reach + 1).astype(np.float64)
    norm = np.sum(np.exp(-every * every / (2.0 * blur_sigma * blur_sigma)))
    weight = np.exp(-offset.astype(np.float64) ** 2 / (2.0 * blur_sigma * blur_sigma)) / norm
    return np.where(np.abs(offset) <= reach, weight, 0.0)


def blur_tables(tile_rows, tile_cols, col_freqs, reach):
    line = np.arange(tile_cols)
    col_blur = rounded(blur_weight(line[None, :] - line[:, None], reach))
    samples = 2 * col_freqs
    step = tile_cols // samples
    offset = (line[None, :] - step * np.arange(samples)[:, None]).astype(np.float64)
    half = np.where(offset == 0, 1.0, np.sin(math.pi * offset / tile_cols))
    spread = np.where(
        offset == 0,
        (samples - 1) / samples,
        np.sin((samples - 1) * math.pi * offset / tile_cols) / (samples * half),
    )
    spread_blur = spread @ col_blur.astype(np.float64)
    row_diff = (
        np.arange(tile_rows + 2 * reach)[None, :] - reach - np.arange(tile_rows)[:, None]
    )
    row_blur = rounded(blur_weight(row_diff, reach))
    inner = row_blur[:, reach : reach + tile_rows]
    outer = np.concatenate([row_blur[:, :reach], row_blur[:, reach + tile_rows :]], axis=1)
    operator = np.ascontiguousarray(shaped(spread_blur.T).T)

    freqs = np.arange(col_freqs)
    gauss = blur_weight(np.arange(-reach, reach + 1), reach)
    gauss = rounded(gauss).astype(np.float64)
    theta = 2.0 * math.pi * freqs / tile_cols
    gain = np.cos(theta[:, None] * np.arange(-reach, reach + 1)[None, :]) @ gauss
    gain = gain * np.where(freqs == 0, 1.0, 2.0) / samples
    cosines, sines = twiddle(freqs, np.arange(samples), samples, 1.0)
    real = (gain[:, None] * cosines).reshape(-1, 8, samples)
    imag = (-gain[:, None] * sines).reshape(-1, 8, samples)
    mid = col_freqs // 16
    above, below = slice(mid + 1, None), slice(mid - 1, 0, -1)
    sides = [
        real[above] + real[below], imag[above] - imag[below],
        imag[above] + imag[below], real[above] - real[below],
    ]
    paired = np.concatenate(
        [np.stack([real[mid], imag[mid], real[0], imag[0]]).reshape(-1, samples)]
        + [np.stack(sides, axis=1).reshape(-1, samples)]
    )
    ring = np.zeros((tile_cols, tile_cols))
    for shift in range(-reach, reach + 1):
        ring[line, (line + shift) % tile_cols] = gauss[shift + reach]
    edge = np.concatenate([line[:reach], line[tile_cols - reach :]])
    cut = (spread @ (col_blur.astype(np.float64) - ring)[:, edge]).T
    waves = np.concatenate([paired, cut], axis=0)
    waves = shaped(waves)
    waves = np.concatenate([waves, waves], axis=1)
    return operator, waves, np.ascontiguousarray(inner), np.ascontiguousarray(outer)


def parity():
    return lax.rem(lax.axis_index("tx"), 2)


def has_chip_side():
    me = lax.axis_index("tx")
    return jnp.logical_and(me != 0, me != lax.axis_size("tx") - 1)


def three_parts(values):
    first = values.astype(BF16)
    rest = values - first.astype(F32)
    second = rest.astype(BF16)
    third = (rest - second.astype(F32)).astype(BF16)
    return first, second, third


def transposed_dot(left, right):
    return lax.dot_general(left, right, (((1,), (1,)), ((), ())), preferred_element_type=F32)


def started(sems, *moves):
    copies = [
        pltpu.make_async_copy(source, target, sems.at[i])
        for i, (source, target) in enumerate(moves)
    ]
    for copy in copies:
        copy.start()
    return copies


def part_spectrum(product, freqs, cols):
    real = product[:freqs, :cols] - product[freqs:, cols:]
    imag = product[:freqs, cols:] + product[freqs:, :cols]
    return jnp.concatenate([real, imag], axis=0)


def front_kernel(
    mask_hbm, forward_hbm, rows_hbm, eval_hbm, records_hbm,
    spectra_ref, core_ref, chip_ref, eval_ref, records_ref,
    mask_ref, forward_ref, rows_ref, sems,
):
    depth = mask_ref.shape[1] // 2
    parts = [pl.ds(i * depth, depth) for i in range(2)]
    copies = started(
        sems,
        (mask_hbm, mask_ref),
        (forward_hbm, forward_ref),
        (rows_hbm, rows_ref),
        (eval_hbm, eval_ref),
        (records_hbm, records_ref),
    )
    copies[0].wait()
    copies[1].wait()
    spectra = jnp.dot(mask_ref[...], forward_ref[...], preferred_element_type=F32).astype(BF16)
    spectra_ref[...] = spectra
    copies[2].wait()
    product = jnp.dot(rows_ref[...], spectra, preferred_element_type=F32)
    freqs, cols = core_ref.shape[0] // 2, core_ref.shape[1]
    upper_side = part_spectrum(product[: 2 * freqs], freqs, cols)
    lower_side = part_spectrum(product[2 * freqs :], freqs, cols)
    odd = parity()
    chip_ref[...] = jnp.where(odd == 1, upper_side, lower_side)
    core_ref[...] = jnp.where(odd == 1, lower_side, upper_side)
    copies[3].wait()
    copies[4].wait()


def pack_kernel(
    after_ref, eval_ref, records_ref, packed_core_ref, packed_chip_ref, packed_own_ref, places_ref,
    chosen_ref,
):
    me = lax.axis_index("tx")
    odd = parity()
    frags = eval_ref.shape[1]
    capacity = frags // 2
    count = records_ref.shape[0]
    before = lax.broadcasted_iota(jnp.int32, (frags, frags), 0)
    after = lax.broadcasted_iota(jnp.int32, (frags, frags), 1)
    upper = (before <= after).astype(F32).astype(BF16)
    slots = lax.broadcasted_iota(jnp.int32, (capacity, frags), 0).astype(F32).astype(BF16)
    member = lax.broadcasted_iota(jnp.int32, (8, frags), 0) == eval_ref[...] - me + 1
    counts = jnp.dot(member.astype(F32).astype(BF16), upper, preferred_element_type=F32)
    code = jnp.where(member, counts - 1.0, -1.0)
    side = lax.broadcasted_iota(jnp.int32, (8, frags), 0) * capacity
    place = jnp.where(member, side + counts.astype(jnp.int32) - 1, 0)
    places_ref[...] = jnp.sum(place, axis=0, keepdims=True)
    for side in range(3):
        row = jnp.broadcast_to(code[side : side + 1].astype(BF16), (capacity, frags))
        chosen_ref[pl.ds(side * capacity, capacity)] = jnp.where(
            slots == row, jnp.ones_like(slots), jnp.zeros_like(slots)
        )
    pieces = jnp.concatenate(three_parts(records_ref[...]), axis=0)

    def packed(side, out_ref):
        chosen = chosen_ref[pl.ds(pl.multiple_of(side * capacity, capacity), capacity)]
        got = transposed_dot(pieces, chosen)
        out_ref[...] = got[:count] + got[count : 2 * count] + got[2 * count :]

    packed(2 - 2 * odd, packed_core_ref)
    packed(2 * odd, packed_chip_ref)
    packed(1, packed_own_ref)


def load_kernel(
    cols, spectra_ref, coords_ref, threshold_ref, rows_hbm, inverse_hbm, lines_hbm, spread_hbm,
    level_ref, own_ref, inverse_ref, lines_ref, spread_ref, tents_ref, spin_ref, ends_ref,
    rows_ref, sems,
):
    copies = started(
        sems,
        (rows_hbm, rows_ref), (inverse_hbm, inverse_ref), (lines_hbm, lines_ref), (spread_hbm, spread_ref),
    )
    level_ref[...] = jnp.full(level_ref.shape, threshold_ref[0], F32)
    site_tables(coords_ref[...], tents_ref, spin_ref, ends_ref, cols)
    copies[0].wait()
    product = jnp.dot(rows_ref[...], spectra_ref[...], preferred_element_type=F32)
    own_ref[...] = part_spectrum(product, own_ref.shape[0] // 2, own_ref.shape[1])
    for copy in copies[1:]:
        copy.wait()


def stacked_pairs(half, rows, kernels, cols):
    pairs = []
    for k in range(kernels):
        lanes = slice(k * cols, (k + 1) * cols)
        pairs.append(jnp.concatenate([half[:rows, lanes], half[rows:, lanes]], axis=1))
    return jnp.concatenate(pairs, axis=0)


def edge_kernel(
    weights_ref, own_ref, core_ref, chip_ref, kern_ref, lines_ref, spread_ref,
    product_ref, edge_core_ref, edge_chip_ref,
):
    freqs, cols = own_ref.shape[0] // 2, own_ref.shape[1]
    kernels = kern_ref.shape[1]
    odd = parity()
    chip = jnp.where(has_chip_side(), chip_ref[...], 0.0)
    spectrum = own_ref[...] + core_ref[...] + chip
    spec_real, spec_imag = spectrum[:freqs], spectrum[freqs:]
    for k in range(kernels):
        kern_real, kern_imag = kern_ref[0, k], kern_ref[1, k]
        lanes = slice(k * cols, (k + 1) * cols)
        product_ref[:freqs, lanes] = (kern_real * spec_real - kern_imag * spec_imag).astype(BF16)
        product_ref[freqs:, lanes] = (kern_real * spec_imag + kern_imag * spec_real).astype(BF16)
    reach = BLUR_REACH
    half = jnp.dot(lines_ref[...], product_ref[...], preferred_element_type=F32).astype(BF16)
    pairs = stacked_pairs(half, 2 * reach, kernels, cols)
    field = jnp.dot(pairs, spread_ref[...], preferred_element_type=F32)
    total = jnp.zeros((2 * reach, 2 * cols), F32)
    for k in range(kernels):
        part = field[2 * reach * k : 2 * reach * (k + 1)]
        real, imag = part[:, : 2 * cols], part[:, 2 * cols :]
        total = total + weights_ref[:, k : k + 1] * (real * real + imag * imag)
    values = total.astype(BF16).astype(F32)
    top, bottom = values[:reach], values[reach:]
    edge_core_ref[...] = jnp.where(odd == 1, top, bottom)
    edge_chip_ref[...] = jnp.where(odd == 1, bottom, top)


def prepare_kernel(
    tile_cols, chip_coords_ref, core_coords_ref,
    chip_tents_ref, chip_spin_ref, chip_ends_ref, core_tents_ref, core_spin_ref, core_ends_ref,
):
    site_tables(chip_coords_ref[...], chip_tents_ref, chip_spin_ref, chip_ends_ref, tile_cols)
    site_tables(core_coords_ref[...], core_tents_ref, core_spin_ref, core_ends_ref, tile_cols)


def imaging_kernel(weights_ref, product_ref, inverse_ref, spread_ref, intensity_ref):
    rows, samples = intensity_ref.shape
    cols = samples // 2
    kernels = product_ref.shape[1] // cols
    half = jnp.dot(inverse_ref[...], product_ref[...], preferred_element_type=F32).astype(BF16)
    fields = jnp.dot(
        stacked_pairs(half, rows, kernels, cols), spread_ref[...], preferred_element_type=F32
    )
    total = jnp.zeros((rows, samples), F32)
    for k in range(kernels):
        field = fields[k * rows : (k + 1) * rows]
        real, imag = field[:, :samples], field[:, samples:]
        total = total + weights_ref[:, k : k + 1] * (real * real + imag * imag)
    intensity_ref[...] = total.astype(BF16)


def turned(index, period):
    turns = index * (1.0 / period)
    part = 2.0 * (turns - jnp.floor(turns + 0.5))
    square = part * part
    sine = SINE[-1]
    for term in SINE[-2::-1]:
        sine = sine * square + term
    sine = sine * part
    cosine = COSINE[-1]
    for term in COSINE[-2::-1]:
        cosine = cosine * square + term
    return 1.0 - 2.0 * sine * sine, 2.0 * sine * cosine


def site_tables(coords, tents_ref, spin_ref, ends_ref, tile_cols):
    tile_rows, slots = tents_ref.shape[1:]
    eight = lax.broadcasted_iota(jnp.int32, (8, slots), 0).astype(F32)
    count = spin_ref.shape[1] // 4
    steps = jnp.concatenate([8.0 * eight + 8.0, eight + 8.0 * count], axis=0)
    one_cosine, one_sine = turned(steps, tile_cols)
    line = lax.broadcasted_iota(jnp.int32, (tile_rows, slots), 0).astype(F32).astype(BF16)
    none = jnp.zeros((tile_rows, slots), BF16)
    edge = lax.broadcasted_iota(jnp.int32, (2 * BLUR_REACH, slots), 0).astype(F32)
    edge = jnp.where(edge < BLUR_REACH, edge, edge + (tile_cols - 2.0 * BLUR_REACH))

    def wide(row, dtype=F32):
        return jnp.broadcast_to(row.astype(dtype), (tile_rows, slots))

    for site in range(SITES):
        position = coords[site : site + 1] * (tile_rows - 1)
        low = jnp.minimum(jnp.floor(position), tile_rows - 2.0)
        part = position - low
        high_tent = jnp.where(line == wide(low + 1.0, BF16), wide(part, BF16), none)
        tents_ref[site] = jnp.where(line == wide(low, BF16), wide(1.0 - part, BF16), high_tent)
        position = coords[SITES + site : SITES + site + 1] * (tile_cols - 1)
        low = jnp.minimum(jnp.floor(position), tile_cols - 2.0)
        part = position - low
        cosine, sine = turned(low * steps, tile_cols)
        next_cosine = cosine * one_cosine - sine * one_sine
        next_sine = sine * one_cosine + cosine * one_sine
        spin_ref[site, :8] = cosine[:8]
        spin_ref[site, 8:16] = sine[:8]
        spin_ref[site, 16:24] = next_cosine[:8]
        spin_ref[site, 24:] = next_sine[:8]
        ends_ref[site, :8] = (1.0 - part) * cosine[8:]
        ends_ref[site, 8:16] = (1.0 - part) * sine[8:]
        ends_ref[site, 16:24] = part * next_cosine[8:]
        ends_ref[site, 24:32] = part * next_sine[8:]
        ends_ref[site, 32:] = jnp.maximum(1.0 - jnp.abs(position - edge), 0.0)


def site_means(table_ref, tents_ref, spin_ref, ends_ref, middle, beside=None):
    slots = tents_ref.shape[2]
    count = spin_ref.shape[1] // 4
    pairs = count - 1
    none = jnp.zeros((8, slots), F32)
    total = none
    for site in range(SITES):
        if beside is not None:
            beside(site)
        picked = jnp.dot(table_ref[...], tents_ref[site], preferred_element_type=F32)
        rows = [picked[8 * i : 8 * i + 8] for i in range(4 * pairs + 6)]

        def spin(i):
            return jnp.broadcast_to(spin_ref[site, i : i + 1], (8, slots))

        def ends(i):
            return ends_ref[site, 8 * i : 8 * i + 8]

        sums = []
        for first in (0, 2 * count):
            cosine, sine = spin(first + pairs), spin(first + count + pairs)
            sums.append(rows[0] + rows[2] * cosine + rows[3] * sine)
            sums.append(rows[1] + rows[3] * cosine - rows[2] * sine)
        for k in range(pairs):
            here = rows[4 * k + 4 : 4 * k + 8]
            for side in range(2):
                first = 2 * count * side
                cosine, sine = spin(first + k), spin(first + count + k)
                sums[2 * side] += here[0] * cosine - here[1] * sine
                sums[2 * side + 1] += here[2] * cosine + here[3] * sine
        total += (sums[0] * ends(0) - sums[1] * ends(1)) + (sums[2] * ends(2) - sums[3] * ends(3))
        total += rows[4 * pairs + 4] * ends(4) + rows[4 * pairs + 5] * ends(5)
    mean = middle + jnp.sum(total, axis=0, keepdims=True) * (1.0 / SITES)
    return jnp.broadcast_to(mean, (8, slots))


def resist_kernel(
    intensity_ref, core_ref, chip_ref, inner_ref, outer_ref, waves_ref,
    tents_ref, spin_ref, ends_ref,
    parts_ref, table_ref, middle_ref, mean_ref,
):
    odd = parity()
    chip_edge = jnp.where(has_chip_side(), chip_ref[...], 0.0)
    core_edge = core_ref[...]
    above = jnp.where(odd == 1, core_edge, chip_edge)
    below = jnp.where(odd == 1, chip_edge, core_edge)
    edges = jnp.concatenate([above, below], axis=0).astype(BF16)
    blurred = jnp.dot(inner_ref[...], intensity_ref[...], preferred_element_type=F32)
    blurred += jnp.dot(outer_ref[...], edges, preferred_element_type=F32)
    middle = jnp.sum(jnp.sum(blurred, axis=0, keepdims=True), axis=1, keepdims=True)
    middle = middle * (1.0 / (blurred.shape[0] * blurred.shape[1]))
    high = blurred.astype(BF16)
    low = (blurred - high.astype(F32)).astype(BF16)
    parts = jnp.concatenate([high, low], axis=1)
    parts_ref[...] = parts
    table = transposed_dot(waves_ref[...], parts)
    first = lax.broadcasted_iota(jnp.int32, table.shape, 0) == 16
    table_ref[...] = jnp.where(first, table - middle, table).astype(BF16)
    middle_ref[...] = jnp.broadcast_to(middle, middle_ref.shape)
    mean_ref[...] = site_means(
        table_ref, tents_ref, spin_ref, ends_ref, middle_ref[:1, :1]
    )


def core_kernel(table_ref, tents_ref, spin_ref, ends_ref, middle_ref, mean_ref):
    mean_ref[...] = site_means(
        table_ref, tents_ref, spin_ref, ends_ref, middle_ref[:1, :1]
    )


def own_kernel(
    parts_ref, operator_ref, table_ref, tents_ref, spin_ref, ends_ref, middle_ref,
    resist_hbm, mean_ref, resist_ref, sem,
):
    cols = resist_ref.shape[1] // 4
    copies = []

    def beside(site):
        if site % 3 == 0 and len(copies) < 4:
            lanes = pl.ds(len(copies) * cols, cols)
            block = operator_ref[:, lanes]
            resist_ref[:, lanes] = jnp.dot(
                parts_ref[...], jnp.concatenate([block, block], axis=0), preferred_element_type=F32
            )
            copies.append(
                pltpu.make_async_copy(
                    resist_ref.at[:, lanes], resist_hbm.at[:, lanes], sem.at[len(copies)]
                )
            )
            copies[-1].start()

    mean_ref[...] = site_means(
        table_ref, tents_ref, spin_ref, ends_ref, middle_ref[:1, :1], beside
    )
    for copy in copies:
        copy.wait()


def bias_kernel(level_ref, places_ref, own_ref, core_ref, chip_ref, steps_ref, out_ref):
    odd = parity() == 1
    core, chip = core_ref[...], chip_ref[...]
    means = (jnp.where(odd, core, chip), own_ref[...], jnp.where(odd, chip, core))
    means = [part[:, i : i + 128] for part in means for i in range(0, part.shape[1], 128)]
    found = []
    for start in range(0, out_ref.shape[1], 128):
        place = jnp.broadcast_to(places_ref[:, start : start + 128], (8, 128))
        tile, lane = place // 128, place % 128
        site_mean = jnp.zeros((8, 128), F32)
        for i, part in enumerate(means):
            site_mean = jnp.where(tile == i, jnp.take_along_axis(part, lane, axis=1), site_mean)
        found.append(site_mean[:1])
    site_mean = jnp.concatenate(found, axis=1)
    out_ref[...] = bias_step * steps_ref[...].astype(F32) - bias_gain * (
        site_mean - level_ref[:1, :1]
    )


def chip_pairs(groups, count):
    pairs = []
    for group in range(groups):
        first = group * count
        for i in range(1, count - 1, 2):
            pairs += [(first + i, first + i + 1), (first + i + 1, first + i)]
    if groups % 2:
        for group in range(groups):
            pairs += [(group * count, (group + 1) * count - 1), ((group + 1) * count - 1, group * count)]
    else:
        for group in range(groups):
            for end in (0, count - 1):
                pairs.append((group * count + end, (group ^ 1) * count + end))
    return pairs


def swap_chips(to_chip):
    pairs = chip_pairs(lax.axis_size("groups"), lax.axis_size("tx"))
    return lax.ppermute(to_chip, ("groups", "tx"), pairs)


def swap_cores(to_core):
    return lax.ppermute(to_core, "tx", [(i, i ^ 1) for i in range(lax.axis_size("tx"))])


def call(kernel, outs, args, smem=(), hbm=(), hbm_outs=(), scratch=(), name=None):
    specs = [
        pl.BlockSpec(
            memory_space=pltpu.SMEM if i in smem else pltpu.HBM if i in hbm else pltpu.VMEM
        )
        for i in range(len(args))
    ]
    args = [
        pltpu.with_memory_space_constraint(arg, pltpu.HBM) if i in hbm else arg
        for i, arg in enumerate(args)
    ]
    return pl.pallas_call(
        kernel,
        out_shape=[jax.ShapeDtypeStruct(s, d) for s, d in outs],
        in_specs=specs,
        out_specs=[
            pl.BlockSpec(memory_space=pltpu.HBM if i in hbm_outs else pltpu.VMEM)
            for i in range(len(outs))
        ],
        scratch_shapes=list(scratch),
        compiler_params=pltpu.CompilerParams(vmem_limit_bytes=VMEM_BYTES),
        name=name,
    )(*args)


def shards(mask, kernel_spectra, kernel_weights, threshold, eval_tile, site_coords, bias_steps):
    tile_rows, tile_cols = mask.shape
    _, row_freqs, kernels, col_freqs = kernel_spectra.shape
    frags = eval_tile.shape[0]
    capacity = frags // 2
    samples = 2 * col_freqs
    flat = kernels * col_freqs
    records = 2 * SITES
    col_forward, side_rows, own_rows, row_inverse, edge_inverse, col_inverse = imaging_tables(
        tile_rows, tile_cols, row_freqs, col_freqs
    )
    operator, waves, inner, outer = blur_tables(tile_rows, tile_cols, col_freqs, BLUR_REACH)
    spectrum = ((2 * row_freqs, col_freqs), F32)
    packed = ((records, capacity), F32)
    edge = ((BLUR_REACH, samples), F32)
    means = ((8, capacity), F32)
    site_shapes = [
        ((SITES, tile_rows, capacity), BF16),
        ((SITES, col_freqs // 4, capacity), F32),
        ((SITES, 32 + 2 * BLUR_REACH, capacity), F32),
    ]
    weights = kernel_weights.reshape(1, kernels)

    spectra, to_core, to_chip, targets, coords = call(
        front_kernel,
        [((tile_rows, 2 * col_freqs), BF16), spectrum, spectrum]
        + [((1, frags), jnp.int32), ((records, frags), F32)],
        (
            mask, col_forward, side_rows,
            eval_tile.reshape(1, frags), site_coords.reshape(records, frags),
        ),
        hbm=range(5),
        scratch=[
            pltpu.VMEM(mask.shape, BF16),
            pltpu.VMEM(col_forward.shape, BF16),
            pltpu.VMEM(side_rows.shape, BF16),
            pltpu.SemaphoreType.DMA((5,)),
        ],
        name="front",
    )
    got_chip = swap_chips(to_chip)
    got_core = swap_cores(to_core)
    packed_core, packed_chip, packed_own, places = call(
        pack_kernel,
        [packed] * 3 + [((1, frags), jnp.int32)],
        (spectra, targets, coords),
        scratch=[pltpu.VMEM((3 * capacity, frags), BF16)],
        name="pack",
    )
    coords_chip = swap_chips(packed_chip)
    coords_core = swap_cores(packed_core)
    tables = (row_inverse, edge_inverse, col_inverse)
    level, own, inverse, lines, spread, *own_sites = call(
        functools.partial(load_kernel, tile_cols),
        [((8, 128), F32), spectrum] + [(table.shape, BF16) for table in tables] + site_shapes,
        (spectra, packed_own, threshold, own_rows, *tables),
        smem=(2,),
        hbm=(3, 4, 5, 6),
        scratch=[pltpu.VMEM(own_rows.shape, BF16), pltpu.SemaphoreType.DMA((4,))],
        name="load",
    )
    kern = jnp.transpose(kernel_spectra, (0, 2, 1, 3))
    product, edge_core, edge_chip = call(
        edge_kernel,
        [((2 * row_freqs, flat), BF16), edge, edge],
        (
            weights, own, got_core, got_chip, kern, lines, spread,
        ),
        name="edges",
    )
    edge_chip = swap_chips(edge_chip)
    edge_core = swap_cores(edge_core)
    (intensity,) = call(
        imaging_kernel,
        [((tile_rows, samples), BF16)],
        (weights, product, inverse, spread),
        name="imaging",
    )
    other_sites = call(
        functools.partial(prepare_kernel, tile_cols),
        site_shapes * 2,
        (coords_chip, coords_core),
        name="prepare",
    )
    chip_sites, core_sites = other_sites[:3], other_sites[3:]
    parts, table, middle, mean_chip = call(
        resist_kernel,
        [((tile_rows, 2 * samples), BF16), ((waves.shape[0], tile_rows), BF16), ((8, 128), F32), means],
        (intensity, edge_core, edge_chip, inner, outer, waves, *chip_sites),
        name="resist",
    )
    back_chip = swap_chips(mean_chip)
    (mean_core,) = call(core_kernel, [means], (table, *core_sites, middle), name="mean_core")
    back_core = swap_cores(mean_core)
    resist, mean_own = call(
        own_kernel,
        [((tile_rows, tile_cols), F32), means],
        (parts, operator, table, *own_sites, middle),
        hbm_outs=(0,),
        scratch=[pltpu.VMEM((tile_rows, tile_cols), F32), pltpu.SemaphoreType.DMA((4,))],
        name="mean_own",
    )
    (new_bias,) = call(
        bias_kernel,
        [((1, frags), F32)],
        (level, places, mean_own, back_core, back_chip, bias_steps.reshape(1, frags)),
        name="bias",
    )
    return resist, new_bias.reshape(frags)


def solution(mesh):
    placed = (
        P(("groups", "tx"), None),
        P(),
        P(),
        P(),
        P(("groups", "tx")),
        P(None, None, ("groups", "tx")),
        P(("groups", "tx")),
    )
    return jax.shard_map(
        shards,
        mesh=mesh,
        in_specs=placed,
        out_specs=(P(("groups", "tx"), None), P(("groups", "tx"))),
        check_vma=False,
    )
```

```python
import functools
import math

import jax
import jax.numpy as jnp
import ml_dtypes
import numpy as np
from jax import lax
from jax.experimental import pallas as pl
from jax.experimental.pallas import tpu as pltpu
from jax.sharding import PartitionSpec as P

HALO = 256
BLUR_REACH = 8
SITES = 16

blur_sigma = 3.0
bias_step = 0.5
bias_gain = 2.0

F32 = jnp.float32
BF16 = jnp.bfloat16
SINE = (1.57079628989, -0.645963358138, 0.0796884742403, -0.0046722194159, 0.000150816735945)
COSINE = (0.99999999978, -1.23370053428, 0.253669322509, -0.0208626876045, 0.000917723911039, -2.38245358719e-05)
VMEM_BYTES = 32 * 1024 * 1024


def rounded(table):
    return np.asarray(table, np.float32).astype(ml_dtypes.bfloat16)


def shaped(table):
    result = np.zeros(table.shape, ml_dtypes.bfloat16)
    carry = np.zeros(table.shape[:-1])
    for i in range(table.shape[-1]):
        wanted = table[..., i] + carry
        result[..., i] = rounded(wanted)
        carry = wanted - result[..., i].astype(np.float64)
    return result


def twiddle(position, frequency, period, amplitude):
    phase_index = (position[:, None] * frequency[None, :]) % period
    phase_angle = phase_index * (2.0 * math.pi / period)
    return np.cos(phase_angle) * amplitude, np.sin(phase_angle) * amplitude


def centered(count):
    return np.arange(count) - count // 2


def imaging_tables(tile_rows, tile_cols, row_freqs, col_freqs):
    window_rows = tile_rows + 2 * HALO
    col_cos, col_sin = twiddle(
        np.arange(tile_cols), centered(col_freqs), tile_cols, 1.0 / math.sqrt(tile_cols)
    )
    col_forward = rounded(np.concatenate([col_cos, -col_sin], axis=1))
    row_cos, row_sin = twiddle(
        centered(row_freqs), np.arange(window_rows), window_rows, 1.0 / math.sqrt(window_rows)
    )
    row_forward = rounded(np.concatenate([row_cos, -row_sin], axis=0))
    row_blocks = [row_forward[:, i * tile_rows : (i + 1) * tile_rows] for i in range(3)]
    side_rows = np.concatenate([row_blocks[0], row_blocks[2]], axis=0)
    own_rows = np.ascontiguousarray(row_blocks[1])
    back_cos, back_sin = twiddle(
        np.arange(tile_rows) + HALO, centered(row_freqs), window_rows, 1.0 / math.sqrt(row_freqs)
    )
    row_inverse = rounded(
        np.block([[back_cos, -back_sin], [back_sin, back_cos]])
    )
    reach = BLUR_REACH
    near = np.r_[:reach, tile_rows - reach : tile_rows]
    edge_inverse = np.ascontiguousarray(row_inverse[np.concatenate([near, tile_rows + near])])
    samples = 2 * col_freqs
    step = tile_cols // samples
    out_cos, out_sin = twiddle(
        centered(col_freqs), np.arange(samples) * step, tile_cols, 1.0 / math.sqrt(col_freqs)
    )
    col_inverse = rounded(np.block([[out_cos, out_sin], [-out_sin, out_cos]]))
    return col_forward, side_rows, own_rows, row_inverse, edge_inverse, col_inverse


def blur_weight(offset, reach):
    every = np.arange(-reach, reach + 1).astype(np.float64)
    norm = np.sum(np.exp(-every * every / (2.0 * blur_sigma * blur_sigma)))
    weight = np.exp(-offset.astype(np.float64) ** 2 / (2.0 * blur_sigma * blur_sigma)) / norm
    return np.where(np.abs(offset) <= reach, weight, 0.0)


def blur_tables(tile_rows, tile_cols, col_freqs, reach):
    line = np.arange(tile_cols)
    col_blur = rounded(blur_weight(line[None, :] - line[:, None], reach))
    samples = 2 * col_freqs
    step = tile_cols // samples
    offset = (line[None, :] - step * np.arange(samples)[:, None]).astype(np.float64)
    half = np.where(offset == 0, 1.0, np.sin(math.pi * offset / tile_cols))
    spread = np.where(
        offset == 0,
        (samples - 1) / samples,
        np.sin((samples - 1) * math.pi * offset / tile_cols) / (samples * half),
    )
    spread_blur = spread @ col_blur.astype(np.float64)
    row_diff = (
        np.arange(tile_rows + 2 * reach)[None, :] - reach - np.arange(tile_rows)[:, None]
    )
    row_blur = rounded(blur_weight(row_diff, reach))
    inner = row_blur[:, reach : reach + tile_rows]
    outer = np.concatenate([row_blur[:, :reach], row_blur[:, reach + tile_rows :]], axis=1)
    operator = np.ascontiguousarray(shaped(spread_blur.T).T)

    freqs = np.arange(col_freqs)
    gauss = blur_weight(np.arange(-reach, reach + 1), reach)
    gauss = rounded(gauss).astype(np.float64)
    theta = 2.0 * math.pi * freqs / tile_cols
    gain = np.cos(theta[:, None] * np.arange(-reach, reach + 1)[None, :]) @ gauss
    gain = gain * np.where(freqs == 0, 1.0, 2.0) / samples
    cosines, sines = twiddle(freqs, np.arange(samples), samples, 1.0)
    real = (gain[:, None] * cosines).reshape(-1, 8, samples)
    imag = (-gain[:, None] * sines).reshape(-1, 8, samples)
    mid = col_freqs // 16
    above, below = slice(mid + 1, None), slice(mid - 1, 0, -1)
    sides = [
        real[above] + real[below], imag[above] - imag[below],
        imag[above] + imag[below], real[above] - real[below],
    ]
    paired = np.concatenate(
        [np.stack([real[mid], imag[mid], real[0], imag[0]]).reshape(-1, samples)]
        + [np.stack(sides, axis=1).reshape(-1, samples)]
    )
    ring = np.zeros((tile_cols, tile_cols))
    for shift in range(-reach, reach + 1):
        ring[line, (line + shift) % tile_cols] = gauss[shift + reach]
    edge = np.concatenate([line[:reach], line[tile_cols - reach :]])
    cut = (spread @ (col_blur.astype(np.float64) - ring)[:, edge]).T
    waves = np.concatenate([paired, cut], axis=0)
    waves = shaped(waves)
    waves = np.concatenate([waves, waves], axis=1)
    return operator, waves, np.ascontiguousarray(inner), np.ascontiguousarray(outer)


def parity():
    return lax.rem(lax.axis_index("tx"), 2)


def has_chip_side():
    me = lax.axis_index("tx")
    return jnp.logical_and(me != 0, me != lax.axis_size("tx") - 1)


def three_parts(values):
    first = values.astype(BF16)
    rest = values - first.astype(F32)
    second = rest.astype(BF16)
    third = (rest - second.astype(F32)).astype(BF16)
    return first, second, third


def transposed_dot(left, right):
    return lax.dot_general(left, right, (((1,), (1,)), ((), ())), preferred_element_type=F32)


def started(sems, *moves):
    copies = [
        pltpu.make_async_copy(source, target, sems.at[i])
        for i, (source, target) in enumerate(moves)
    ]
    for copy in copies:
        copy.start()
    return copies


def part_spectrum(product, freqs, cols):
    real = product[:freqs, :cols] - product[freqs:, cols:]
    imag = product[:freqs, cols:] + product[freqs:, :cols]
    return jnp.concatenate([real, imag], axis=0)


def front_kernel(
    mask_hbm, forward_hbm, rows_hbm, eval_hbm, records_hbm,
    spectra_ref, core_ref, chip_ref, eval_ref, records_ref,
    mask_ref, forward_ref, rows_ref, sems,
):
    depth = mask_ref.shape[1] // 2
    parts = [pl.ds(i * depth, depth) for i in range(2)]
    copies = started(
        sems,
        (mask_hbm, mask_ref),
        (forward_hbm, forward_ref),
        (rows_hbm, rows_ref),
        (eval_hbm, eval_ref),
        (records_hbm, records_ref),
    )
    copies[0].wait()
    copies[1].wait()
    spectra = jnp.dot(mask_ref[...], forward_ref[...], preferred_element_type=F32).astype(BF16)
    spectra_ref[...] = spectra
    copies[2].wait()
    product = jnp.dot(rows_ref[...], spectra, preferred_element_type=F32)
    freqs, cols = core_ref.shape[0] // 2, core_ref.shape[1]
    upper_side = part_spectrum(product[: 2 * freqs], freqs, cols)
    lower_side = part_spectrum(product[2 * freqs :], freqs, cols)
    odd = parity()
    chip_ref[...] = jnp.where(odd == 1, upper_side, lower_side)
    core_ref[...] = jnp.where(odd == 1, lower_side, upper_side)
    copies[3].wait()
    copies[4].wait()


def pack_kernel(
    after_ref, eval_ref, records_ref, packed_core_ref, packed_chip_ref, packed_own_ref, places_ref,
    chosen_ref,
):
    me = lax.axis_index("tx")
    odd = parity()
    frags = eval_ref.shape[1]
    capacity = frags // 2
    count = records_ref.shape[0]
    before = lax.broadcasted_iota(jnp.int32, (frags, frags), 0)
    after = lax.broadcasted_iota(jnp.int32, (frags, frags), 1)
    upper = (before <= after).astype(F32).astype(BF16)
    slots = lax.broadcasted_iota(jnp.int32, (capacity, frags), 0).astype(F32).astype(BF16)
    member = lax.broadcasted_iota(jnp.int32, (8, frags), 0) == eval_ref[...] - me + 1
    counts = jnp.dot(member.astype(F32).astype(BF16), upper, preferred_element_type=F32)
    code = jnp.where(member, counts - 1.0, -1.0)
    side = lax.broadcasted_iota(jnp.int32, (8, frags), 0) * capacity
    place = jnp.where(member, side + counts.astype(jnp.int32) - 1, 0)
    places_ref[...] = jnp.sum(place, axis=0, keepdims=True)
    for side in range(3):
        row = jnp.broadcast_to(code[side : side + 1].astype(BF16), (capacity, frags))
        chosen_ref[pl.ds(side * capacity, capacity)] = jnp.where(
            slots == row, jnp.ones_like(slots), jnp.zeros_like(slots)
        )
    pieces = jnp.concatenate(three_parts(records_ref[...]), axis=0)

    def packed(side, out_ref):
        chosen = chosen_ref[pl.ds(pl.multiple_of(side * capacity, capacity), capacity)]
        got = transposed_dot(pieces, chosen)
        out_ref[...] = got[:count] + got[count : 2 * count] + got[2 * count :]

    packed(2 - 2 * odd, packed_core_ref)
    packed(2 * odd, packed_chip_ref)
    packed(1, packed_own_ref)


def load_kernel(
    cols, spectra_ref, coords_ref, threshold_ref, rows_hbm, inverse_hbm, lines_hbm, spread_hbm,
    level_ref, own_ref, inverse_ref, lines_ref, spread_ref, tents_ref, spin_ref, ends_ref,
    rows_ref, sems,
):
    copies = started(
        sems,
        (rows_hbm, rows_ref), (inverse_hbm, inverse_ref), (lines_hbm, lines_ref), (spread_hbm, spread_ref),
    )
    level_ref[...] = jnp.full(level_ref.shape, threshold_ref[0], F32)
    site_tables(coords_ref[...], tents_ref, spin_ref, ends_ref, cols)
    copies[0].wait()
    product = jnp.dot(rows_ref[...], spectra_ref[...], preferred_element_type=F32)
    own_ref[...] = part_spectrum(product, own_ref.shape[0] // 2, own_ref.shape[1])
    for copy in copies[1:]:
        copy.wait()


def stacked_pairs(half, rows, kernels, cols):
    pairs = []
    for k in range(kernels):
        lanes = slice(k * cols, (k + 1) * cols)
        pairs.append(jnp.concatenate([half[:rows, lanes], half[rows:, lanes]], axis=1))
    return jnp.concatenate(pairs, axis=0)


def edge_kernel(
    weights_ref, own_ref, core_ref, chip_ref, kern_ref, lines_ref, spread_ref,
    product_ref, edge_core_ref, edge_chip_ref,
):
    freqs, cols = own_ref.shape[0] // 2, own_ref.shape[1]
    kernels = kern_ref.shape[1]
    odd = parity()
    chip = jnp.where(has_chip_side(), chip_ref[...], 0.0)
    spectrum = own_ref[...] + core_ref[...] + chip
    spec_real, spec_imag = spectrum[:freqs], spectrum[freqs:]
    for k in range(kernels):
        kern_real, kern_imag = kern_ref[0, k], kern_ref[1, k]
        lanes = slice(k * cols, (k + 1) * cols)
        product_ref[:freqs, lanes] = (kern_real * spec_real - kern_imag * spec_imag).astype(BF16)
        product_ref[freqs:, lanes] = (kern_real * spec_imag + kern_imag * spec_real).astype(BF16)
    reach = BLUR_REACH
    half = jnp.dot(lines_ref[...], product_ref[...], preferred_element_type=F32).astype(BF16)
    pairs = stacked_pairs(half, 2 * reach, kernels, cols)
    field = jnp.dot(pairs, spread_ref[...], preferred_element_type=F32)
    total = jnp.zeros((2 * reach, 2 * cols), F32)
    for k in range(kernels):
        part = field[2 * reach * k : 2 * reach * (k + 1)]
        real, imag = part[:, : 2 * cols], part[:, 2 * cols :]
        total = total + weights_ref[:, k : k + 1] * (real * real + imag * imag)
    values = total.astype(BF16).astype(F32)
    top, bottom = values[:reach], values[reach:]
    edge_core_ref[...] = jnp.where(odd == 1, top, bottom)
    edge_chip_ref[...] = jnp.where(odd == 1, bottom, top)


def prepare_kernel(
    tile_cols, chip_coords_ref, core_coords_ref,
    chip_tents_ref, chip_spin_ref, chip_ends_ref, core_tents_ref, core_spin_ref, core_ends_ref,
):
    site_tables(chip_coords_ref[...], chip_tents_ref, chip_spin_ref, chip_ends_ref, tile_cols)
    site_tables(core_coords_ref[...], core_tents_ref, core_spin_ref, core_ends_ref, tile_cols)


def imaging_kernel(weights_ref, product_ref, inverse_ref, spread_ref, intensity_ref):
    rows, samples = intensity_ref.shape
    cols = samples // 2
    kernels = product_ref.shape[1] // cols
    half = jnp.dot(inverse_ref[...], product_ref[...], preferred_element_type=F32).astype(BF16)
    fields = jnp.dot(
        stacked_pairs(half, rows, kernels, cols), spread_ref[...], preferred_element_type=F32
    )
    total = jnp.zeros((rows, samples), F32)
    for k in range(kernels):
        field = fields[k * rows : (k + 1) * rows]
        real, imag = field[:, :samples], field[:, samples:]
        total = total + weights_ref[:, k : k + 1] * (real * real + imag * imag)
    intensity_ref[...] = total.astype(BF16)


def turned(index, period):
    turns = index * (1.0 / period)
    part = 2.0 * (turns - jnp.floor(turns + 0.5))
    square = part * part
    sine = SINE[-1]
    for term in SINE[-2::-1]:
        sine = sine * square + term
    sine = sine * part
    cosine = COSINE[-1]
    for term in COSINE[-2::-1]:
        cosine = cosine * square + term
    return 1.0 - 2.0 * sine * sine, 2.0 * sine * cosine


def site_tables(coords, tents_ref, spin_ref, ends_ref, tile_cols):
    tile_rows, slots = tents_ref.shape[1:]
    eight = lax.broadcasted_iota(jnp.int32, (8, slots), 0).astype(F32)
    count = spin_ref.shape[1] // 4
    steps = jnp.concatenate([8.0 * eight + 8.0, eight + 8.0 * count], axis=0)
    one_cosine, one_sine = turned(steps, tile_cols)
    line = lax.broadcasted_iota(jnp.int32, (tile_rows, slots), 0).astype(F32).astype(BF16)
    none = jnp.zeros((tile_rows, slots), BF16)
    edge = lax.broadcasted_iota(jnp.int32, (2 * BLUR_REACH, slots), 0).astype(F32)
    edge = jnp.where(edge < BLUR_REACH, edge, edge + (tile_cols - 2.0 * BLUR_REACH))

    def wide(row, dtype=F32):
        return jnp.broadcast_to(row.astype(dtype), (tile_rows, slots))

    for site in range(SITES):
        position = coords[site : site + 1] * (tile_rows - 1)
        low = jnp.minimum(jnp.floor(position), tile_rows - 2.0)
        part = position - low
        high_tent = jnp.where(line == wide(low + 1.0, BF16), wide(part, BF16), none)
        tents_ref[site] = jnp.where(line == wide(low, BF16), wide(1.0 - part, BF16), high_tent)
        position = coords[SITES + site : SITES + site + 1] * (tile_cols - 1)
        low = jnp.minimum(jnp.floor(position), tile_cols - 2.0)
        part = position - low
        cosine, sine = turned(low * steps, tile_cols)
        next_cosine = cosine * one_cosine - sine * one_sine
        next_sine = sine * one_cosine + cosine * one_sine
        spin_ref[site, :8] = cosine[:8]
        spin_ref[site, 8:16] = sine[:8]
        spin_ref[site, 16:24] = next_cosine[:8]
        spin_ref[site, 24:] = next_sine[:8]
        ends_ref[site, :8] = (1.0 - part) * cosine[8:]
        ends_ref[site, 8:16] = (1.0 - part) * sine[8:]
        ends_ref[site, 16:24] = part * next_cosine[8:]
        ends_ref[site, 24:32] = part * next_sine[8:]
        ends_ref[site, 32:] = jnp.maximum(1.0 - jnp.abs(position - edge), 0.0)


def site_means(table_ref, tents_ref, spin_ref, ends_ref, middle, beside=None):
    slots = tents_ref.shape[2]
    count = spin_ref.shape[1] // 4
    pairs = count - 1
    none = jnp.zeros((8, slots), F32)
    total = none
    for site in range(SITES):
        if beside is not None:
            beside(site)
        picked = jnp.dot(table_ref[...], tents_ref[site], preferred_element_type=F32)
        rows = [picked[8 * i : 8 * i + 8] for i in range(4 * pairs + 6)]

        def spin(i):
            return jnp.broadcast_to(spin_ref[site, i : i + 1], (8, slots))

        def ends(i):
            return ends_ref[site, 8 * i : 8 * i + 8]

        sums = []
        for first in (0, 2 * count):
            cosine, sine = spin(first + pairs), spin(first + count + pairs)
            sums.append(rows[0] + rows[2] * cosine + rows[3] * sine)
            sums.append(rows[1] + rows[3] * cosine - rows[2] * sine)
        for k in range(pairs):
            here = rows[4 * k + 4 : 4 * k + 8]
            for side in range(2):
                first = 2 * count * side
                cosine, sine = spin(first + k), spin(first + count + k)
                sums[2 * side] = (sums[2 * side] + here[0] * cosine) - here[1] * sine
                sums[2 * side + 1] = (sums[2 * side + 1] + here[2] * cosine) + here[3] * sine
        total += (sums[0] * ends(0) - sums[1] * ends(1)) + (sums[2] * ends(2) - sums[3] * ends(3))
        total += rows[4 * pairs + 4] * ends(4) + rows[4 * pairs + 5] * ends(5)
    mean = middle + jnp.sum(total, axis=0, keepdims=True) * (1.0 / SITES)
    return jnp.broadcast_to(mean, (8, slots))


def resist_kernel(
    intensity_ref, core_ref, chip_ref, inner_ref, outer_ref, waves_ref,
    tents_ref, spin_ref, ends_ref,
    parts_ref, table_ref, middle_ref, mean_ref,
):
    odd = parity()
    chip_edge = jnp.where(has_chip_side(), chip_ref[...], 0.0)
    core_edge = core_ref[...]
    above = jnp.where(odd == 1, core_edge, chip_edge)
    below = jnp.where(odd == 1, chip_edge, core_edge)
    edges = jnp.concatenate([above, below], axis=0).astype(BF16)
    blurred = jnp.dot(inner_ref[...], intensity_ref[...], preferred_element_type=F32)
    blurred += jnp.dot(outer_ref[...], edges, preferred_element_type=F32)
    middle = jnp.sum(jnp.sum(blurred, axis=0, keepdims=True), axis=1, keepdims=True)
    middle = middle * (1.0 / (blurred.shape[0] * blurred.shape[1]))
    high = blurred.astype(BF16)
    low = (blurred - high.astype(F32)).astype(BF16)
    parts = jnp.concatenate([high, low], axis=1)
    parts_ref[...] = parts
    table = transposed_dot(waves_ref[...], parts)
    first = lax.broadcasted_iota(jnp.int32, table.shape, 0) == 16
    table_ref[...] = jnp.where(first, table - middle, table).astype(BF16)
    middle_ref[...] = jnp.broadcast_to(middle, middle_ref.shape)
    mean_ref[...] = site_means(
        table_ref, tents_ref, spin_ref, ends_ref, middle_ref[:1, :1]
    )


def core_kernel(table_ref, tents_ref, spin_ref, ends_ref, middle_ref, mean_ref):
    mean_ref[...] = site_means(
        table_ref, tents_ref, spin_ref, ends_ref, middle_ref[:1, :1]
    )


def own_kernel(
    parts_ref, operator_ref, table_ref, tents_ref, spin_ref, ends_ref, middle_ref,
    resist_hbm, mean_ref, resist_ref, sem,
):
    cols = resist_ref.shape[1] // 4
    copies = []

    def beside(site):
        if site % 3 == 0 and len(copies) < 4:
            lanes = pl.ds(len(copies) * cols, cols)
            block = operator_ref[:, lanes]
            resist_ref[:, lanes] = jnp.dot(
                parts_ref[...], jnp.concatenate([block, block], axis=0), preferred_element_type=F32
            )
            copies.append(
                pltpu.make_async_copy(
                    resist_ref.at[:, lanes], resist_hbm.at[:, lanes], sem.at[len(copies)]
                )
            )
            copies[-1].start()

    mean_ref[...] = site_means(
        table_ref, tents_ref, spin_ref, ends_ref, middle_ref[:1, :1], beside
    )
    for copy in copies:
        copy.wait()


def bias_kernel(level_ref, places_ref, own_ref, core_ref, chip_ref, steps_ref, out_ref):
    odd = parity() == 1
    core, chip = core_ref[...], chip_ref[...]
    means = (jnp.where(odd, core, chip), own_ref[...], jnp.where(odd, chip, core))
    means = [part[:, i : i + 128] for part in means for i in range(0, part.shape[1], 128)]
    found = []
    for start in range(0, out_ref.shape[1], 128):
        place = jnp.broadcast_to(places_ref[:, start : start + 128], (8, 128))
        tile, lane = place // 128, place % 128
        site_mean = jnp.zeros((8, 128), F32)
        for i, part in enumerate(means):
            site_mean = jnp.where(tile == i, jnp.take_along_axis(part, lane, axis=1), site_mean)
        found.append(site_mean[:1])
    site_mean = jnp.concatenate(found, axis=1)
    out_ref[...] = bias_step * steps_ref[...].astype(F32) - bias_gain * (
        site_mean - level_ref[:1, :1]
    )


def chip_pairs(groups, count):
    pairs = []
    for group in range(groups):
        first = group * count
        for i in range(1, count - 1, 2):
            pairs += [(first + i, first + i + 1), (first + i + 1, first + i)]
    if groups % 2:
        for group in range(groups):
            pairs += [(group * count, (group + 1) * count - 1), ((group + 1) * count - 1, group * count)]
    else:
        for group in range(groups):
            for end in (0, count - 1):
                pairs.append((group * count + end, (group ^ 1) * count + end))
    return pairs


def swap_chips(to_chip):
    pairs = chip_pairs(lax.axis_size("groups"), lax.axis_size("tx"))
    return lax.ppermute(to_chip, ("groups", "tx"), pairs)


def swap_cores(to_core):
    return lax.ppermute(to_core, "tx", [(i, i ^ 1) for i in range(lax.axis_size("tx"))])


def call(kernel, outs, args, smem=(), hbm=(), hbm_outs=(), scratch=(), name=None):
    specs = [
        pl.BlockSpec(
            memory_space=pltpu.SMEM if i in smem else pltpu.HBM if i in hbm else pltpu.VMEM
        )
        for i in range(len(args))
    ]
    args = [
        pltpu.with_memory_space_constraint(arg, pltpu.HBM) if i in hbm else arg
        for i, arg in enumerate(args)
    ]
    return pl.pallas_call(
        kernel,
        out_shape=[jax.ShapeDtypeStruct(s, d) for s, d in outs],
        in_specs=specs,
        out_specs=[
            pl.BlockSpec(memory_space=pltpu.HBM if i in hbm_outs else pltpu.VMEM)
            for i in range(len(outs))
        ],
        scratch_shapes=list(scratch),
        compiler_params=pltpu.CompilerParams(vmem_limit_bytes=VMEM_BYTES),
        name=name,
    )(*args)


def shards(mask, kernel_spectra, kernel_weights, threshold, eval_tile, site_coords, bias_steps):
    tile_rows, tile_cols = mask.shape
    _, row_freqs, kernels, col_freqs = kernel_spectra.shape
    frags = eval_tile.shape[0]
    capacity = frags // 2
    samples = 2 * col_freqs
    flat = kernels * col_freqs
    records = 2 * SITES
    col_forward, side_rows, own_rows, row_inverse, edge_inverse, col_inverse = imaging_tables(
        tile_rows, tile_cols, row_freqs, col_freqs
    )
    operator, waves, inner, outer = blur_tables(tile_rows, tile_cols, col_freqs, BLUR_REACH)
    spectrum = ((2 * row_freqs, col_freqs), F32)
    packed = ((records, capacity), F32)
    edge = ((BLUR_REACH, samples), F32)
    means = ((8, capacity), F32)
    site_shapes = [
        ((SITES, tile_rows, capacity), BF16),
        ((SITES, col_freqs // 4, capacity), F32),
        ((SITES, 32 + 2 * BLUR_REACH, capacity), F32),
    ]
    weights = kernel_weights.reshape(1, kernels)

    spectra, to_core, to_chip, targets, coords = call(
        front_kernel,
        [((tile_rows, 2 * col_freqs), BF16), spectrum, spectrum]
        + [((1, frags), jnp.int32), ((records, frags), F32)],
        (
            mask, col_forward, side_rows,
            eval_tile.reshape(1, frags), site_coords.reshape(records, frags),
        ),
        hbm=range(5),
        scratch=[
            pltpu.VMEM(mask.shape, BF16),
            pltpu.VMEM(col_forward.shape, BF16),
            pltpu.VMEM(side_rows.shape, BF16),
            pltpu.SemaphoreType.DMA((5,)),
        ],
        name="front",
    )
    got_chip = swap_chips(to_chip)
    got_core = swap_cores(to_core)
    packed_core, packed_chip, packed_own, places = call(
        pack_kernel,
        [packed] * 3 + [((1, frags), jnp.int32)],
        (spectra, targets, coords),
        scratch=[pltpu.VMEM((3 * capacity, frags), BF16)],
        name="pack",
    )
    coords_chip = swap_chips(packed_chip)
    coords_core = swap_cores(packed_core)
    tables = (row_inverse, edge_inverse, col_inverse)
    level, own, inverse, lines, spread, *own_sites = call(
        functools.partial(load_kernel, tile_cols),
        [((8, 128), F32), spectrum] + [(table.shape, BF16) for table in tables] + site_shapes,
        (spectra, packed_own, threshold, own_rows, *tables),
        smem=(2,),
        hbm=(3, 4, 5, 6),
        scratch=[pltpu.VMEM(own_rows.shape, BF16), pltpu.SemaphoreType.DMA((4,))],
        name="load",
    )
    kern = jnp.transpose(kernel_spectra, (0, 2, 1, 3))
    product, edge_core, edge_chip = call(
        edge_kernel,
        [((2 * row_freqs, flat), BF16), edge, edge],
        (
            weights, own, got_core, got_chip, kern, lines, spread,
        ),
        name="edges",
    )
    edge_chip = swap_chips(edge_chip)
    edge_core = swap_cores(edge_core)
    (intensity,) = call(
        imaging_kernel,
        [((tile_rows, samples), BF16)],
        (weights, product, inverse, spread),
        name="imaging",
    )
    other_sites = call(
        functools.partial(prepare_kernel, tile_cols),
        site_shapes * 2,
        (coords_chip, coords_core),
        name="prepare",
    )
    chip_sites, core_sites = other_sites[:3], other_sites[3:]
    parts, table, middle, mean_chip = call(
        resist_kernel,
        [((tile_rows, 2 * samples), BF16), ((waves.shape[0], tile_rows), BF16), ((8, 128), F32), means],
        (intensity, edge_core, edge_chip, inner, outer, waves, *chip_sites),
        name="resist",
    )
    back_chip = swap_chips(mean_chip)
    (mean_core,) = call(core_kernel, [means], (table, *core_sites, middle), name="mean_core")
    back_core = swap_cores(mean_core)
    resist, mean_own = call(
        own_kernel,
        [((tile_rows, tile_cols), F32), means],
        (parts, operator, table, *own_sites, middle),
        hbm_outs=(0,),
        scratch=[pltpu.VMEM((tile_rows, tile_cols), F32), pltpu.SemaphoreType.DMA((4,))],
        name="mean_own",
    )
    (new_bias,) = call(
        bias_kernel,
        [((1, frags), F32)],
        (level, places, mean_own, back_core, back_chip, bias_steps.reshape(1, frags)),
        name="bias",
    )
    return resist, new_bias.reshape(frags)


def solution(mesh):
    placed = (
        P(("groups", "tx"), None),
        P(),
        P(),
        P(),
        P(("groups", "tx")),
        P(None, None, ("groups", "tx")),
        P(("groups", "tx")),
    )
    return jax.shard_map(
        shards,
        mesh=mesh,
        in_specs=placed,
        out_specs=(P(("groups", "tx"), None), P(("groups", "tx"))),
        check_vma=False,
    )
```

```python
import functools
import math

import jax
import jax.numpy as jnp
import ml_dtypes
import numpy as np
from jax import lax
from jax.experimental import pallas as pl
from jax.experimental.pallas import tpu as pltpu
from jax.sharding import PartitionSpec as P

HALO = 256
BLUR_REACH = 8
SITES = 16

blur_sigma = 3.0
bias_step = 0.5
bias_gain = 2.0

F32 = jnp.float32
BF16 = jnp.bfloat16
SINE = (1.57079628989, -0.645963358138, 0.0796884742403, -0.0046722194159, 0.000150816735945)
COSINE = (0.99999999978, -1.23370053428, 0.253669322509, -0.0208626876045, 0.000917723911039, -2.38245358719e-05)
VMEM_BYTES = 32 * 1024 * 1024


def rounded(table):
    return np.asarray(table, np.float32).astype(ml_dtypes.bfloat16)


def shaped(table):
    result = np.zeros(table.shape, ml_dtypes.bfloat16)
    carry = np.zeros(table.shape[:-1])
    for i in range(table.shape[-1]):
        wanted = table[..., i] + carry
        result[..., i] = rounded(wanted)
        carry = wanted - result[..., i].astype(np.float64)
    return result


def twiddle(position, frequency, period, amplitude):
    phase_index = (position[:, None] * frequency[None, :]) % period
    phase_angle = phase_index * (2.0 * math.pi / period)
    return np.cos(phase_angle) * amplitude, np.sin(phase_angle) * amplitude


def centered(count):
    return np.arange(count) - count // 2


def imaging_tables(tile_rows, tile_cols, row_freqs, col_freqs):
    window_rows = tile_rows + 2 * HALO
    col_cos, col_sin = twiddle(
        np.arange(tile_cols), centered(col_freqs), tile_cols, 1.0 / math.sqrt(tile_cols)
    )
    col_forward = rounded(np.concatenate([col_cos, -col_sin], axis=1))
    row_cos, row_sin = twiddle(
        centered(row_freqs), np.arange(window_rows), window_rows, 1.0 / math.sqrt(window_rows)
    )
    row_forward = rounded(np.concatenate([row_cos, -row_sin], axis=0))
    row_blocks = [row_forward[:, i * tile_rows : (i + 1) * tile_rows] for i in range(3)]
    side_rows = np.concatenate([row_blocks[0], row_blocks[2]], axis=0)
    own_rows = np.ascontiguousarray(row_blocks[1])
    back_cos, back_sin = twiddle(
        np.arange(tile_rows) + HALO, centered(row_freqs), window_rows, 1.0 / math.sqrt(row_freqs)
    )
    row_inverse = rounded(
        np.block([[back_cos, -back_sin], [back_sin, back_cos]])
    )
    reach = BLUR_REACH
    near = np.r_[:reach, tile_rows - reach : tile_rows]
    edge_inverse = np.ascontiguousarray(row_inverse[np.concatenate([near, tile_rows + near])])
    samples = 2 * col_freqs
    step = tile_cols // samples
    out_cos, out_sin = twiddle(
        centered(col_freqs), np.arange(samples) * step, tile_cols, 1.0 / math.sqrt(col_freqs)
    )
    col_inverse = rounded(np.block([[out_cos, out_sin], [-out_sin, out_cos]]))
    return col_forward, side_rows, own_rows, row_inverse, edge_inverse, col_inverse


def blur_weight(offset, reach):
    every = np.arange(-reach, reach + 1).astype(np.float64)
    norm = np.sum(np.exp(-every * every / (2.0 * blur_sigma * blur_sigma)))
    weight = np.exp(-offset.astype(np.float64) ** 2 / (2.0 * blur_sigma * blur_sigma)) / norm
    return np.where(np.abs(offset) <= reach, weight, 0.0)


def blur_tables(tile_rows, tile_cols, col_freqs, reach):
    line = np.arange(tile_cols)
    col_blur = rounded(blur_weight(line[None, :] - line[:, None], reach))
    samples = 2 * col_freqs
    step = tile_cols // samples
    offset = (line[None, :] - step * np.arange(samples)[:, None]).astype(np.float64)
    half = np.where(offset == 0, 1.0, np.sin(math.pi * offset / tile_cols))
    spread = np.where(
        offset == 0,
        (samples - 1) / samples,
        np.sin((samples - 1) * math.pi * offset / tile_cols) / (samples * half),
    )
    spread_blur = spread @ col_blur.astype(np.float64)
    row_diff = (
        np.arange(tile_rows + 2 * reach)[None, :] - reach - np.arange(tile_rows)[:, None]
    )
    row_blur = rounded(blur_weight(row_diff, reach))
    inner = row_blur[:, reach : reach + tile_rows]
    outer = np.concatenate([row_blur[:, :reach], row_blur[:, reach + tile_rows :]], axis=1)
    operator = np.ascontiguousarray(shaped(spread_blur.T).T)

    freqs = np.arange(col_freqs)
    gauss = blur_weight(np.arange(-reach, reach + 1), reach)
    gauss = rounded(gauss).astype(np.float64)
    theta = 2.0 * math.pi * freqs / tile_cols
    gain = np.cos(theta[:, None] * np.arange(-reach, reach + 1)[None, :]) @ gauss
    gain = gain * np.where(freqs == 0, 1.0, 2.0) / samples
    cosines, sines = twiddle(freqs, np.arange(samples), samples, 1.0)
    real = (gain[:, None] * cosines).reshape(-1, 8, samples)
    imag = (-gain[:, None] * sines).reshape(-1, 8, samples)
    mid = col_freqs // 16
    above, below = slice(mid + 1, None), slice(mid - 1, 0, -1)
    sides = [
        real[above] + real[below], imag[above] - imag[below],
        imag[above] + imag[below], real[above] - real[below],
    ]
    paired = np.concatenate(
        [np.stack([real[mid], imag[mid], real[0], imag[0]]).reshape(-1, samples)]
        + [np.stack(sides, axis=1).reshape(-1, samples)]
    )
    ring = np.zeros((tile_cols, tile_cols))
    for shift in range(-reach, reach + 1):
        ring[line, (line + shift) % tile_cols] = gauss[shift + reach]
    edge = np.concatenate([line[:reach], line[tile_cols - reach :]])
    cut = (spread @ (col_blur.astype(np.float64) - ring)[:, edge]).T
    waves = np.concatenate([paired, cut], axis=0)
    waves = shaped(waves)
    waves = np.concatenate([waves, waves], axis=1)
    return operator, waves, np.ascontiguousarray(inner), np.ascontiguousarray(outer)


def parity():
    return lax.rem(lax.axis_index("tx"), 2)


def has_chip_side():
    me = lax.axis_index("tx")
    return jnp.logical_and(me != 0, me != lax.axis_size("tx") - 1)


def three_parts(values):
    first = values.astype(BF16)
    rest = values - first.astype(F32)
    second = rest.astype(BF16)
    third = (rest - second.astype(F32)).astype(BF16)
    return first, second, third


def transposed_dot(left, right):
    return lax.dot_general(left, right, (((1,), (1,)), ((), ())), preferred_element_type=F32)


def started(sems, *moves):
    copies = [
        pltpu.make_async_copy(source, target, sems.at[i])
        for i, (source, target) in enumerate(moves)
    ]
    for copy in copies:
        copy.start()
    return copies


def part_spectrum(product, freqs, cols):
    real = product[:freqs, :cols] - product[freqs:, cols:]
    imag = product[:freqs, cols:] + product[freqs:, :cols]
    return jnp.concatenate([real, imag], axis=0)


def front_kernel(
    mask_hbm, forward_hbm, rows_hbm, eval_hbm, records_hbm,
    spectra_ref, core_ref, chip_ref, eval_ref, records_ref,
    mask_ref, forward_ref, rows_ref, sems,
):
    copies = started(
        sems,
        (mask_hbm, mask_ref),
        (forward_hbm, forward_ref),
        (rows_hbm, rows_ref),
        (eval_hbm, eval_ref),
        (records_hbm, records_ref),
    )
    copies[0].wait()
    copies[1].wait()
    spectra = jnp.dot(mask_ref[...], forward_ref[...], preferred_element_type=F32).astype(BF16)
    spectra_ref[...] = spectra
    copies[2].wait()
    product = jnp.dot(rows_ref[...], spectra, preferred_element_type=F32)
    freqs, cols = core_ref.shape[0] // 2, core_ref.shape[1]
    upper_side = part_spectrum(product[: 2 * freqs], freqs, cols)
    lower_side = part_spectrum(product[2 * freqs :], freqs, cols)
    odd = parity()
    chip_ref[...] = jnp.where(odd == 1, upper_side, lower_side)
    core_ref[...] = jnp.where(odd == 1, lower_side, upper_side)
    copies[3].wait()
    copies[4].wait()


def pack_kernel(
    after_ref, eval_ref, records_ref, packed_core_ref, packed_chip_ref, packed_own_ref, places_ref,
    chosen_ref,
):
    me = lax.axis_index("tx")
    odd = parity()
    frags = eval_ref.shape[1]
    capacity = frags // 2
    count = records_ref.shape[0]
    before = lax.broadcasted_iota(jnp.int32, (frags, frags), 0)
    after = lax.broadcasted_iota(jnp.int32, (frags, frags), 1)
    upper = (before <= after).astype(F32).astype(BF16)
    slots = lax.broadcasted_iota(jnp.int32, (capacity, frags), 0).astype(F32).astype(BF16)
    member = lax.broadcasted_iota(jnp.int32, (8, frags), 0) == eval_ref[...] - me + 1
    counts = jnp.dot(member.astype(F32).astype(BF16), upper, preferred_element_type=F32)
    code = jnp.where(member, counts - 1.0, -1.0)
    side = lax.broadcasted_iota(jnp.int32, (8, frags), 0) * capacity
    place = jnp.where(member, side + counts.astype(jnp.int32) - 1, 0)
    places_ref[...] = jnp.sum(place, axis=0, keepdims=True)
    for side in range(3):
        row = jnp.broadcast_to(code[side : side + 1].astype(BF16), (capacity, frags))
        chosen_ref[pl.ds(side * capacity, capacity)] = jnp.where(
            slots == row, jnp.ones_like(slots), jnp.zeros_like(slots)
        )
    pieces = jnp.concatenate(three_parts(records_ref[...]), axis=0)

    def packed(side, out_ref):
        chosen = chosen_ref[pl.ds(pl.multiple_of(side * capacity, capacity), capacity)]
        got = transposed_dot(pieces, chosen)
        out_ref[...] = got[:count] + got[count : 2 * count] + got[2 * count :]

    packed(2 - 2 * odd, packed_core_ref)
    packed(2 * odd, packed_chip_ref)
    packed(1, packed_own_ref)


def load_kernel(
    cols, spectra_ref, coords_ref, threshold_ref, rows_hbm, inverse_hbm, lines_hbm, spread_hbm,
    level_ref, own_ref, inverse_ref, lines_ref, spread_ref, tents_ref, spin_ref, ends_ref,
    rows_ref, sems,
):
    copies = started(
        sems,
        (rows_hbm, rows_ref), (inverse_hbm, inverse_ref), (lines_hbm, lines_ref), (spread_hbm, spread_ref),
    )
    level_ref[...] = jnp.full(level_ref.shape, threshold_ref[0], F32)
    site_tables(coords_ref[...], tents_ref, spin_ref, ends_ref, cols)
    copies[0].wait()
    product = jnp.dot(rows_ref[...], spectra_ref[...], preferred_element_type=F32)
    own_ref[...] = part_spectrum(product, own_ref.shape[0] // 2, own_ref.shape[1])
    for copy in copies[1:]:
        copy.wait()


def stacked_pairs(half, rows, kernels, cols):
    pairs = []
    for k in range(kernels):
        lanes = slice(k * cols, (k + 1) * cols)
        pairs.append(jnp.concatenate([half[:rows, lanes], half[rows:, lanes]], axis=1))
    return jnp.concatenate(pairs, axis=0)


def edge_kernel(
    weights_ref, own_ref, core_ref, chip_ref, kern_ref, lines_ref, spread_ref,
    product_ref, edge_core_ref, edge_chip_ref,
):
    freqs, cols = own_ref.shape[0] // 2, own_ref.shape[1]
    kernels = kern_ref.shape[1]
    odd = parity()
    chip = jnp.where(has_chip_side(), chip_ref[...], 0.0)
    spectrum = own_ref[...] + core_ref[...] + chip
    spec_real, spec_imag = spectrum[:freqs], spectrum[freqs:]
    for k in range(kernels):
        kern_real, kern_imag = kern_ref[0, k], kern_ref[1, k]
        lanes = slice(k * cols, (k + 1) * cols)
        product_ref[:freqs, lanes] = (kern_real * spec_real - kern_imag * spec_imag).astype(BF16)
        product_ref[freqs:, lanes] = (kern_real * spec_imag + kern_imag * spec_real).astype(BF16)
    reach = BLUR_REACH
    half = jnp.dot(lines_ref[...], product_ref[...], preferred_element_type=F32).astype(BF16)
    pairs = stacked_pairs(half, 2 * reach, kernels, cols)
    field = jnp.dot(pairs, spread_ref[...], preferred_element_type=F32)
    total = jnp.zeros((2 * reach, 2 * cols), F32)
    for k in range(kernels):
        part = field[2 * reach * k : 2 * reach * (k + 1)]
        real, imag = part[:, : 2 * cols], part[:, 2 * cols :]
        total = total + weights_ref[:, k : k + 1] * (real * real + imag * imag)
    values = total.astype(BF16).astype(F32)
    top, bottom = values[:reach], values[reach:]
    edge_core_ref[...] = jnp.where(odd == 1, top, bottom)
    edge_chip_ref[...] = jnp.where(odd == 1, bottom, top)


def prepare_kernel(
    tile_cols, chip_coords_ref, core_coords_ref,
    chip_tents_ref, chip_spin_ref, chip_ends_ref, core_tents_ref, core_spin_ref, core_ends_ref,
):
    site_tables(chip_coords_ref[...], chip_tents_ref, chip_spin_ref, chip_ends_ref, tile_cols)
    site_tables(core_coords_ref[...], core_tents_ref, core_spin_ref, core_ends_ref, tile_cols)


def imaging_kernel(weights_ref, product_ref, inverse_ref, spread_ref, intensity_ref):
    rows, samples = intensity_ref.shape
    cols = samples // 2
    kernels = product_ref.shape[1] // cols
    half = jnp.dot(inverse_ref[...], product_ref[...], preferred_element_type=F32).astype(BF16)
    fields = jnp.dot(
        stacked_pairs(half, rows, kernels, cols), spread_ref[...], preferred_element_type=F32
    )
    total = jnp.zeros((rows, samples), F32)
    for k in range(kernels):
        field = fields[k * rows : (k + 1) * rows]
        real, imag = field[:, :samples], field[:, samples:]
        total = total + weights_ref[:, k : k + 1] * (real * real + imag * imag)
    intensity_ref[...] = total.astype(BF16)


def turned(index, period):
    turns = index * (1.0 / period)
    part = 2.0 * (turns - jnp.floor(turns + 0.5))
    square = part * part
    sine = SINE[-1]
    for term in SINE[-2::-1]:
        sine = sine * square + term
    sine = sine * part
    cosine = COSINE[-1]
    for term in COSINE[-2::-1]:
        cosine = cosine * square + term
    return 1.0 - 2.0 * sine * sine, 2.0 * sine * cosine


def site_tables(coords, tents_ref, spin_ref, ends_ref, tile_cols):
    tile_rows, slots = tents_ref.shape[1:]
    eight = lax.broadcasted_iota(jnp.int32, (8, slots), 0).astype(F32)
    count = spin_ref.shape[1] // 4
    steps = jnp.concatenate([8.0 * eight + 8.0, eight + 8.0 * count], axis=0)
    one_cosine, one_sine = turned(steps, tile_cols)
    line = lax.broadcasted_iota(jnp.int32, (tile_rows, slots), 0).astype(F32).astype(BF16)
    none = jnp.zeros((tile_rows, slots), BF16)
    edge = lax.broadcasted_iota(jnp.int32, (2 * BLUR_REACH, slots), 0).astype(F32)
    edge = jnp.where(edge < BLUR_REACH, edge, edge + (tile_cols - 2.0 * BLUR_REACH))

    def wide(row, dtype=F32):
        return jnp.broadcast_to(row.astype(dtype), (tile_rows, slots))

    for site in range(SITES):
        position = coords[site : site + 1] * (tile_rows - 1)
        low = jnp.minimum(jnp.floor(position), tile_rows - 2.0)
        part = position - low
        high_tent = jnp.where(line == wide(low + 1.0, BF16), wide(part, BF16), none)
        tents_ref[site] = jnp.where(line == wide(low, BF16), wide(1.0 - part, BF16), high_tent)
        position = coords[SITES + site : SITES + site + 1] * (tile_cols - 1)
        low = jnp.minimum(jnp.floor(position), tile_cols - 2.0)
        part = position - low
        cosine, sine = turned(low * steps, tile_cols)
        next_cosine = cosine * one_cosine - sine * one_sine
        next_sine = sine * one_cosine + cosine * one_sine
        spin_ref[site, :8] = cosine[:8]
        spin_ref[site, 8:16] = sine[:8]
        spin_ref[site, 16:24] = next_cosine[:8]
        spin_ref[site, 24:] = next_sine[:8]
        ends_ref[site, :8] = (1.0 - part) * cosine[8:]
        ends_ref[site, 8:16] = (1.0 - part) * sine[8:]
        ends_ref[site, 16:24] = part * next_cosine[8:]
        ends_ref[site, 24:32] = part * next_sine[8:]
        ends_ref[site, 32:] = jnp.maximum(1.0 - jnp.abs(position - edge), 0.0)


def site_means(table_ref, tents_ref, spin_ref, ends_ref, middle, beside=None):
    slots = tents_ref.shape[2]
    count = spin_ref.shape[1] // 4
    pairs = count - 1
    none = jnp.zeros((8, slots), F32)
    total = none
    for site in range(SITES):
        if beside is not None:
            beside(site)
        picked = jnp.dot(table_ref[...], tents_ref[site], preferred_element_type=F32)
        rows = [picked[8 * i : 8 * i + 8] for i in range(4 * pairs + 6)]

        def spin(i):
            return jnp.broadcast_to(spin_ref[site, i : i + 1], (8, slots))

        def ends(i):
            return ends_ref[site, 8 * i : 8 * i + 8]

        sums = []
        for first in (0, 2 * count):
            cosine, sine = spin(first + pairs), spin(first + count + pairs)
            sums.append(rows[0] + rows[2] * cosine + rows[3] * sine)
            sums.append(rows[1] + rows[3] * cosine - rows[2] * sine)
        for k in range(pairs):
            here = rows[4 * k + 4 : 4 * k + 8]
            for side in range(2):
                first = 2 * count * side
                cosine, sine = spin(first + k), spin(first + count + k)
                sums[2 * side] = (sums[2 * side] + here[0] * cosine) - here[1] * sine
                sums[2 * side + 1] = (sums[2 * side + 1] + here[2] * cosine) + here[3] * sine
        total += (sums[0] * ends(0) - sums[1] * ends(1)) + (sums[2] * ends(2) - sums[3] * ends(3))
        total += rows[4 * pairs + 4] * ends(4) + rows[4 * pairs + 5] * ends(5)
    mean = middle + jnp.sum(total, axis=0, keepdims=True) * (1.0 / SITES)
    return mean


def resist_kernel(
    intensity_ref, core_ref, chip_ref, inner_ref, outer_ref, waves_ref,
    tents_ref, spin_ref, ends_ref,
    parts_ref, table_ref, middle_ref, mean_ref,
):
    odd = parity()
    chip_edge = jnp.where(has_chip_side(), chip_ref[...], 0.0)
    core_edge = core_ref[...]
    above = jnp.where(odd == 1, core_edge, chip_edge)
    below = jnp.where(odd == 1, chip_edge, core_edge)
    edges = jnp.concatenate([above, below], axis=0).astype(BF16)
    blurred = jnp.dot(inner_ref[...], intensity_ref[...], preferred_element_type=F32)
    blurred += jnp.dot(outer_ref[...], edges, preferred_element_type=F32)
    middle = jnp.sum(jnp.sum(blurred, axis=0, keepdims=True), axis=1, keepdims=True)
    middle = middle * (1.0 / (blurred.shape[0] * blurred.shape[1]))
    high = blurred.astype(BF16)
    low = (blurred - high.astype(F32)).astype(BF16)
    parts = jnp.concatenate([high, low], axis=1)
    parts_ref[...] = parts
    table = transposed_dot(waves_ref[...], parts)
    first = lax.broadcasted_iota(jnp.int32, table.shape, 0) == 16
    table_ref[...] = jnp.where(first, table - middle, table).astype(BF16)
    middle_ref[...] = jnp.broadcast_to(middle, middle_ref.shape)
    mean_ref[...] = site_means(
        table_ref, tents_ref, spin_ref, ends_ref, middle_ref[:1, :1]
    )


def core_kernel(table_ref, tents_ref, spin_ref, ends_ref, middle_ref, mean_ref):
    mean_ref[...] = site_means(
        table_ref, tents_ref, spin_ref, ends_ref, middle_ref[:1, :1]
    )


def own_kernel(
    parts_ref, operator_ref, table_ref, tents_ref, spin_ref, ends_ref, middle_ref,
    resist_hbm, mean_ref, resist_ref, sem,
):
    cols = resist_ref.shape[1] // 4
    copies = []

    def beside(site):
        if site % 3 == 0 and len(copies) < 4:
            lanes = pl.ds(len(copies) * cols, cols)
            block = operator_ref[:, lanes]
            resist_ref[:, lanes] = jnp.dot(
                parts_ref[...], jnp.concatenate([block, block], axis=0), preferred_element_type=F32
            )
            copies.append(
                pltpu.make_async_copy(
                    resist_ref.at[:, lanes], resist_hbm.at[:, lanes], sem.at[len(copies)]
                )
            )
            copies[-1].start()

    mean_ref[...] = site_means(
        table_ref, tents_ref, spin_ref, ends_ref, middle_ref[:1, :1], beside
    )
    for copy in copies:
        copy.wait()


def bias_kernel(level_ref, places_ref, own_ref, core_ref, chip_ref, steps_ref, out_ref):
    odd = parity() == 1
    core, chip = core_ref[...], chip_ref[...]
    means = (jnp.where(odd, core, chip), own_ref[...], jnp.where(odd, chip, core))
    means = [
        jnp.broadcast_to(part[:, i : i + 128], (8, 128))
        for part in means
        for i in range(0, part.shape[1], 128)
    ]
    found = []
    for start in range(0, out_ref.shape[1], 128):
        place = jnp.broadcast_to(places_ref[:, start : start + 128], (8, 128))
        tile, lane = place // 128, place % 128
        site_mean = jnp.zeros((8, 128), F32)
        for i, part in enumerate(means):
            site_mean = jnp.where(tile == i, jnp.take_along_axis(part, lane, axis=1), site_mean)
        found.append(site_mean[:1])
    site_mean = jnp.concatenate(found, axis=1)
    out_ref[...] = bias_step * steps_ref[...].astype(F32) - bias_gain * (
        site_mean - level_ref[:1, :1]
    )


def chip_pairs(groups, count):
    pairs = []
    for group in range(groups):
        first = group * count
        for i in range(1, count - 1, 2):
            pairs += [(first + i, first + i + 1), (first + i + 1, first + i)]
    if groups % 2:
        for group in range(groups):
            pairs += [(group * count, (group + 1) * count - 1), ((group + 1) * count - 1, group * count)]
    else:
        for group in range(groups):
            for end in (0, count - 1):
                pairs.append((group * count + end, (group ^ 1) * count + end))
    return pairs


def swap_chips(to_chip):
    pairs = chip_pairs(lax.axis_size("groups"), lax.axis_size("tx"))
    return lax.ppermute(to_chip, ("groups", "tx"), pairs)


def swap_cores(to_core):
    return lax.ppermute(to_core, "tx", [(i, i ^ 1) for i in range(lax.axis_size("tx"))])


def call(kernel, outs, args, smem=(), hbm=(), hbm_outs=(), scratch=(), name=None):
    specs = [
        pl.BlockSpec(
            memory_space=pltpu.SMEM if i in smem else pltpu.HBM if i in hbm else pltpu.VMEM
        )
        for i in range(len(args))
    ]
    args = [
        pltpu.with_memory_space_constraint(arg, pltpu.HBM) if i in hbm else arg
        for i, arg in enumerate(args)
    ]
    return pl.pallas_call(
        kernel,
        out_shape=[jax.ShapeDtypeStruct(s, d) for s, d in outs],
        in_specs=specs,
        out_specs=[
            pl.BlockSpec(memory_space=pltpu.HBM if i in hbm_outs else pltpu.VMEM)
            for i in range(len(outs))
        ],
        scratch_shapes=list(scratch),
        compiler_params=pltpu.CompilerParams(vmem_limit_bytes=VMEM_BYTES),
        name=name,
    )(*args)


def shards(mask, kernel_spectra, kernel_weights, threshold, eval_tile, site_coords, bias_steps):
    tile_rows, tile_cols = mask.shape
    _, row_freqs, kernels, col_freqs = kernel_spectra.shape
    frags = eval_tile.shape[0]
    capacity = frags // 2
    samples = 2 * col_freqs
    flat = kernels * col_freqs
    records = 2 * SITES
    col_forward, side_rows, own_rows, row_inverse, edge_inverse, col_inverse = imaging_tables(
        tile_rows, tile_cols, row_freqs, col_freqs
    )
    operator, waves, inner, outer = blur_tables(tile_rows, tile_cols, col_freqs, BLUR_REACH)
    spectrum = ((2 * row_freqs, col_freqs), F32)
    packed = ((records, capacity), F32)
    edge = ((BLUR_REACH, samples), F32)
    means = ((1, capacity), F32)
    site_shapes = [
        ((SITES, tile_rows, capacity), BF16),
        ((SITES, col_freqs // 4, capacity), F32),
        ((SITES, 32 + 2 * BLUR_REACH, capacity), F32),
    ]
    weights = kernel_weights.reshape(1, kernels)

    spectra, to_core, to_chip, targets, coords = call(
        front_kernel,
        [((tile_rows, 2 * col_freqs), BF16), spectrum, spectrum]
        + [((1, frags), jnp.int32), ((records, frags), F32)],
        (
            mask, col_forward, side_rows,
            eval_tile.reshape(1, frags), site_coords.reshape(records, frags),
        ),
        hbm=range(5),
        scratch=[
            pltpu.VMEM(mask.shape, BF16),
            pltpu.VMEM(col_forward.shape, BF16),
            pltpu.VMEM(side_rows.shape, BF16),
            pltpu.SemaphoreType.DMA((5,)),
        ],
        name="front",
    )
    got_chip = swap_chips(to_chip)
    got_core = swap_cores(to_core)
    packed_core, packed_chip, packed_own, places = call(
        pack_kernel,
        [packed] * 3 + [((1, frags), jnp.int32)],
        (spectra, targets, coords),
        scratch=[pltpu.VMEM((3 * capacity, frags), BF16)],
        name="pack",
    )
    coords_chip = swap_chips(packed_chip)
    coords_core = swap_cores(packed_core)
    tables = (row_inverse, edge_inverse, col_inverse)
    level, own, inverse, lines, spread, *own_sites = call(
        functools.partial(load_kernel, tile_cols),
        [((8, 128), F32), spectrum] + [(table.shape, BF16) for table in tables] + site_shapes,
        (spectra, packed_own, threshold, own_rows, *tables),
        smem=(2,),
        hbm=(3, 4, 5, 6),
        scratch=[pltpu.VMEM(own_rows.shape, BF16), pltpu.SemaphoreType.DMA((4,))],
        name="load",
    )
    kern = jnp.transpose(kernel_spectra, (0, 2, 1, 3))
    product, edge_core, edge_chip = call(
        edge_kernel,
        [((2 * row_freqs, flat), BF16), edge, edge],
        (
            weights, own, got_core, got_chip, kern, lines, spread,
        ),
        name="edges",
    )
    edge_chip = swap_chips(edge_chip)
    edge_core = swap_cores(edge_core)
    (intensity,) = call(
        imaging_kernel,
        [((tile_rows, samples), BF16)],
        (weights, product, inverse, spread),
        name="imaging",
    )
    other_sites = call(
        functools.partial(prepare_kernel, tile_cols),
        site_shapes * 2,
        (coords_chip, coords_core),
        name="prepare",
    )
    chip_sites, core_sites = other_sites[:3], other_sites[3:]
    parts, table, middle, mean_chip = call(
        resist_kernel,
        [((tile_rows, 2 * samples), BF16), ((waves.shape[0], tile_rows), BF16), ((8, 128), F32), means],
        (intensity, edge_core, edge_chip, inner, outer, waves, *chip_sites),
        name="resist",
    )
    back_chip = swap_chips(mean_chip)
    (mean_core,) = call(core_kernel, [means], (table, *core_sites, middle), name="mean_core")
    back_core = swap_cores(mean_core)
    resist, mean_own = call(
        own_kernel,
        [((tile_rows, tile_cols), F32), means],
        (parts, operator, table, *own_sites, middle),
        hbm_outs=(0,),
        scratch=[pltpu.VMEM((tile_rows, tile_cols), F32), pltpu.SemaphoreType.DMA((4,))],
        name="mean_own",
    )
    (new_bias,) = call(
        bias_kernel,
        [((1, frags), F32)],
        (level, places, mean_own, back_core, back_chip, bias_steps.reshape(1, frags)),
        name="bias",
    )
    return resist, new_bias.reshape(frags)


def solution(mesh):
    placed = (
        P(("groups", "tx"), None),
        P(),
        P(),
        P(),
        P(("groups", "tx")),
        P(None, None, ("groups", "tx")),
        P(("groups", "tx")),
    )
    return jax.shard_map(
        shards,
        mesh=mesh,
        in_specs=placed,
        out_specs=(P(("groups", "tx"), None), P(("groups", "tx"))),
        check_vma=False,
    )
```

```python
import functools
import math

import jax
import jax.numpy as jnp
import ml_dtypes
import numpy as np
from jax import lax
from jax.experimental import pallas as pl
from jax.experimental.pallas import tpu as pltpu
from jax.sharding import PartitionSpec as P

HALO = 256
BLUR_REACH = 8
SITES = 16

blur_sigma = 3.0
bias_step = 0.5
bias_gain = 2.0

F32 = jnp.float32
BF16 = jnp.bfloat16
SINE = (1.57079628989, -0.645963358138, 0.0796884742403, -0.0046722194159, 0.000150816735945)
COSINE = (0.999999953341, -1.23369820859, 0.25365071182, -0.0208105729184, 0.000858162571361)
VMEM_BYTES = 32 * 1024 * 1024


def rounded(table):
    return np.asarray(table, np.float32).astype(ml_dtypes.bfloat16)


def shaped(table):
    result = np.zeros(table.shape, ml_dtypes.bfloat16)
    carry = np.zeros(table.shape[:-1])
    for i in range(table.shape[-1]):
        wanted = table[..., i] + carry
        result[..., i] = rounded(wanted)
        carry = wanted - result[..., i].astype(np.float64)
    return result


def twiddle(position, frequency, period, amplitude):
    phase_index = (position[:, None] * frequency[None, :]) % period
    phase_angle = phase_index * (2.0 * math.pi / period)
    return np.cos(phase_angle) * amplitude, np.sin(phase_angle) * amplitude


def centered(count):
    return np.arange(count) - count // 2


def imaging_tables(tile_rows, tile_cols, row_freqs, col_freqs):
    window_rows = tile_rows + 2 * HALO
    col_cos, col_sin = twiddle(
        np.arange(tile_cols), centered(col_freqs), tile_cols, 1.0 / math.sqrt(tile_cols)
    )
    col_forward = rounded(np.concatenate([col_cos, -col_sin], axis=1))
    row_cos, row_sin = twiddle(
        centered(row_freqs), np.arange(window_rows), window_rows, 1.0 / math.sqrt(window_rows)
    )
    row_forward = rounded(np.concatenate([row_cos, -row_sin], axis=0))
    row_blocks = [row_forward[:, i * tile_rows : (i + 1) * tile_rows] for i in range(3)]
    side_rows = np.concatenate([row_blocks[0], row_blocks[2]], axis=0)
    own_rows = np.ascontiguousarray(row_blocks[1])
    back_cos, back_sin = twiddle(
        np.arange(tile_rows) + HALO, centered(row_freqs), window_rows, 1.0 / math.sqrt(row_freqs)
    )
    row_inverse = rounded(
        np.block([[back_cos, -back_sin], [back_sin, back_cos]])
    )
    reach = BLUR_REACH
    near = np.r_[:reach, tile_rows - reach : tile_rows]
    edge_inverse = np.ascontiguousarray(row_inverse[np.concatenate([near, tile_rows + near])])
    samples = 2 * col_freqs
    step = tile_cols // samples
    out_cos, out_sin = twiddle(
        centered(col_freqs), np.arange(samples) * step, tile_cols, 1.0 / math.sqrt(col_freqs)
    )
    col_inverse = rounded(np.block([[out_cos, out_sin], [-out_sin, out_cos]]))
    return col_forward, side_rows, own_rows, row_inverse, edge_inverse, col_inverse


def blur_weight(offset, reach):
    every = np.arange(-reach, reach + 1).astype(np.float64)
    norm = np.sum(np.exp(-every * every / (2.0 * blur_sigma * blur_sigma)))
    weight = np.exp(-offset.astype(np.float64) ** 2 / (2.0 * blur_sigma * blur_sigma)) / norm
    return np.where(np.abs(offset) <= reach, weight, 0.0)


def blur_tables(tile_rows, tile_cols, col_freqs, reach):
    line = np.arange(tile_cols)
    col_blur = rounded(blur_weight(line[None, :] - line[:, None], reach))
    samples = 2 * col_freqs
    step = tile_cols // samples
    offset = (line[None, :] - step * np.arange(samples)[:, None]).astype(np.float64)
    half = np.where(offset == 0, 1.0, np.sin(math.pi * offset / tile_cols))
    spread = np.where(
        offset == 0,
        (samples - 1) / samples,
        np.sin((samples - 1) * math.pi * offset / tile_cols) / (samples * half),
    )
    spread_blur = spread @ col_blur.astype(np.float64)
    row_diff = (
        np.arange(tile_rows + 2 * reach)[None, :] - reach - np.arange(tile_rows)[:, None]
    )
    row_blur = rounded(blur_weight(row_diff, reach))
    inner = row_blur[:, reach : reach + tile_rows]
    outer = np.concatenate([row_blur[:, :reach], row_blur[:, reach + tile_rows :]], axis=1)
    operator = np.ascontiguousarray(shaped(spread_blur.T).T)

    freqs = np.arange(col_freqs)
    gauss = blur_weight(np.arange(-reach, reach + 1), reach)
    gauss = rounded(gauss).astype(np.float64)
    theta = 2.0 * math.pi * freqs / tile_cols
    gain = np.cos(theta[:, None] * np.arange(-reach, reach + 1)[None, :]) @ gauss
    gain = gain * np.where(freqs == 0, 1.0, 2.0) / samples
    cosines, sines = twiddle(freqs, np.arange(samples), samples, 1.0)
    real = (gain[:, None] * cosines).reshape(-1, 8, samples)
    imag = (-gain[:, None] * sines).reshape(-1, 8, samples)
    mid = col_freqs // 16
    above, below = slice(mid + 1, None), slice(mid - 1, 0, -1)
    sides = [
        real[above] + real[below], imag[above] - imag[below],
        imag[above] + imag[below], real[above] - real[below],
    ]
    paired = np.concatenate(
        [np.stack([real[mid], imag[mid], real[0], imag[0]]).reshape(-1, samples)]
        + [np.stack(sides, axis=1).reshape(-1, samples)]
    )
    ring = np.zeros((tile_cols, tile_cols))
    for shift in range(-reach, reach + 1):
        ring[line, (line + shift) % tile_cols] = gauss[shift + reach]
    edge = np.concatenate([line[:reach], line[tile_cols - reach :]])
    cut = (spread @ (col_blur.astype(np.float64) - ring)[:, edge]).T
    waves = np.concatenate([paired, cut], axis=0)
    waves = shaped(waves)
    waves = np.concatenate([waves, waves], axis=1)
    return operator, waves, np.ascontiguousarray(inner), np.ascontiguousarray(outer)


def parity():
    return lax.rem(lax.axis_index("tx"), 2)


def has_chip_side():
    me = lax.axis_index("tx")
    return jnp.logical_and(me != 0, me != lax.axis_size("tx") - 1)


def three_parts(values):
    first = values.astype(BF16)
    rest = values - first.astype(F32)
    second = rest.astype(BF16)
    third = (rest - second.astype(F32)).astype(BF16)
    return first, second, third


def transposed_dot(left, right):
    return lax.dot_general(left, right, (((1,), (1,)), ((), ())), preferred_element_type=F32)


def started(sems, *moves):
    copies = [
        pltpu.make_async_copy(source, target, sems.at[i])
        for i, (source, target) in enumerate(moves)
    ]
    for copy in copies:
        copy.start()
    return copies


def part_spectrum(product, freqs, cols):
    real = product[:freqs, :cols] - product[freqs:, cols:]
    imag = product[:freqs, cols:] + product[freqs:, :cols]
    return jnp.concatenate([real, imag], axis=0)


def front_kernel(
    mask_hbm, forward_hbm, rows_hbm, eval_hbm, records_hbm,
    spectra_ref, core_ref, chip_ref, eval_ref, records_ref,
    mask_ref, forward_ref, rows_ref, sems,
):
    copies = started(
        sems,
        (mask_hbm, mask_ref),
        (forward_hbm, forward_ref),
        (rows_hbm, rows_ref),
        (eval_hbm, eval_ref),
        (records_hbm, records_ref),
    )
    copies[0].wait()
    copies[1].wait()
    spectra = jnp.dot(mask_ref[...], forward_ref[...], preferred_element_type=F32).astype(BF16)
    spectra_ref[...] = spectra
    copies[2].wait()
    product = jnp.dot(rows_ref[...], spectra, preferred_element_type=F32)
    freqs, cols = core_ref.shape[0] // 2, core_ref.shape[1]
    upper_side = part_spectrum(product[: 2 * freqs], freqs, cols)
    lower_side = part_spectrum(product[2 * freqs :], freqs, cols)
    odd = parity()
    chip_ref[...] = jnp.where(odd == 1, upper_side, lower_side)
    core_ref[...] = jnp.where(odd == 1, lower_side, upper_side)
    copies[3].wait()
    copies[4].wait()


def pack_kernel(
    after_ref, eval_ref, records_ref, packed_core_ref, packed_chip_ref, packed_own_ref, places_ref,
    chosen_ref,
):
    me = lax.axis_index("tx")
    odd = parity()
    frags = eval_ref.shape[1]
    capacity = frags // 2
    count = records_ref.shape[0]
    before = lax.broadcasted_iota(jnp.int32, (frags, frags), 0)
    after = lax.broadcasted_iota(jnp.int32, (frags, frags), 1)
    upper = (before <= after).astype(F32).astype(BF16)
    slots = lax.broadcasted_iota(jnp.int32, (capacity, frags), 0).astype(F32).astype(BF16)
    member = lax.broadcasted_iota(jnp.int32, (8, frags), 0) == eval_ref[...] - me + 1
    counts = jnp.dot(member.astype(F32).astype(BF16), upper, preferred_element_type=F32)
    code = jnp.where(member, counts - 1.0, -1.0)
    side = lax.broadcasted_iota(jnp.int32, (8, frags), 0) * capacity
    place = jnp.where(member, side + counts.astype(jnp.int32) - 1, 0)
    places_ref[...] = jnp.sum(place, axis=0, keepdims=True)
    for side in range(3):
        row = jnp.broadcast_to(code[side : side + 1].astype(BF16), (capacity, frags))
        chosen_ref[pl.ds(side * capacity, capacity)] = jnp.where(
            slots == row, jnp.ones_like(slots), jnp.zeros_like(slots)
        )
    pieces = jnp.concatenate(three_parts(records_ref[...]), axis=0)

    def packed(side, out_ref):
        chosen = chosen_ref[pl.ds(pl.multiple_of(side * capacity, capacity), capacity)]
        got = transposed_dot(pieces, chosen)
        out_ref[...] = got[:count] + got[count : 2 * count] + got[2 * count :]

    packed(2 - 2 * odd, packed_core_ref)
    packed(2 * odd, packed_chip_ref)
    packed(1, packed_own_ref)


def load_kernel(
    cols, spectra_ref, coords_ref, threshold_ref, rows_hbm, inverse_hbm, lines_hbm, spread_hbm,
    level_ref, own_ref, inverse_ref, lines_ref, spread_ref, tents_ref, spin_ref, ends_ref,
    rows_ref, sems,
):
    copies = started(
        sems,
        (rows_hbm, rows_ref), (inverse_hbm, inverse_ref), (lines_hbm, lines_ref), (spread_hbm, spread_ref),
    )
    level_ref[...] = jnp.full(level_ref.shape, threshold_ref[0], F32)
    site_tables(coords_ref[...], tents_ref, spin_ref, ends_ref, cols)
    copies[0].wait()
    product = jnp.dot(rows_ref[...], spectra_ref[...], preferred_element_type=F32)
    own_ref[...] = part_spectrum(product, own_ref.shape[0] // 2, own_ref.shape[1])
    for copy in copies[1:]:
        copy.wait()


def stacked_pairs(half, rows, kernels, cols):
    pairs = []
    for k in range(kernels):
        lanes = slice(k * cols, (k + 1) * cols)
        pairs.append(jnp.concatenate([half[:rows, lanes], half[rows:, lanes]], axis=1))
    return jnp.concatenate(pairs, axis=0)


def edge_kernel(
    weights_ref, own_ref, core_ref, chip_ref, kern_ref, lines_ref, spread_ref,
    product_ref, edge_core_ref, edge_chip_ref,
):
    freqs, cols = own_ref.shape[0] // 2, own_ref.shape[1]
    kernels = kern_ref.shape[1]
    odd = parity()
    chip = jnp.where(has_chip_side(), chip_ref[...], 0.0)
    spectrum = own_ref[...] + core_ref[...] + chip
    spec_real, spec_imag = spectrum[:freqs], spectrum[freqs:]
    for k in range(kernels):
        kern_real, kern_imag = kern_ref[0, k], kern_ref[1, k]
        lanes = slice(k * cols, (k + 1) * cols)
        product_ref[:freqs, lanes] = (kern_real * spec_real - kern_imag * spec_imag).astype(BF16)
        product_ref[freqs:, lanes] = (kern_real * spec_imag + kern_imag * spec_real).astype(BF16)
    reach = BLUR_REACH
    half = jnp.dot(lines_ref[...], product_ref[...], preferred_element_type=F32).astype(BF16)
    pairs = stacked_pairs(half, 2 * reach, kernels, cols)
    field = jnp.dot(pairs, spread_ref[...], preferred_element_type=F32)
    total = jnp.zeros((2 * reach, 2 * cols), F32)
    for k in range(kernels):
        part = field[2 * reach * k : 2 * reach * (k + 1)]
        real, imag = part[:, : 2 * cols], part[:, 2 * cols :]
        total = total + weights_ref[:, k : k + 1] * (real * real + imag * imag)
    values = total.astype(BF16).astype(F32)
    top, bottom = values[:reach], values[reach:]
    edge_core_ref[...] = jnp.where(odd == 1, top, bottom)
    edge_chip_ref[...] = jnp.where(odd == 1, bottom, top)


def prepare_kernel(
    tile_cols, chip_coords_ref, core_coords_ref,
    chip_tents_ref, chip_spin_ref, chip_ends_ref, core_tents_ref, core_spin_ref, core_ends_ref,
):
    site_tables(chip_coords_ref[...], chip_tents_ref, chip_spin_ref, chip_ends_ref, tile_cols)
    site_tables(core_coords_ref[...], core_tents_ref, core_spin_ref, core_ends_ref, tile_cols)


def imaging_kernel(weights_ref, product_ref, inverse_ref, spread_ref, intensity_ref):
    rows, samples = intensity_ref.shape
    cols = samples // 2
    kernels = product_ref.shape[1] // cols
    half = jnp.dot(inverse_ref[...], product_ref[...], preferred_element_type=F32).astype(BF16)
    fields = jnp.dot(
        stacked_pairs(half, rows, kernels, cols), spread_ref[...], preferred_element_type=F32
    )
    total = jnp.zeros((rows, samples), F32)
    for k in range(kernels):
        field = fields[k * rows : (k + 1) * rows]
        real, imag = field[:, :samples], field[:, samples:]
        total = total + weights_ref[:, k : k + 1] * (real * real + imag * imag)
    intensity_ref[...] = total.astype(BF16)


def turned(index, period):
    turns = index * (1.0 / period)
    part = 2.0 * (turns - jnp.floor(turns + 0.5))
    square = part * part
    sine = SINE[-1]
    for term in SINE[-2::-1]:
        sine = sine * square + term
    sine = sine * part
    cosine = COSINE[-1]
    for term in COSINE[-2::-1]:
        cosine = cosine * square + term
    return 1.0 - 2.0 * sine * sine, 2.0 * sine * cosine


def site_tables(coords, tents_ref, spin_ref, ends_ref, tile_cols):
    tile_rows, slots = tents_ref.shape[1:]
    eight = lax.broadcasted_iota(jnp.int32, (8, slots), 0).astype(F32)
    count = spin_ref.shape[1] // 4
    steps = jnp.concatenate([8.0 * eight + 8.0, eight + 8.0 * count], axis=0)
    one_cosine, one_sine = turned(steps, tile_cols)
    line = lax.broadcasted_iota(jnp.int32, (tile_rows, slots), 0).astype(F32).astype(BF16)
    none = jnp.zeros((tile_rows, slots), BF16)
    edge = lax.broadcasted_iota(jnp.int32, (2 * BLUR_REACH, slots), 0).astype(F32)
    edge = jnp.where(edge < BLUR_REACH, edge, edge + (tile_cols - 2.0 * BLUR_REACH))

    def wide(row, dtype=F32):
        return jnp.broadcast_to(row.astype(dtype), (tile_rows, slots))

    for site in range(SITES):
        position = coords[site : site + 1] * (tile_rows - 1)
        low = jnp.minimum(jnp.floor(position), tile_rows - 2.0)
        part = position - low
        high_tent = jnp.where(line == wide(low + 1.0, BF16), wide(part, BF16), none)
        tents_ref[site] = jnp.where(line == wide(low, BF16), wide(1.0 - part, BF16), high_tent)
        position = coords[SITES + site : SITES + site + 1] * (tile_cols - 1)
        low = jnp.minimum(jnp.floor(position), tile_cols - 2.0)
        part = position - low
        cosine, sine = turned(low * steps, tile_cols)
        next_cosine = cosine * one_cosine - sine * one_sine
        next_sine = sine * one_cosine + cosine * one_sine
        spin_ref[site, :8] = cosine[:8]
        spin_ref[site, 8:16] = sine[:8]
        spin_ref[site, 16:24] = next_cosine[:8]
        spin_ref[site, 24:] = next_sine[:8]
        ends_ref[site, :8] = (1.0 - part) * cosine[8:]
        ends_ref[site, 8:16] = (1.0 - part) * sine[8:]
        ends_ref[site, 16:24] = part * next_cosine[8:]
        ends_ref[site, 24:32] = part * next_sine[8:]
        ends_ref[site, 32:] = jnp.maximum(1.0 - jnp.abs(position - edge), 0.0)


def site_means(table_ref, tents_ref, spin_ref, ends_ref, middle, beside=None):
    slots = tents_ref.shape[2]
    count = spin_ref.shape[1] // 4
    pairs = count - 1
    none = jnp.zeros((8, slots), F32)
    total = none
    for site in range(SITES):
        if beside is not None:
            beside(site)
        picked = jnp.dot(table_ref[...], tents_ref[site], preferred_element_type=F32)
        rows = [picked[8 * i : 8 * i + 8] for i in range(4 * pairs + 6)]

        def spin(i):
            return jnp.broadcast_to(spin_ref[site, i : i + 1], (8, slots))

        def ends(i):
            return ends_ref[site, 8 * i : 8 * i + 8]

        sums = []
        for first in (0, 2 * count):
            cosine, sine = spin(first + pairs), spin(first + count + pairs)
            sums.append(rows[0] + rows[2] * cosine + rows[3] * sine)
            sums.append(rows[1] + rows[3] * cosine - rows[2] * sine)
        for k in range(pairs):
            here = rows[4 * k + 4 : 4 * k + 8]
            for side in range(2):
                first = 2 * count * side
                cosine, sine = spin(first + k), spin(first + count + k)
                sums[2 * side] = (sums[2 * side] + here[0] * cosine) - here[1] * sine
                sums[2 * side + 1] = (sums[2 * side + 1] + here[2] * cosine) + here[3] * sine
        total += (sums[0] * ends(0) - sums[1] * ends(1)) + (sums[2] * ends(2) - sums[3] * ends(3))
        total += rows[4 * pairs + 4] * ends(4) + rows[4 * pairs + 5] * ends(5)
    mean = middle + jnp.sum(total, axis=0, keepdims=True) * (1.0 / SITES)
    return mean


def resist_kernel(
    intensity_ref, core_ref, chip_ref, inner_ref, outer_ref, waves_ref,
    tents_ref, spin_ref, ends_ref,
    parts_ref, table_ref, middle_ref, mean_ref,
):
    odd = parity()
    chip_edge = jnp.where(has_chip_side(), chip_ref[...], 0.0)
    core_edge = core_ref[...]
    above = jnp.where(odd == 1, core_edge, chip_edge)
    below = jnp.where(odd == 1, chip_edge, core_edge)
    edges = jnp.concatenate([above, below], axis=0).astype(BF16)
    blurred = jnp.dot(inner_ref[...], intensity_ref[...], preferred_element_type=F32)
    blurred += jnp.dot(outer_ref[...], edges, preferred_element_type=F32)
    middle = jnp.sum(jnp.sum(blurred, axis=0, keepdims=True), axis=1, keepdims=True)
    middle = middle * (1.0 / (blurred.shape[0] * blurred.shape[1]))
    high = blurred.astype(BF16)
    low = (blurred - high.astype(F32)).astype(BF16)
    parts = jnp.concatenate([high, low], axis=1)
    parts_ref[...] = parts
    table = transposed_dot(waves_ref[...], parts)
    first = lax.broadcasted_iota(jnp.int32, table.shape, 0) == 16
    table_ref[...] = jnp.where(first, table - middle, table).astype(BF16)
    middle_ref[...] = jnp.broadcast_to(middle, middle_ref.shape)
    mean_ref[...] = site_means(
        table_ref, tents_ref, spin_ref, ends_ref, middle_ref[:1, :1]
    )


def core_kernel(table_ref, tents_ref, spin_ref, ends_ref, middle_ref, mean_ref):
    mean_ref[...] = site_means(
        table_ref, tents_ref, spin_ref, ends_ref, middle_ref[:1, :1]
    )


def own_kernel(
    parts_ref, operator_ref, table_ref, tents_ref, spin_ref, ends_ref, middle_ref,
    resist_hbm, mean_ref, resist_ref, sem,
):
    cols = resist_ref.shape[1] // 4
    copies = []

    def beside(site):
        if site % 3 == 0 and len(copies) < 4:
            lanes = pl.ds(len(copies) * cols, cols)
            block = operator_ref[:, lanes]
            resist_ref[:, lanes] = jnp.dot(
                parts_ref[...], jnp.concatenate([block, block], axis=0), preferred_element_type=F32
            )
            copies.append(
                pltpu.make_async_copy(
                    resist_ref.at[:, lanes], resist_hbm.at[:, lanes], sem.at[len(copies)]
                )
            )
            copies[-1].start()

    mean_ref[...] = site_means(
        table_ref, tents_ref, spin_ref, ends_ref, middle_ref[:1, :1], beside
    )
    for copy in copies:
        copy.wait()


def bias_kernel(level_ref, places_ref, own_ref, core_ref, chip_ref, steps_ref, out_ref):
    odd = parity() == 1
    core, chip = core_ref[...], chip_ref[...]
    means = (jnp.where(odd, core, chip), own_ref[...], jnp.where(odd, chip, core))
    means = [
        jnp.broadcast_to(part[:, i : i + 128], (8, 128))
        for part in means
        for i in range(0, part.shape[1], 128)
    ]
    found = []
    for start in range(0, out_ref.shape[1], 128):
        place = jnp.broadcast_to(places_ref[:, start : start + 128], (8, 128))
        tile, lane = place // 128, place % 128
        site_mean = jnp.zeros((8, 128), F32)
        for i, part in enumerate(means):
            site_mean = jnp.where(tile == i, jnp.take_along_axis(part, lane, axis=1), site_mean)
        found.append(site_mean[:1])
    site_mean = jnp.concatenate(found, axis=1)
    out_ref[...] = bias_step * steps_ref[...].astype(F32) - bias_gain * (
        site_mean - level_ref[:1, :1]
    )


def chip_pairs(groups, count):
    pairs = []
    for group in range(groups):
        first = group * count
        for i in range(1, count - 1, 2):
            pairs += [(first + i, first + i + 1), (first + i + 1, first + i)]
    if groups % 2:
        for group in range(groups):
            pairs += [(group * count, (group + 1) * count - 1), ((group + 1) * count - 1, group * count)]
    else:
        for group in range(groups):
            for end in (0, count - 1):
                pairs.append((group * count + end, (group ^ 1) * count + end))
    return pairs


def swap_chips(to_chip):
    pairs = chip_pairs(lax.axis_size("groups"), lax.axis_size("tx"))
    return lax.ppermute(to_chip, ("groups", "tx"), pairs)


def swap_cores(to_core):
    return lax.ppermute(to_core, "tx", [(i, i ^ 1) for i in range(lax.axis_size("tx"))])


def call(kernel, outs, args, smem=(), hbm=(), hbm_outs=(), scratch=(), name=None):
    specs = [
        pl.BlockSpec(
            memory_space=pltpu.SMEM if i in smem else pltpu.HBM if i in hbm else pltpu.VMEM
        )
        for i in range(len(args))
    ]
    args = [
        pltpu.with_memory_space_constraint(arg, pltpu.HBM) if i in hbm else arg
        for i, arg in enumerate(args)
    ]
    return pl.pallas_call(
        kernel,
        out_shape=[jax.ShapeDtypeStruct(s, d) for s, d in outs],
        in_specs=specs,
        out_specs=[
            pl.BlockSpec(memory_space=pltpu.HBM if i in hbm_outs else pltpu.VMEM)
            for i in range(len(outs))
        ],
        scratch_shapes=list(scratch),
        compiler_params=pltpu.CompilerParams(vmem_limit_bytes=VMEM_BYTES),
        name=name,
    )(*args)


def shards(mask, kernel_spectra, kernel_weights, threshold, eval_tile, site_coords, bias_steps):
    tile_rows, tile_cols = mask.shape
    _, row_freqs, kernels, col_freqs = kernel_spectra.shape
    frags = eval_tile.shape[0]
    capacity = frags // 2
    samples = 2 * col_freqs
    flat = kernels * col_freqs
    records = 2 * SITES
    col_forward, side_rows, own_rows, row_inverse, edge_inverse, col_inverse = imaging_tables(
        tile_rows, tile_cols, row_freqs, col_freqs
    )
    operator, waves, inner, outer = blur_tables(tile_rows, tile_cols, col_freqs, BLUR_REACH)
    spectrum = ((2 * row_freqs, col_freqs), F32)
    packed = ((records, capacity), F32)
    edge = ((BLUR_REACH, samples), F32)
    means = ((1, capacity), F32)
    site_shapes = [
        ((SITES, tile_rows, capacity), BF16),
        ((SITES, col_freqs // 4, capacity), F32),
        ((SITES, 32 + 2 * BLUR_REACH, capacity), F32),
    ]
    weights = kernel_weights.reshape(1, kernels)

    spectra, to_core, to_chip, targets, coords = call(
        front_kernel,
        [((tile_rows, 2 * col_freqs), BF16), spectrum, spectrum]
        + [((1, frags), jnp.int32), ((records, frags), F32)],
        (
            mask, col_forward, side_rows,
            eval_tile.reshape(1, frags), site_coords.reshape(records, frags),
        ),
        hbm=range(5),
        scratch=[
            pltpu.VMEM(mask.shape, BF16),
            pltpu.VMEM(col_forward.shape, BF16),
            pltpu.VMEM(side_rows.shape, BF16),
            pltpu.SemaphoreType.DMA((5,)),
        ],
        name="front",
    )
    got_chip = swap_chips(to_chip)
    got_core = swap_cores(to_core)
    packed_core, packed_chip, packed_own, places = call(
        pack_kernel,
        [packed] * 3 + [((1, frags), jnp.int32)],
        (spectra, targets, coords),
        scratch=[pltpu.VMEM((3 * capacity, frags), BF16)],
        name="pack",
    )
    coords_chip = swap_chips(packed_chip)
    coords_core = swap_cores(packed_core)
    tables = (row_inverse, edge_inverse, col_inverse)
    level, own, inverse, lines, spread, *own_sites = call(
        functools.partial(load_kernel, tile_cols),
        [((8, 128), F32), spectrum] + [(table.shape, BF16) for table in tables] + site_shapes,
        (spectra, packed_own, threshold, own_rows, *tables),
        smem=(2,),
        hbm=(3, 4, 5, 6),
        scratch=[pltpu.VMEM(own_rows.shape, BF16), pltpu.SemaphoreType.DMA((4,))],
        name="load",
    )
    kern = jnp.transpose(kernel_spectra, (0, 2, 1, 3))
    product, edge_core, edge_chip = call(
        edge_kernel,
        [((2 * row_freqs, flat), BF16), edge, edge],
        (
            weights, own, got_core, got_chip, kern, lines, spread,
        ),
        name="edges",
    )
    edge_chip = swap_chips(edge_chip)
    edge_core = swap_cores(edge_core)
    (intensity,) = call(
        imaging_kernel,
        [((tile_rows, samples), BF16)],
        (weights, product, inverse, spread),
        name="imaging",
    )
    other_sites = call(
        functools.partial(prepare_kernel, tile_cols),
        site_shapes * 2,
        (coords_chip, coords_core),
        name="prepare",
    )
    chip_sites, core_sites = other_sites[:3], other_sites[3:]
    parts, table, middle, mean_chip = call(
        resist_kernel,
        [((tile_rows, 2 * samples), BF16), ((waves.shape[0], tile_rows), BF16), ((8, 128), F32), means],
        (intensity, edge_core, edge_chip, inner, outer, waves, *chip_sites),
        name="resist",
    )
    back_chip = swap_chips(mean_chip)
    (mean_core,) = call(core_kernel, [means], (table, *core_sites, middle), name="mean_core")
    back_core = swap_cores(mean_core)
    resist, mean_own = call(
        own_kernel,
        [((tile_rows, tile_cols), F32), means],
        (parts, operator, table, *own_sites, middle),
        hbm_outs=(0,),
        scratch=[pltpu.VMEM((tile_rows, tile_cols), F32), pltpu.SemaphoreType.DMA((4,))],
        name="mean_own",
    )
    (new_bias,) = call(
        bias_kernel,
        [((1, frags), F32)],
        (level, places, mean_own, back_core, back_chip, bias_steps.reshape(1, frags)),
        name="bias",
    )
    return resist, new_bias.reshape(frags)


def solution(mesh):
    placed = (
        P(("groups", "tx"), None),
        P(),
        P(),
        P(),
        P(("groups", "tx")),
        P(None, None, ("groups", "tx")),
        P(("groups", "tx")),
    )
    return jax.shard_map(
        shards,
        mesh=mesh,
        in_specs=placed,
        out_specs=(P(("groups", "tx"), None), P(("groups", "tx"))),
        check_vma=False,
    )
```
